32 devices in a mesh: load: 4 (over y, x), gz: 8 (over z, core).
Axes of the slice: x: 2, y: 2, z: 4, core: 2. Of those that a mesh axis runs over, the one named last changes fastest.
Arguments:
- density: float32 [16, 32, 128], P('gz', 'load'), may hold values from 0.1 to 1
- labels: int32 [16, 32, 128], P('gz'), may hold values from 0 to 11
- forces: float32 [8, 3, 16, 32, 128], P('load', None, 'gz'), may hold values from -6 to 6
- case_weights: int32 [8], replicated, may hold values from 1 to 4
Outputs:
- new_density: float32 [16, 32, 128], P('gz', 'load')
- displacement: float32 [8, 3, 16, 32, 128], P('load', None, 'gz')
The draws below stay inside these ranges and needn't reach their ends.
All inputs are finite; a program needn't handle non-finite values.
Results may differ from the reference program's by a relative error of at most 0.00016.
Values sent between devices are 32-bit elements; how exact they have to be, the bound alone decides.
No kernel may reach another device: no remote copies, remote signals or barrier semaphores. Data moves between devices by JAX's collectives and lax.ppermute only.
A program may use at most 64 MiB of HBM per device.

```python
import jax
import jax.numpy as jnp
import numpy as np
from jax import lax

NX = 128
SWEEPS = 3
NY = 32
NZ = 16
LOADS = 8


def touch_ends(drawn, stream_key, smallest, high):
    shape = drawn.shape
    place = [jax.random.randint(jax.random.fold_in(stream_key, axis), (), 0, shape[axis]) for axis in range(len(shape))]
    drawn = drawn.at[tuple(place)].set(smallest)
    longest = shape.index(max(shape))
    place[longest] = (place[longest] + 1) % shape[longest]
    return drawn.at[tuple(place)].set(high)


def block_scale(rng, extent, cuts, low, largest):
    gain = 1.0
    for position, shards_of in cuts:
        steps = jax.random.uniform(jax.random.fold_in(jax.random.fold_in(rng, 6), position), (shards_of,), jnp.float32, low / len(cuts), largest / len(cuts))
        gain = gain * jnp.repeat(jnp.exp(steps), extent[position] // shards_of).reshape((-1,) + (1,) * (len(extent) - 1 - position))
    return gain


def normal_values(key, dims, scale, reach, cuts=(), kind=jnp.bfloat16):
    values = jax.random.normal(key, dims, jnp.float32) * scale
    if len(cuts) > 0:
        values = block_scale(key, dims, cuts, -0.22, 0.18) * values
    return jnp.clip(values, min=-reach, max=reach).astype(kind)


def setup_inputs(seed: int = 0) -> dict:
    seeds = jax.random.split(jax.random.key(seed), 5)
    return {
        "density": jnp.clip(0.1 + 0.9 * jax.random.uniform(seeds[0], (NZ, NY, NX), jnp.float32) ** block_scale(seeds[0], (NZ, NY, NX), ((0, 8), (1, 4)), -0.2, 0.2), 0.1, 1.0),
        "labels": touch_ends(jax.random.randint(seeds[1], (NZ, NY, NX), 0, 12), jax.random.fold_in(seeds[1], 1), 0, 11).astype(jnp.int32),
        "forces": normal_values(seeds[2], (LOADS, 3, NZ, NY, NX), 1.0, 6.0, ((0, 4), (2, 8)), jnp.float32),
        "case_weights": touch_ends(jax.random.randint(seeds[3], (LOADS,), 1, 5), jax.random.fold_in(seeds[3], 1), 1, 4).astype(jnp.int32),
    }


EMIN = 0.001
LOWER_EIG = 0.1
UPPER_EIG = 2.5
MOVE_LIMIT = 0.2
FLOOR_DENSITY = 0.001
CORNER_OFFSETS = [(corner // 4, corner // 2 % 2, corner % 2) for corner in range(8)]

def element_matrix():
    poisson = 0.3
    lame_first = poisson / ((1 + poisson) * (1 - 2 * poisson))
    shear_modulus = 1.0 / (2 * (1 + poisson))
    elastic = np.zeros((6, 6))
    elastic[:3, :3] = lame_first
    for which in range(3):
        elastic[which, which] += 2 * shear_modulus
        elastic[which + 3, which + 3] = shear_modulus
    points = [0.5 - 0.5 / np.sqrt(3.0), 0.5 + 0.5 / np.sqrt(3.0)]
    result = np.zeros((24, 24))
    for point_z in points:
        for point_y in points:
            for point_x in points:
                strain = np.zeros((6, 24))
                for corner in range(8):
                    corner_z, corner_y, corner_x = CORNER_OFFSETS[corner]
                    along_x = point_x if corner_x else 1.0 - point_x
                    along_y = point_y if corner_y else 1.0 - point_y
                    along_z = point_z if corner_z else 1.0 - point_z
                    sign_x = 1.0 if corner_x else -1.0
                    sign_y = 1.0 if corner_y else -1.0
                    sign_z = 1.0 if corner_z else -1.0
                    grad_x = sign_x * along_y * along_z
                    grad_y = sign_y * along_x * along_z
                    grad_z = sign_z * along_x * along_y
                    column = 3 * corner
                    strain[0, column] = grad_x
                    strain[1, column + 1] = grad_y
                    strain[2, column + 2] = grad_z
                    strain[3, column] = grad_y
                    strain[3, column + 1] = grad_x
                    strain[4, column + 1] = grad_z
                    strain[4, column + 2] = grad_y
                    strain[5, column] = grad_z
                    strain[5, column + 2] = grad_x
                result += strain.T @ elastic @ strain / 8.0
    return result

def corner_views(padded, layers, rows, columns):
    views = []
    for shift_z, shift_y, shift_x in CORNER_OFFSETS:
        views.append(padded[:, :, shift_z:shift_z + layers, shift_y:shift_y + rows, shift_x:shift_x + columns])
    return views

def element_forces(views, stiffness, scale):
    stacked = jnp.concatenate(views, axis=1)
    product = jnp.einsum('ij,bjzyx->bizyx', stiffness, stacked, precision=lax.Precision.HIGHEST) * scale
    return [product[:, 3 * target:3 * target + 3] for target in range(8)]

def assemble(weighted, first, layers):
    total = None
    for target in range(8):
        shift_z, shift_y, shift_x = CORNER_OFFSETS[target]
        piece = weighted[target]
        rows = piece.shape[3]
        columns = piece.shape[4]
        padded = jnp.pad(piece, ((0, 0), (0, 0), (1, 1), (1, 0), (1, 0)))
        part_sum = padded[:, :, first - shift_z:first - shift_z + layers, 1 - shift_y:1 - shift_y + rows, 1 - shift_x:1 - shift_x + columns]
        total = part_sum if total is None else total + part_sum
    return total

def smooth(padded, layers, rows, columns):
    total = None
    for off_z in (-1, 0, 1):
        for off_y in (-1, 0, 1):
            for off_x in (-1, 0, 1):
                weight = 1.5 - float(np.sqrt(off_z * off_z + off_y * off_y + off_x * off_x))
                if weight > 0:
                    term = weight * padded[1 + off_z:1 + off_z + layers, 1 + off_y:1 + off_y + rows, 1 + off_x:1 + off_x + columns]
                    total = term if total is None else total + term
    return total

def reference(density, labels, forces, case_weights):
    stiffness = jnp.asarray(element_matrix(), jnp.float32)
    layers, rows, columns = density.shape
    solid = jnp.where(labels == 2, jnp.float32(1.0), density)
    moduli = EMIN + (1.0 - EMIN) * solid * solid * solid
    scale = moduli[None, None]
    free = (labels != 1).astype(jnp.float32)[None, None]
    diag_terms = []
    for target in range(8):
        entries = jnp.stack([stiffness[3 * target + comp, 3 * target + comp] for comp in range(3)])
        diag_terms.append(entries[None, :, None, None, None] * scale)
    diagonal = assemble(diag_terms, 1, layers)
    inverse_diag = free / diagonal
    theta = 0.5 * (UPPER_EIG + LOWER_EIG)
    delta = 0.5 * (UPPER_EIG - LOWER_EIG)
    sigma = theta / delta

    def pad_high(field):
        return jnp.pad(field, ((0, 0), (0, 0), (0, 1), (0, 1), (0, 1)))

    def operate(field):
        views = corner_views(pad_high(field), layers, rows, columns)
        return assemble(element_forces(views, stiffness, scale), 1, layers)

    def one_case(case_force):
        load = case_force[None] * free
        residual = load
        step_dir = inverse_diag * residual / theta
        solution = step_dir
        factor = 1.0 / sigma
        for sweep in range(SWEEPS):
            residual = residual - free * operate(step_dir)
            next_factor = 1.0 / (2.0 * sigma - factor)
            step_dir = next_factor * factor * step_dir + 2.0 * next_factor / delta * inverse_diag * residual
            solution = solution + step_dir
            factor = next_factor
        views = corner_views(pad_high(solution), layers, rows, columns)
        pushed = element_forces(views, stiffness, jnp.float32(1.0))
        energy = None
        for target in range(8):
            term = lax.optimization_barrier(jnp.sum(views[target] * pushed[target], axis=1))
            energy = term if energy is None else energy + term
        return (solution[0], energy[0])
    solutions, energies = lax.map(one_case, forces)
    weights = case_weights.astype(jnp.float32)
    weighted = lax.optimization_barrier(jnp.sum(weights[:, None, None, None] * energies, axis=0)) / jnp.sum(weights)
    sensitivity = 3.0 * (1.0 - EMIN) * solid * solid * weighted
    numer = smooth(jnp.pad(density * sensitivity, 1), layers, rows, columns)
    denom = smooth(jnp.pad(density, 1), layers, rows, columns)
    filtered = numer / denom
    mean_value = jnp.sum(filtered) / (layers * rows * columns)
    candidate = density * jnp.sqrt(filtered / mean_value)
    lower = jnp.maximum(density - MOVE_LIMIT, FLOOR_DENSITY)
    upper = jnp.minimum(density + MOVE_LIMIT, 1.0)
    new_density = jnp.clip(candidate, lower, upper)
    new_density = jnp.where(labels == 2, jnp.float32(1.0), new_density)
    return (new_density, solutions)
```

```python
import functools

import jax
import jax.numpy as jnp
from jax import lax
from jax.experimental import pallas as pl
from jax.experimental.pallas import tpu as pltpu
from jax.sharding import PartitionSpec as P

SWEEPS = 3
EMIN = 0.001
LOWER_EIG = 0.1
UPPER_EIG = 2.5
MOVE_LIMIT = 0.2
FLOOR_DENSITY = 0.001
POISSON = 0.3
LAME = POISSON / ((1 + POISSON) * (1 - 2 * POISSON))
SHEAR = 1.0 / (2 * (1 + POISSON))
KE_DIAG = (LAME + 4 * SHEAR) / 9
EDGE = 1.5 - 2.0**0.5
PLANE = ("ss", "sd", "ds", "dd")


def next_x(a):
    lanes = a.shape[1]
    lane = lax.broadcasted_iota(jnp.int32, a.shape, 1)
    return jnp.where(lane == lanes - 1, 0.0, pltpu.roll(a, lanes - 1, 1))


def last_x(a):
    lane = lax.broadcasted_iota(jnp.int32, a.shape, 1)
    return jnp.where(lane == 0, 0.0, pltpu.roll(a, 1, 1))


def next_y(a):
    rows = a.shape[0]
    row = lax.broadcasted_iota(jnp.int32, a.shape, 0)
    return jnp.where(row == rows - 1, 0.0, pltpu.roll(a, rows - 1, 0))


def last_y(a):
    row = lax.broadcasted_iota(jnp.int32, a.shape, 0)
    return jnp.where(row == 0, 0.0, pltpu.roll(a, 1, 0))


def to_modes_xy(u):
    ux = next_x(u)
    s, d = ux + u, ux - u
    sy, dy = next_y(s), next_y(d)
    return {"ss": sy + s, "sd": sy - s, "ds": dy + d, "dd": dy - d}


def from_modes_xy(g):
    s = (g["ss"] - g["sd"]) + last_y(g["ss"] + g["sd"])
    d = (g["ds"] - g["dd"]) + last_y(g["ds"] + g["dd"])
    return (s - d) + last_x(s + d)


def modes_z(low, high):
    modes = []
    for comp in range(3):
        one = {}
        for pq in PLANE:
            if pq != "ss":
                one[pq + "s"] = high[comp][pq] + low[comp][pq]
            one[pq + "d"] = high[comp][pq] - low[comp][pq]
        modes.append(one)
    return modes


NORMAL = ((0, "dss"), (1, "sds"), (2, "ssd"))
BENDS = (((1, "dds"), (2, "dsd")), ((0, "dds"), (2, "sdd")), ((0, "dsd"), (1, "sdd")))
SHEARS = (((0, "sds"), (1, "dss")), ((0, "ssd"), (2, "dss")), ((1, "ssd"), (2, "sds")))
TWIST = ((0, "sdd"), (1, "dsd"), (2, "dds"))


def mode_forces(modes, e1):
    m = lambda key: modes[key[0]][key[1]]
    out = [{}, {}, {}]

    def put(key, value):
        out[key[0]][key[1]] = value

    e4 = e1 + e1
    e2 = e1 * (1.0 / 3.0)
    e3 = e1 * ((LAME + 4 * SHEAR) / (9 * SHEAR))
    trace = (LAME / (2 * SHEAR)) * (m(NORMAL[0]) + m(NORMAL[1]) + m(NORMAL[2]))
    for key in NORMAL:
        put(key, e4 * (trace + m(key)))
    for a, b in BENDS:
        t = (LAME / (3 * SHEAR)) * (m(a) + m(b))
        put(a, e1 * (t + m(a)))
        put(b, e1 * (t + m(b)))
    for a, b in SHEARS:
        f = e1 * (m(a) + m(b))
        put(a, f)
        put(b, f)
    t = m(TWIST[0]) + m(TWIST[1]) + m(TWIST[2])
    for key in TWIST:
        put(key, e2 * (t + m(key)))
    for comp in range(3):
        put((comp, "ddd"), e3 * modes[comp]["ddd"])
    return out


def mode_energy(modes):
    m = lambda key: modes[key[0]][key[1]]
    sq = lambda v: v * v
    n = [m(key) for key in NORMAL]
    total = (3 * LAME / SHEAR) * sq(n[0] + n[1] + n[2]) + 6.0 * (sq(n[0]) + sq(n[1]) + sq(n[2]))
    shear = None
    for a, b in SHEARS:
        t = sq(m(a) + m(b))
        shear = t if shear is None else shear + t
    total = total + 3.0 * shear
    sums, own = None, None
    for a, b in BENDS:
        t = sq(m(a) + m(b))
        o = sq(m(a)) + sq(m(b))
        sums = t if sums is None else sums + t
        own = o if own is None else own + o
    total = total + (LAME / SHEAR) * sums + 3.0 * own
    a, b, c = (m(key) for key in TWIST)
    total = total + (sq(a + b) + sq(a + c) + sq(b + c))
    bulk = sq(modes[0]["ddd"]) + sq(modes[1]["ddd"]) + sq(modes[2]["ddd"])
    return total + ((LAME + 4 * SHEAR) / (3 * SHEAR)) * bulk


def filter_planes(a):
    x = last_x(a) + next_x(a)
    cross = x + (last_y(a) + next_y(a))
    diagonal = last_y(x) + next_y(x)
    return 1.5 * a + 0.5 * cross + EDGE * diagonal, 0.5 * a + EDGE * cross


def filter_layers(layers):
    pairs = [filter_planes(a) for a in layers]
    return [
        pairs[at][0] + (pairs[at - 1][1] + pairs[at + 1][1]) for at in range(1, len(layers) - 1)
    ]


def smooth_kernel(hops, count_gz, *refs):
    blocks = 1 + 2 * hops
    weights_ref = refs[0]
    design_refs = refs[1 : 1 + blocks]
    force_refs = refs[1 + blocks : 1 + 2 * blocks]
    disp_hbm, sens_ref, rec_ref = refs[1 + 2 * blocks : 4 + 2 * blocks]
    (e1_ref, inv_ref, res_ref, step_ref, sol_ref, mode_ref, carry_ref, node_ref) = refs[4 + 2 * blocks : 12 + 2 * blocks]
    disp_ref, weight_ref, disp_sem = refs[12 + 2 * blocks :]

    cases, _, layers, rows, columns = disp_ref.shape
    nodes = layers + 2 * SWEEPS + 1
    gz = lax.axis_index("gz")
    load = lax.axis_index("load")

    def from_hop(refs, hop, pick):
        if hop == 0:
            return pick(refs[0])
        far = abs(hop)
        first, second = pick(refs[2 * far - 1]), pick(refs[2 * far])
        meets_above = (gz // far) % 2 == (0 if hop > 0 else 1)
        return jnp.where(meets_above, first, second)

    def inside(layer):
        owner = gz + layer // layers
        return jnp.logical_and(owner >= 0, owner < count_gz)

    def design(kind, layer):
        hop = layer // layers
        return from_hop(design_refs, hop, lambda ref: ref[kind, layer - hop * layers])

    below = None
    for at in range(nodes + 1):
        layer = at - SWEEPS - 1
        dense, marks = design(0, layer), design(1, layer)
        solid = jnp.where(marks == 2.0, 1.0, dense)
        live = jnp.where(inside(layer), 1.0, 0.0)
        moduli = (EMIN + (1.0 - EMIN) * solid * solid * solid) * live
        if 0 <= layer < layers:
            weight_ref[layer] = (3.0 * (1.0 - EMIN)) * solid * solid * dense
        if 1 <= at < nodes:
            e1_ref[at - 1] = moduli * (SHEAR / 16)
        spread = moduli + last_x(moduli)
        spread = spread + last_y(spread)
        if at > 0:
            diag = KE_DIAG * (below + spread)
            free = jnp.logical_and(marks != 1.0, inside(layer))
            inv_ref[at - 1] = jnp.where(free, 1.0 / jnp.where(free, diag, 1.0), 0.0)
        below = spread

    theta = 0.5 * (UPPER_EIG + LOWER_EIG)
    delta = 0.5 * (UPPER_EIG - LOWER_EIG)
    sigma = theta / delta

    def load_modes(slot, chunk):
        return [
            {pq: mode_ref[slot, comp * 4 + i, chunk] for i, pq in enumerate(PLANE)}
            for comp in range(3)
        ]

    def store_modes(slot, field_ref, node):
        for comp in range(3):
            planes = to_modes_xy(field_ref[comp, node])
            for i, pq in enumerate(PLANE):
                mode_ref[slot, comp * 4 + i] = planes[pq]

    def one_case(case, weighted):
        for at in range(nodes):
            node = at - SWEEPS
            hop = node // layers
            for comp in range(3):
                force = from_hop(force_refs, hop, lambda ref: ref[case, comp, node - hop * layers])
                step = inv_ref[at] * force * (1.0 / theta)
                res_ref[comp, at] = force
                step_ref[comp, at] = step
                if SWEEPS <= at <= SWEEPS + layers:
                    sol_ref[comp, at - SWEEPS] = step

        factor = 1.0 / sigma
        for sweep in range(1, SWEEPS + 1):
            factor_next = 1.0 / (2.0 * sigma - factor)
            keep, take = factor_next * factor, 2.0 * factor_next / delta
            first = sweep - 1
            store_modes(first % 2, step_ref, first)
            for element in range(first, nodes - sweep):
                store_modes((element + 1) % 2, step_ref, element + 1)
                whole = element > first
                for chunk_at in range(0, rows, 8):
                    chunk = pl.ds(chunk_at, 8)
                    low = load_modes(element % 2, chunk)
                    high = load_modes((element + 1) % 2, chunk)
                    f = mode_forces(modes_z(low, high), e1_ref[element, chunk])
                    for comp in range(3):
                        for i, pq in enumerate(PLANE):
                            diff = f[comp][pq + "d"]
                            if pq == "ss":
                                down, up = -diff, diff
                            else:
                                both = f[comp][pq + "s"]
                                down, up = both - diff, both + diff
                            if whole:
                                node_ref[comp * 4 + i, chunk] = carry_ref[comp * 4 + i, chunk] + down
                            carry_ref[comp * 4 + i, chunk] = up
                if whole:
                    for comp in range(3):
                        g = {pq: node_ref[comp * 4 + i] for i, pq in enumerate(PLANE)}
                        res = res_ref[comp, element] - from_modes_xy(g)
                        step = keep * step_ref[comp, element] + take * (inv_ref[element] * res)
                        if sweep < SWEEPS:
                            res_ref[comp, element] = res
                            step_ref[comp, element] = step
                        if SWEEPS <= element <= SWEEPS + layers:
                            sol = sol_ref[comp, element - SWEEPS] + step
                            sol_ref[comp, element - SWEEPS] = sol
                            if sweep == SWEEPS and element < SWEEPS + layers:
                                disp_ref[case, comp, element - SWEEPS] = sol
            factor = factor_next
        pltpu.make_async_copy(disp_ref.at[case], disp_hbm.at[case], disp_sem.at[case]).start()

        weight = weights_ref[load * cases + case].astype(jnp.float32)
        store_modes(0, sol_ref, 0)
        for layer in range(layers):
            store_modes((layer + 1) % 2, sol_ref, layer + 1)
            for chunk_at in range(0, rows, 8):
                chunk = pl.ds(chunk_at, 8)
                low = load_modes(layer % 2, chunk)
                high = load_modes((layer + 1) % 2, chunk)
                energy = weight * mode_energy(modes_z(low, high))
                node_ref[12 + layer, chunk] = jnp.where(case == 0, 0.0, node_ref[12 + layer, chunk]) + energy
        return weighted

    lax.fori_loop(0, cases, one_case, 0)
    weight_sum = weights_ref[0]
    for at in range(1, weights_ref.shape[0]):
        weight_sum = weight_sum + weights_ref[at]
    weight_sum = jnp.full((8, columns), weight_sum.astype(jnp.float32))
    scale = (SHEAR / 48) / weight_sum

    spans = filter_layers([design(0, layer) for layer in range(-2, layers + 2)])
    recs = [
        jnp.where(inside(layer), 1.0 / jnp.where(inside(layer), span, 1.0), 0.0)
        for layer, span in zip(range(-1, layers + 1), spans)
    ]
    shares = filter_layers(recs)
    total = jnp.zeros((8, columns), jnp.float32)
    for layer in range(layers):
        rec_ref[layer] = recs[layer + 1]
        for chunk_at in range(0, rows, 8):
            chunk = pl.ds(chunk_at, 8)
            sens = weight_ref[layer, chunk] * (node_ref[12 + layer, chunk] * scale)
            sens_ref[pl.ds(layer * rows + chunk_at, 8)] = sens
            total = total + sens * shares[layer][chunk_at : chunk_at + 8]
    sens_ref[pl.ds(layers * rows, 8)] = total
    for case in range(cases):
        pltpu.make_async_copy(disp_ref.at[case], disp_hbm.at[case], disp_sem.at[case]).wait()


def stage_kernel(labels_ref, density_ref, forces_ref, marks_ref, own_density_ref, own_forces_ref):
    marks_ref[...] = labels_ref[...].astype(jnp.float32)
    own_density_ref[...] = density_ref[...]
    own_forces_ref[...] = forces_ref[...]


def design_kernel(count_load, *refs):
    marks_ref = refs[0]
    density_refs = refs[1 : 1 + count_load]
    out_ref = refs[-1]
    load = lax.axis_index("load")
    own_rows = density_refs[0].shape[1]
    for step in range(count_load):
        start = pl.multiple_of(partner(load, step, count_load) * own_rows, own_rows)
        out_ref[0, :, pl.ds(start, own_rows)] = density_refs[step][...]
    out_ref[1] = marks_ref[...]


def sum_kernel(rows, *refs):
    sum_ref, first_ref, second_ref = refs[-3:]
    total = refs[0][...]
    for ref in refs[1:-3]:
        total = total + ref[...]
    sum_ref[...] = total
    end = total.shape[0] - 8
    top, bottom, share = total[end - rows : end], total[:rows], total[end:]
    even = lax.axis_index("gz") % 2 == 0
    first_ref[:rows] = jnp.where(even, top, bottom)
    first_ref[rows:] = share
    second_ref[...] = jnp.where(even, bottom, top)


def update_kernel(count_gz, *refs):
    sum_ref, first_ref, second_ref = refs[:3]
    share_refs = refs[3:-5]
    rec_ref, density_ref, marks_ref, new_ref, filt_ref = refs[-5:]
    layers, own_rows, columns = density_ref.shape
    rows = marks_ref.shape[1]
    load = lax.axis_index("load")
    even = lax.axis_index("gz") % 2 == 0
    first, second = first_ref[:rows], second_ref[...]
    numers = [jnp.where(even, second, first)]
    numers += [sum_ref[layer * rows : (layer + 1) * rows] for layer in range(layers)]
    numers += [jnp.where(even, first, second)]
    for layer, numer in enumerate(filter_layers(numers)):
        filt_ref[layer] = numer * rec_ref[layer]
    total = sum_ref[layers * rows :] + first_ref[rows:]
    for ref in share_refs:
        total = total + ref[...]
    mean = jnp.sum(total, keepdims=True) * (1.0 / (count_gz * layers * rows * columns))
    mean = jnp.broadcast_to(mean, (own_rows, columns))
    start = pl.multiple_of(load * own_rows, own_rows)
    for layer in range(layers):
        density = density_ref[layer]
        candidate = density * jnp.sqrt(filt_ref[layer, pl.ds(start, own_rows)] / mean)
        lower = jnp.maximum(density - MOVE_LIMIT, FLOOR_DENSITY)
        upper = jnp.minimum(density + MOVE_LIMIT, 1.0)
        updated = jnp.minimum(jnp.maximum(candidate, lower), upper)
        new_ref[layer] = jnp.where(marks_ref[layer, pl.ds(start, own_rows)] == 2.0, 1.0, updated)


def partner(index, step, count):
    if count & (count - 1) == 0:
        return index ^ step
    return (index + step) % count


def met(block, axis, step):
    count = lax.axis_size(axis)
    return lax.ppermute(block, axis, [(partner(i, step, count), i) for i in range(count)])


def swapped(block, axis, distance, odd):
    count = lax.axis_size(axis)
    low = [i for i in range(count - distance) if i // distance % 2 == odd]
    return lax.ppermute(block, axis, [(i, i + distance) for i in low] + [(i + distance, i) for i in low])


def on_device(density, labels, forces, case_weights):
    count_gz, count_load = lax.axis_size("gz"), lax.axis_size("load")
    cases, _, layers, rows, columns = forces.shape
    nodes = layers + 2 * SWEEPS + 1
    hops = -(-(SWEEPS + 1) // layers)
    vmem = pl.BlockSpec(memory_space=pltpu.VMEM)
    plane = (rows, columns)
    f32 = jnp.float32
    plane_bytes = rows * columns * 4

    def call(kernel, out, scratch, planes, cost, *args):
        return pl.pallas_call(
            kernel,
            out_shape=out,
            in_specs=[vmem] * len(args),
            out_specs=vmem if not isinstance(out, tuple) else (vmem,) * len(out),
            scratch_shapes=[pltpu.VMEM(shape, f32) for shape in scratch],
            compiler_params=pltpu.CompilerParams(vmem_limit_bytes=planes * plane_bytes + (4 << 20)),
            cost_estimate=pl.CostEstimate(flops=cost, bytes_accessed=cost // 10, transcendentals=0),
        )(*args)

    def along_gz(block):
        return [swapped(block, "gz", far, odd) for far in range(1, hops + 1) for odd in range(2)]

    shape = jax.ShapeDtypeStruct
    marks, own_density, own_forces = call(
        stage_kernel,
        (shape(labels.shape, f32), shape(density.shape, f32), shape(forces.shape, f32)),
        [],
        6 * layers + 4 * cases * 3 * layers,
        1_000_000,
        labels,
        density,
        forces,
    )
    force_swaps = along_gz(forces)
    early = force_swaps[-2:]
    design = pl.pallas_call(
        functools.partial(design_kernel, count_load),
        out_shape=shape((2, layers) + plane, f32),
        in_specs=[vmem] * (1 + count_load) + [pl.BlockSpec(memory_space=pl.ANY)] * len(early),
        out_specs=vmem,
        cost_estimate=pl.CostEstimate(flops=1_000_000, bytes_accessed=100_000, transcendentals=0),
    )(marks, own_density, *[met(density, "load", step) for step in range(1, count_load)], *early)
    design_blocks = [design] + along_gz(design)

    hbm = pl.BlockSpec(memory_space=pltpu.HBM)
    smooth_planes = nodes * 8 + 3 * (layers + 1) + 24 + 24 + layers
    smooth_planes += 2 * len(design_blocks) * (cases * 3 + 2) * layers + 8 * cases * layers
    displacement, sens, rec = pl.pallas_call(
        functools.partial(smooth_kernel, hops, count_gz),
        out_shape=(
            shape(forces.shape, f32),
            shape((layers * rows + 8, columns), f32),
            shape((layers,) + plane, f32),
        ),
        in_specs=[pl.BlockSpec(memory_space=pltpu.SMEM)] + [vmem] * (2 * len(design_blocks)),
        out_specs=(hbm, vmem, vmem),
        scratch_shapes=[
            pltpu.VMEM((nodes - 1,) + plane, f32),
            pltpu.VMEM((nodes,) + plane, f32),
            pltpu.VMEM((3, nodes) + plane, f32),
            pltpu.VMEM((3, nodes) + plane, f32),
            pltpu.VMEM((3, layers + 1) + plane, f32),
            pltpu.VMEM((2, 12) + plane, f32),
            pltpu.VMEM((12,) + plane, f32),
            pltpu.VMEM((12 + layers,) + plane, f32),
            pltpu.VMEM(forces.shape, f32),
            pltpu.VMEM((layers,) + plane, f32),
            pltpu.SemaphoreType.DMA((cases,)),
        ],
        compiler_params=pltpu.CompilerParams(vmem_limit_bytes=smooth_planes * plane_bytes + (4 << 20)),
        cost_estimate=pl.CostEstimate(flops=60_000_000, bytes_accessed=2_000_000, transcendentals=0),
    )(case_weights, *design_blocks, own_forces, *force_swaps)

    whole, first, second = call(
        functools.partial(sum_kernel, rows),
        (shape(sens.shape, f32), shape((rows + 8, columns), f32), shape(plane, f32)),
        [],
        2 * (count_load + 3) * (layers + 1),
        1_000_000,
        sens,
        *[met(sens, "load", step) for step in range(1, count_load)],
    )
    share = whole[layers * rows :]
    new_density = call(
        functools.partial(update_kernel, count_gz),
        shape(density.shape, f32),
        [(layers,) + plane],
        10 * layers + 4 + count_gz,
        1_000_000,
        whole,
        swapped(first, "gz", 1, 0),
        swapped(second, "gz", 1, 1),
        *[met(share, "gz", step) for step in range(2, count_gz)],
        rec,
        own_density,
        marks,
    )
    return (new_density, displacement)


def solution(mesh):
    return jax.shard_map(
        on_device,
        mesh=mesh,
        in_specs=(
            P("gz", "load", None),
            P("gz", None, None),
            P("load", None, "gz", None, None),
            P(),
        ),
        out_specs=(P("gz", "load", None), P("load", None, "gz", None, None)),
        check_vma=False,
    )
```

```python
import functools

import jax
import jax.numpy as jnp
from jax import lax
from jax.experimental import pallas as pl
from jax.experimental.pallas import tpu as pltpu
from jax.sharding import PartitionSpec as P

SWEEPS = 3
EMIN = 0.001
LOWER_EIG = 0.1
UPPER_EIG = 2.5
MOVE_LIMIT = 0.2
FLOOR_DENSITY = 0.001
POISSON = 0.3
LAME = POISSON / ((1 + POISSON) * (1 - 2 * POISSON))
SHEAR = 1.0 / (2 * (1 + POISSON))
KE_DIAG = (LAME + 4 * SHEAR) / 9
EDGE = 1.5 - 2.0**0.5
PLANE = ("ss", "sd", "ds", "dd")


def chunks_of(rows):
    return [pl.ds(at, 8) for at in range(0, rows, 8)]


def next_x(a):
    lanes = a.shape[1]
    lane = lax.broadcasted_iota(jnp.int32, a.shape, 1)
    return jnp.where(lane == lanes - 1, 0.0, pltpu.roll(a, lanes - 1, 1))


def last_x(a):
    lane = lax.broadcasted_iota(jnp.int32, a.shape, 1)
    return jnp.where(lane == 0, 0.0, pltpu.roll(a, 1, 1))


def next_y(plane):
    row = lax.broadcasted_iota(jnp.int32, plane[0].shape, 0)
    rolled = [pltpu.roll(a, 7, 0) for a in plane] + [jnp.zeros_like(plane[0])]
    return [jnp.where(row == 7, rolled[at + 1], rolled[at]) for at in range(len(plane))]


def last_y(plane):
    row = lax.broadcasted_iota(jnp.int32, plane[0].shape, 0)
    rolled = [jnp.zeros_like(plane[0])] + [pltpu.roll(a, 1, 0) for a in plane]
    return [jnp.where(row == 0, rolled[at], rolled[at + 1]) for at in range(len(plane))]


def add(*planes):
    return [sum(chunks[1:], chunks[0]) for chunks in zip(*planes)]


def sub(one, other):
    return [a - b for a, b in zip(one, other)]


def to_modes_xy(u):
    ux = [next_x(a) for a in u]
    s, d = add(ux, u), sub(ux, u)
    sy, dy = next_y(s), next_y(d)
    return add(sy, s), sub(sy, s), add(dy, d), sub(dy, d)


def from_modes_xy(ss, sd, ds, dd):
    s = add(sub(ss, sd), last_y(add(ss, sd)))
    d = add(sub(ds, dd), last_y(add(ds, dd)))
    return add(sub(s, d), [last_x(a) for a in add(s, d)])


def modes_z(low, high):
    modes = []
    for comp in range(3):
        one = {}
        for pq in PLANE:
            if pq != "ss":
                one[pq + "s"] = high[comp][pq] + low[comp][pq]
            one[pq + "d"] = high[comp][pq] - low[comp][pq]
        modes.append(one)
    return modes


NORMAL = ((0, "dss"), (1, "sds"), (2, "ssd"))
BENDS = (((1, "dds"), (2, "dsd")), ((0, "dds"), (2, "sdd")), ((0, "dsd"), (1, "sdd")))
SHEARS = (((0, "sds"), (1, "dss")), ((0, "ssd"), (2, "dss")), ((1, "ssd"), (2, "sds")))
STIFF = (SHEAR / 16, SHEAR / 48, (LAME + 4 * SHEAR) / 144, SHEAR / 8)
TWIST = ((0, "sdd"), (1, "dsd"), (2, "dds"))


def mode_forces(modes, e1, e2, e3, e4):
    m = lambda key: modes[key[0]][key[1]]
    out = [{}, {}, {}]

    def put(key, value):
        out[key[0]][key[1]] = value

    trace = (LAME / (2 * SHEAR)) * (m(NORMAL[0]) + m(NORMAL[1]) + m(NORMAL[2]))
    for key in NORMAL:
        put(key, e4 * (trace + m(key)))
    for a, b in BENDS:
        t = (LAME / (3 * SHEAR)) * (m(a) + m(b))
        put(a, e1 * (t + m(a)))
        put(b, e1 * (t + m(b)))
    for a, b in SHEARS:
        f = e1 * (m(a) + m(b))
        put(a, f)
        put(b, f)
    t = m(TWIST[0]) + m(TWIST[1]) + m(TWIST[2])
    for key in TWIST:
        put(key, e2 * (t + m(key)))
    for comp in range(3):
        put((comp, "ddd"), e3 * modes[comp]["ddd"])
    return out


def mode_energy(modes):
    m = lambda key: modes[key[0]][key[1]]
    sq = lambda v: v * v
    n = [m(key) for key in NORMAL]
    total = (3 * LAME / SHEAR) * sq(n[0] + n[1] + n[2]) + 6.0 * (sq(n[0]) + sq(n[1]) + sq(n[2]))
    shear = None
    for a, b in SHEARS:
        t = sq(m(a) + m(b))
        shear = t if shear is None else shear + t
    total = total + 3.0 * shear
    sums, own = None, None
    for a, b in BENDS:
        t = sq(m(a) + m(b))
        o = sq(m(a)) + sq(m(b))
        sums = t if sums is None else sums + t
        own = o if own is None else own + o
    total = total + (LAME / SHEAR) * sums + 3.0 * own
    a, b, c = (m(key) for key in TWIST)
    total = total + (sq(a + b) + sq(a + c) + sq(b + c))
    bulk = sq(modes[0]["ddd"]) + sq(modes[1]["ddd"]) + sq(modes[2]["ddd"])
    return total + ((LAME + 4 * SHEAR) / (3 * SHEAR)) * bulk


def filter_planes(plane):
    x = [last_x(a) + next_x(a) for a in plane]
    cross = add(x, add(last_y(plane), next_y(plane)))
    diagonal = add(last_y(x), next_y(x))
    near = [1.5 * a + 0.5 * c + EDGE * d for a, c, d in zip(plane, cross, diagonal)]
    return near, [0.5 * a + EDGE * c for a, c in zip(plane, cross)]


def filter_layers(layers):
    pairs = [filter_planes(plane) for plane in layers]
    return [
        add(pairs[at][0], add(pairs[at - 1][1], pairs[at + 1][1])) for at in range(1, len(layers) - 1)
    ]


def partner(index, step):
    return index ^ step


def smooth_kernel(hops, count_gz, *refs):
    blocks = 1 + 2 * hops
    weights_ref = refs[0]
    pack_refs = refs[1 : 1 + blocks]
    disp_hbm, own_ref = refs[1 + blocks : 3 + blocks]
    slot_refs = refs[3 + blocks : -11]
    stiff_ref, inv_ref, res_ref, step_ref, sol_ref, mode_ref, node_ref = refs[-11:-4]
    disp_ref, weight_ref, energy_ref, disp_sem = refs[-4:]

    cases, _, layers, rows, columns = disp_ref.shape
    nodes = layers + 2 * SWEEPS + 1
    chunks = chunks_of(rows)
    gz = lax.axis_index("gz")
    load = lax.axis_index("load")
    even = gz % 2 == 0

    def packed(layer, group, kind):
        hop = layer // layers
        plane = pack_plane(cases, layers, group, kind, layer - hop * layers)
        if hop == 0:
            return [pack_refs[0][plane, chunk] for chunk in chunks]
        far = abs(hop)
        beside, across = pack_refs[2 * far - 1], pack_refs[2 * far]
        by_sibling = even == (hop > 0)
        return [jnp.where(by_sibling, beside[plane, chunk], across[plane, chunk]) for chunk in chunks]

    def inside(layer):
        owner = gz + layer // layers
        return jnp.logical_and(owner >= 0, owner < count_gz)

    below = None
    for at in range(nodes + 1):
        layer = at - SWEEPS - 1
        live = jnp.where(inside(layer), 1.0, 0.0)
        marks = packed(layer, cases, 1)
        moduli = []
        for chunk_at, (dense, mark) in enumerate(zip(packed(layer, cases, 0), marks)):
            solid = jnp.where(mark == 2.0, 1.0, dense)
            modulus = (EMIN + (1.0 - EMIN) * solid * solid * solid) * live
            moduli.append(modulus)
            if 0 <= layer < layers:
                weight = (3.0 * (1.0 - EMIN)) * solid * solid * dense
                weight_ref[layer, pl.ds(8 + 8 * chunk_at, 8)] = weight
            if 1 <= at < nodes:
                for kind, factor in enumerate(STIFF):
                    stiff_ref[kind, at - 1, chunks[chunk_at]] = modulus * factor
        spread = add(moduli, [last_x(a) for a in moduli])
        spread = add(spread, last_y(spread))
        if at > 0:
            for chunk, mark, low, high in zip(chunks, marks, below, spread):
                free = jnp.logical_and(mark != 1.0, inside(layer))
                diag = jnp.where(free, KE_DIAG * (low + high), 1.0)
                inv_ref[at - 1, chunk] = jnp.where(free, 1.0 / diag, 0.0)
        below = spread

    theta = 0.5 * (UPPER_EIG + LOWER_EIG)
    delta = 0.5 * (UPPER_EIG - LOWER_EIG)
    sigma = theta / delta

    def load_modes(node, chunk):
        return [
            {pq: mode_ref[node, comp * 4 + i, chunk] for i, pq in enumerate(PLANE)}
            for comp in range(3)
        ]

    def store_modes(node, comp, field):
        for i, plane in enumerate(to_modes_xy(field)):
            for chunk, a in zip(chunks, plane):
                mode_ref[node, comp * 4 + i, chunk] = a

    def one_case(case, carry):
        for at in range(nodes):
            for comp in range(3):
                field = []
                for chunk, force in zip(chunks, packed(at - SWEEPS, case, comp)):
                    step = inv_ref[at, chunk] * force * (1.0 / theta)
                    field.append(step)
                    if 1 <= at < nodes - 1:
                        step_ref[comp, at, chunk] = step
                    if SWEEPS <= at <= SWEEPS + layers:
                        sol_ref[comp, at - SWEEPS, chunk] = step
                store_modes(at, comp, field)

        factor = 1.0 / sigma
        for sweep in range(1, SWEEPS + 1):
            factor_next = 1.0 / (2.0 * sigma - factor)
            keep, take = factor_next * factor, 2.0 * factor_next / delta
            first, end = sweep - 1, nodes - sweep
            if sweep > 1:
                for node in range(first, end + 1):
                    for comp in range(3):
                        store_modes(node, comp, [step_ref[comp, node, chunk] for chunk in chunks])
            for chunk in chunks:
                low = load_modes(first, chunk)
                up = None
                for element in range(first, end):
                    high = load_modes(element + 1, chunk)
                    stiff = [stiff_ref[kind, element, chunk] for kind in range(4)]
                    f = mode_forces(modes_z(low, high), *stiff)
                    ups = []
                    for comp in range(3):
                        for i, pq in enumerate(PLANE):
                            diff = f[comp][pq + "d"]
                            at = comp * 4 + i
                            if pq == "ss":
                                ups.append(diff)
                                if up:
                                    node_ref[element, at, chunk] = up[at] - diff
                            else:
                                both = f[comp][pq + "s"]
                                ups.append(both + diff)
                                if up:
                                    node_ref[element, at, chunk] = up[at] + (both - diff)
                    low, up = high, ups
            for node in range(first + 1, end):
                for comp in range(3):
                    g = [[node_ref[node, comp * 4 + i, chunk] for chunk in chunks] for i in range(4)]
                    if sweep == 1:
                        before = packed(node - SWEEPS, case, comp)
                    else:
                        before = [res_ref[comp, node, chunk] for chunk in chunks]
                    for chunk, res in zip(chunks, sub(before, from_modes_xy(*g))):
                        step = keep * step_ref[comp, node, chunk] + take * (inv_ref[node, chunk] * res)
                        if sweep < SWEEPS:
                            res_ref[comp, node, chunk] = res
                            step_ref[comp, node, chunk] = step
                        if SWEEPS <= node <= SWEEPS + layers:
                            sol = sol_ref[comp, node - SWEEPS, chunk] + step
                            sol_ref[comp, node - SWEEPS, chunk] = sol
                            if sweep == SWEEPS and node < SWEEPS + layers:
                                disp_ref[case, comp, node - SWEEPS, chunk] = sol
            factor = factor_next
        pltpu.make_async_copy(disp_ref.at[case], disp_hbm.at[case], disp_sem.at[case]).start()

        weight = weights_ref[load * cases + case].astype(jnp.float32)
        for node in range(layers + 1):
            for comp in range(3):
                store_modes(node, comp, [sol_ref[comp, node, chunk] for chunk in chunks])
        for chunk in chunks:
            low = load_modes(0, chunk)
            for layer in range(layers):
                high = load_modes(layer + 1, chunk)
                energy = weight * mode_energy(modes_z(low, high))
                before = jnp.where(case == 0, 0.0, energy_ref[layer, chunk])
                energy_ref[layer, chunk] = before + energy
                low = high
        return carry

    lax.fori_loop(0, cases, one_case, 0)
    weight_sum = weights_ref[0]
    for at in range(1, weights_ref.shape[0]):
        weight_sum = weight_sum + weights_ref[at]
    weight_sum = jnp.full((8, columns), weight_sum.astype(jnp.float32))
    scale = (SHEAR / 48) / weight_sum

    spans = filter_layers([packed(layer, cases, 0) for layer in range(-2, layers + 2)])
    recs = [
        [jnp.where(inside(layer), 1.0 / jnp.where(inside(layer), a, 1.0), 0.0) for a in span]
        for layer, span in zip(range(-1, layers + 1), spans)
    ]
    shares = filter_layers(recs)
    total = jnp.zeros((8, columns), jnp.float32)
    own_rows = own_ref.shape[2]
    own = pl.ds(pl.multiple_of(load * own_rows, own_rows), own_rows)
    for layer in range(layers):
        for kind in range(2):
            own_ref[1 + kind, layer] = pack_refs[0][pack_plane(cases, layers, cases, kind, layer), own]
        for at, chunk in enumerate(chunks):
            inner = pl.ds(8 + 8 * at, 8)
            sens = weight_ref[layer, inner] * (energy_ref[layer, chunk] * scale)
            weight_ref[layer, inner] = sens
            total = total + sens * shares[layer][at]
            energy_ref[layer, chunk] = recs[layer + 1][at]
        own_ref[0, layer] = energy_ref[layer, own]
        weight_ref[layer, :8] = jnp.zeros((8, columns), jnp.float32)
        weight_ref[layer, 8 + rows :] = jnp.zeros((8, columns), jnp.float32)
    share = jnp.sum(total, axis=0, keepdims=True)
    wide = own_rows + 2
    for step, slot_ref in enumerate(slot_refs):
        start = pl.multiple_of(partner(load, step) * own_rows, own_rows)
        for layer in range(layers):
            window = weight_ref[layer, pl.ds(start, own_rows + 16)]
            slot_ref[layer * wide : (layer + 1) * wide] = window[7 : 7 + wide]
        slot_ref[layers * wide : layers * wide + 1] = share
    for case in range(cases):
        pltpu.make_async_copy(disp_ref.at[case], disp_hbm.at[case], disp_sem.at[case]).wait()


def pack_plane(cases, layers, group, kind, layer):
    return (group * 3 + kind) * layers + layer


def stage_kernel(labels_ref, forces_ref, pack_ref):
    cases, _, layers, _, _ = forces_ref.shape
    for case in range(cases):
        for comp in range(3):
            for layer in range(layers):
                pack_ref[pack_plane(cases, layers, case, comp, layer)] = forces_ref[case, comp, layer]
    for layer in range(layers):
        marks = labels_ref[layer].astype(jnp.float32)
        pack_ref[pack_plane(cases, layers, cases, 1, layer)] = marks


def design_kernel(cases, *refs):
    density_refs, pack_ref = refs[1:-1], refs[-1]
    layers, own_rows, _ = density_refs[0].shape
    load = lax.axis_index("load")
    for step, density_ref in enumerate(density_refs):
        start = pl.multiple_of(partner(load, step) * own_rows, own_rows)
        for layer in range(layers):
            plane = pack_plane(cases, layers, cases, 0, layer)
            pack_ref[plane, pl.ds(start, own_rows)] = density_ref[layer]


def sum_kernel(*refs):
    total = refs[0][...]
    for ref in refs[1:-1]:
        total = total + ref[...]
    refs[-1][...] = total


def forward_kernel(layers, wide, sum_ref, beside_ref, out_ref):
    even = lax.axis_index("gz") % 2 == 0
    end = layers * wide
    out_ref[:wide] = jnp.where(even, beside_ref[end - wide : end], beside_ref[:wide])
    out_ref[wide : wide + 1] = sum_ref[end : end + 1] + beside_ref[end : end + 1]


def share_kernel(wide, mine_ref, other_ref, out_ref):
    out_ref[...] = mine_ref[...]
    out_ref[wide : wide + 1] = mine_ref[wide : wide + 1] + other_ref[wide : wide + 1]


def chip_masks(count_gz):
    masks = []
    while 2 ** (len(masks) + 1) < count_gz:
        masks.append(2 ** (len(masks) + 1) - 1)
    return masks


def update_kernel(cells, masks, *refs):
    sum_ref, beside_ref, mine_ref = refs[:3]
    other_refs = refs[3:-2]
    own_ref, new_ref = refs[-2:]
    _, layers, own_rows, columns = own_ref.shape
    wide = own_rows + 2
    gz = lax.axis_index("gz")
    even, chip = gz % 2 == 0, gz // 2
    beside = jnp.where(even, beside_ref[:wide], beside_ref[(layers - 1) * wide : layers * wide])
    across = jnp.zeros((wide, columns), jnp.float32)
    for mask, other_ref in zip(masks, other_refs):
        borders = (chip ^ mask) == jnp.where(even, chip - 1, chip + 1)
        across = jnp.where(borders, other_ref[:wide], across)
    numers = [jnp.where(even, across, beside)]
    numers += [sum_ref[layer * wide : (layer + 1) * wide] for layer in range(layers)]
    numers += [jnp.where(even, beside, across)]
    near, far = [], []
    for numer in numers:
        back, mid, front = (numer[at : at + own_rows] for at in range(3))
        sides = back + front
        cross = sides + (last_x(mid) + next_x(mid))
        near.append(1.5 * mid + 0.5 * cross + EDGE * (last_x(sides) + next_x(sides)))
        far.append(0.5 * mid + EDGE * cross)
    total = mine_ref[wide : wide + 1] + other_refs[-1][wide : wide + 1]
    mean = jnp.sum(total, keepdims=True) * (1.0 / cells)
    mean = jnp.broadcast_to(mean, (own_rows, columns))
    for layer in range(layers):
        numer = near[layer + 1] + (far[layer] + far[layer + 2])
        filtered = numer * own_ref[0, layer]
        density = own_ref[1, layer]
        candidate = density * jnp.sqrt(filtered / mean)
        lower = jnp.maximum(density - MOVE_LIMIT, FLOOR_DENSITY)
        upper = jnp.minimum(density + MOVE_LIMIT, 1.0)
        updated = jnp.minimum(jnp.maximum(candidate, lower), upper)
        new_ref[layer] = jnp.where(own_ref[2, layer] == 2.0, 1.0, updated)


def met(block, axis, step):
    count = lax.axis_size(axis)
    return lax.ppermute(block, axis, [(partner(i, step), i) for i in range(count)])


def swapped_across(block, count):
    low = range(1, count - 1, 2)
    return lax.ppermute(block, "gz", [(i, i + 1) for i in low] + [(i + 1, i) for i in low])


def from_neighbours(pack, hops, count):
    beside, across = met(pack, "gz", 1), swapped_across(pack, count)
    blocks = [beside, across]
    for far in range(2, hops + 1):
        beside = met(across, "gz", 1)
        up = [(i - far, i) for i in range(0, count, 2) if i - far >= 0]
        down = [(i + far, i) for i in range(1, count, 2) if i + far < count]
        across = lax.ppermute(pack, "gz", up + down)
        blocks += [beside, across]
    return blocks


def on_device(density, labels, forces, case_weights):
    count_gz, count_load = lax.axis_size("gz"), lax.axis_size("load")
    cases, _, layers, rows, columns = forces.shape
    own_rows = density.shape[1]
    nodes = layers + 2 * SWEEPS + 1
    hops = -(-(SWEEPS + 1) // layers)
    wide = own_rows + 2
    f32 = jnp.float32
    plane = (rows, columns)
    plane_bytes = rows * columns * 4
    vmem = pl.BlockSpec(memory_space=pltpu.VMEM)
    smem = pl.BlockSpec(memory_space=pltpu.SMEM)

    def shape(*dims):
        return jax.ShapeDtypeStruct(dims, f32)

    def call(kernel, out, args, planes, flops, in_specs=None, scratch=(), **more):
        limit = planes * plane_bytes + (2 << 20)
        return pl.pallas_call(
            kernel,
            out_shape=out,
            in_specs=in_specs or [vmem] * len(args),
            out_specs=more.pop("out_specs", vmem),
            scratch_shapes=scratch,
            compiler_params=pltpu.CompilerParams(vmem_limit_bytes=limit),
            cost_estimate=pl.CostEstimate(flops=flops, bytes_accessed=flops // 10, transcendentals=0),
            **more,
        )(*args)

    planes = (cases * 3 + 2) * layers
    pack = call(stage_kernel, shape(planes, rows, columns), (labels, forces), 2 * planes, 1_000_000)
    densities = [density] + [met(density, "load", step) for step in range(1, count_load)]
    pack = call(
        functools.partial(design_kernel, cases),
        shape(planes, rows, columns),
        (pack, *densities),
        2 * planes + 2 * layers,
        100_000,
        input_output_aliases={0: 0},
    )
    packs = [pack] + from_neighbours(pack, hops, count_gz)

    slot_rows = -(-(layers * wide + 1) // 8) * 8
    scratch = [
        pltpu.VMEM((4, nodes - 1) + plane, f32),
        pltpu.VMEM((nodes,) + plane, f32),
        pltpu.VMEM((3, nodes) + plane, f32),
        pltpu.VMEM((3, nodes) + plane, f32),
        pltpu.VMEM((3, layers + 1) + plane, f32),
        pltpu.VMEM((nodes, 12) + plane, f32),
        pltpu.VMEM((nodes, 12) + plane, f32),
        pltpu.VMEM(forces.shape, f32),
        pltpu.VMEM((layers, rows + 16, columns), f32),
        pltpu.VMEM((layers,) + plane, f32),
        pltpu.SemaphoreType.DMA((cases,)),
    ]
    smooth_planes = nodes * 35 + 3 * (layers + 1) + 4 * layers
    smooth_planes += len(packs) * planes + cases * 3 * layers + 8 * layers
    displacement, own, *slots = call(
        functools.partial(smooth_kernel, hops, count_gz),
        (shape(*forces.shape), shape(3, layers, own_rows, columns))
        + (shape(slot_rows, columns),) * count_load,
        (case_weights, *packs),
        smooth_planes,
        60_000_000,
        in_specs=[smem] + [vmem] * len(packs),
        out_specs=(pl.BlockSpec(memory_space=pltpu.HBM),) + (vmem,) * (1 + count_load),
        scratch=scratch,
    )

    received = [met(slots[step], "load", step) for step in range(1, count_load)]
    whole = call(sum_kernel, shape(slot_rows, columns), (slots[0], *received), 2 * count_load, 100_000)
    beside = met(whole, "gz", 1)
    forward_rows = -(-(wide + 1) // 8) * 8
    mine = call(
        functools.partial(forward_kernel, layers, wide),
        shape(forward_rows, columns),
        (whole, beside),
        4 * layers,
        10_000,
    )
    others = []
    masks = chip_masks(count_gz)
    for mask in masks:
        if others:
            mine = call(
                functools.partial(share_kernel, wide),
                shape(forward_rows, columns),
                (mine, others[-1]),
                4,
                10_000,
            )
        others.append(met(mine, "gz", 2 * mask))
    new_density = call(
        functools.partial(update_kernel, float(count_gz * layers * rows * columns), masks),
        shape(*density.shape),
        (whole, beside, mine, *others, own),
        8 * layers,
        100_000,
    )
    return (new_density, displacement)


def solution(mesh):
    return jax.shard_map(
        on_device,
        mesh=mesh,
        in_specs=(
            P("gz", "load", None),
            P("gz", None, None),
            P("load", None, "gz", None, None),
            P(),
        ),
        out_specs=(P("gz", "load", None), P("load", None, "gz", None, None)),
        check_vma=False,
    )
```

```python
import functools

import jax
import jax.numpy as jnp
from jax import lax
from jax.experimental import pallas as pl
from jax.experimental.pallas import tpu as pltpu
from jax.sharding import PartitionSpec as P

SWEEPS = 3
EMIN = 0.001
LOWER_EIG = 0.1
UPPER_EIG = 2.5
MOVE_LIMIT = 0.2
FLOOR_DENSITY = 0.001
POISSON = 0.3
LAME = POISSON / ((1 + POISSON) * (1 - 2 * POISSON))
SHEAR = 1.0 / (2 * (1 + POISSON))
KE_DIAG = (LAME + 4 * SHEAR) / 9
EDGE = 1.5 - 2.0**0.5
PLANE = ("ss", "sd", "ds", "dd")


def chunks_of(rows):
    return [pl.ds(at, 8) for at in range(0, rows, 8)]


def next_x(a):
    lanes = a.shape[1]
    lane = lax.broadcasted_iota(jnp.int32, a.shape, 1)
    return jnp.where(lane == lanes - 1, 0.0, pltpu.roll(a, lanes - 1, 1))


def last_x(a):
    lane = lax.broadcasted_iota(jnp.int32, a.shape, 1)
    return jnp.where(lane == 0, 0.0, pltpu.roll(a, 1, 1))


def next_y(plane):
    row = lax.broadcasted_iota(jnp.int32, plane[0].shape, 0)
    rolled = [pltpu.roll(a, 7, 0) for a in plane] + [jnp.zeros_like(plane[0])]
    return [jnp.where(row == 7, rolled[at + 1], rolled[at]) for at in range(len(plane))]


def last_y(plane):
    row = lax.broadcasted_iota(jnp.int32, plane[0].shape, 0)
    rolled = [jnp.zeros_like(plane[0])] + [pltpu.roll(a, 1, 0) for a in plane]
    return [jnp.where(row == 0, rolled[at], rolled[at + 1]) for at in range(len(plane))]


def add(*planes):
    return [sum(chunks[1:], chunks[0]) for chunks in zip(*planes)]


def sub(one, other):
    return [a - b for a, b in zip(one, other)]


def to_modes_xy(u):
    ux = [next_x(a) for a in u]
    s, d = add(ux, u), sub(ux, u)
    sy, dy = next_y(s), next_y(d)
    return add(sy, s), sub(sy, s), add(dy, d), sub(dy, d)


def from_modes_xy(ss, sd, ds, dd):
    s = add(sub(ss, sd), last_y(add(ss, sd)))
    d = add(sub(ds, dd), last_y(add(ds, dd)))
    return add(sub(s, d), [last_x(a) for a in add(s, d)])


def modes_z(low, high):
    modes = []
    for comp in range(3):
        one = {}
        for pq in PLANE:
            if pq != "ss":
                one[pq + "s"] = high[comp][pq] + low[comp][pq]
            one[pq + "d"] = high[comp][pq] - low[comp][pq]
        modes.append(one)
    return modes


NORMAL = ((0, "dss"), (1, "sds"), (2, "ssd"))
BENDS = (((1, "dds"), (2, "dsd")), ((0, "dds"), (2, "sdd")), ((0, "dsd"), (1, "sdd")))
SHEARS = (((0, "sds"), (1, "dss")), ((0, "ssd"), (2, "dss")), ((1, "ssd"), (2, "sds")))
STIFF = (SHEAR / 16, SHEAR / 48, (LAME + 4 * SHEAR) / 144, SHEAR / 8)
TWIST = ((0, "sdd"), (1, "dsd"), (2, "dds"))


def mode_forces(modes, e1, e2, e3, e4):
    m = lambda key: modes[key[0]][key[1]]
    out = [{}, {}, {}]

    def put(key, value):
        out[key[0]][key[1]] = value

    trace = (LAME / (2 * SHEAR)) * (m(NORMAL[0]) + m(NORMAL[1]) + m(NORMAL[2]))
    for key in NORMAL:
        put(key, e4 * (trace + m(key)))
    for a, b in BENDS:
        t = (LAME / (3 * SHEAR)) * (m(a) + m(b))
        put(a, e1 * (t + m(a)))
        put(b, e1 * (t + m(b)))
    for a, b in SHEARS:
        f = e1 * (m(a) + m(b))
        put(a, f)
        put(b, f)
    t = m(TWIST[0]) + m(TWIST[1]) + m(TWIST[2])
    for key in TWIST:
        put(key, e2 * (t + m(key)))
    for comp in range(3):
        put((comp, "ddd"), e3 * modes[comp]["ddd"])
    return out


def mode_energy(modes):
    m = lambda key: modes[key[0]][key[1]]
    sq = lambda v: v * v
    n = [m(key) for key in NORMAL]
    total = (3 * LAME / SHEAR) * sq(n[0] + n[1] + n[2]) + 6.0 * (sq(n[0]) + sq(n[1]) + sq(n[2]))
    shear = None
    for a, b in SHEARS:
        t = sq(m(a) + m(b))
        shear = t if shear is None else shear + t
    total = total + 3.0 * shear
    sums, own = None, None
    for a, b in BENDS:
        t = sq(m(a) + m(b))
        o = sq(m(a)) + sq(m(b))
        sums = t if sums is None else sums + t
        own = o if own is None else own + o
    total = total + (LAME / SHEAR) * sums + 3.0 * own
    a, b, c = (m(key) for key in TWIST)
    total = total + (sq(a + b) + sq(a + c) + sq(b + c))
    bulk = sq(modes[0]["ddd"]) + sq(modes[1]["ddd"]) + sq(modes[2]["ddd"])
    return total + ((LAME + 4 * SHEAR) / (3 * SHEAR)) * bulk


def filter_planes(plane):
    x = [last_x(a) + next_x(a) for a in plane]
    cross = add(x, add(last_y(plane), next_y(plane)))
    diagonal = add(last_y(x), next_y(x))
    near = [1.5 * a + 0.5 * c + EDGE * d for a, c, d in zip(plane, cross, diagonal)]
    return near, [0.5 * a + EDGE * c for a, c in zip(plane, cross)]


def filter_layers(layers):
    pairs = [filter_planes(plane) for plane in layers]
    return [
        add(pairs[at][0], add(pairs[at - 1][1], pairs[at + 1][1])) for at in range(1, len(layers) - 1)
    ]


def partner(index, step):
    return index ^ step


def smooth_kernel(hops, count_gz, *refs):
    blocks = 1 + 2 * hops
    weights_ref = refs[0]
    pack_refs = refs[1 : 1 + blocks]
    disp_hbm, own_ref, keep_ref, send_ref = refs[1 + blocks : -11]
    stiff_ref, inv_ref, res_ref, step_ref, sol_ref, mode_ref, node_ref = refs[-11:-4]
    disp_ref, weight_ref, energy_ref, disp_sem = refs[-4:]

    cases, _, layers, rows, columns = disp_ref.shape
    nodes = layers + 2 * SWEEPS + 1
    chunks = chunks_of(rows)
    gz = lax.axis_index("gz")
    load = lax.axis_index("load")
    even = gz % 2 == 0

    def packed(layer, group, kind):
        hop = layer // layers
        plane = pack_plane(cases, layers, group, kind, layer - hop * layers)
        if hop == 0:
            return [pack_refs[0][plane, chunk] for chunk in chunks]
        far = abs(hop)
        beside, across = pack_refs[2 * far - 1], pack_refs[2 * far]
        by_sibling = even == (hop > 0)
        return [jnp.where(by_sibling, beside[plane, chunk], across[plane, chunk]) for chunk in chunks]

    def inside(layer):
        owner = gz + layer // layers
        return jnp.logical_and(owner >= 0, owner < count_gz)

    below = None
    for at in range(nodes + 1):
        layer = at - SWEEPS - 1
        live = jnp.where(inside(layer), 1.0, 0.0)
        marks = packed(layer, cases, 1)
        moduli = []
        for chunk_at, (dense, mark) in enumerate(zip(packed(layer, cases, 0), marks)):
            solid = jnp.where(mark == 2.0, 1.0, dense)
            modulus = (EMIN + (1.0 - EMIN) * solid * solid * solid) * live
            moduli.append(modulus)
            if 0 <= layer < layers:
                weight = (3.0 * (1.0 - EMIN)) * solid * solid * dense
                weight_ref[layer, pl.ds(8 + 8 * chunk_at, 8)] = weight
            if 1 <= at < nodes:
                for kind, factor in enumerate(STIFF):
                    stiff_ref[kind, at - 1, chunks[chunk_at]] = modulus * factor
        spread = add(moduli, [last_x(a) for a in moduli])
        spread = add(spread, last_y(spread))
        if at > 0:
            for chunk, mark, low, high in zip(chunks, marks, below, spread):
                free = jnp.logical_and(mark != 1.0, inside(layer))
                diag = jnp.where(free, KE_DIAG * (low + high), 1.0)
                inv_ref[at - 1, chunk] = jnp.where(free, 1.0 / diag, 0.0)
        below = spread

    theta = 0.5 * (UPPER_EIG + LOWER_EIG)
    delta = 0.5 * (UPPER_EIG - LOWER_EIG)
    sigma = theta / delta

    def load_modes(node, chunk):
        return [
            {pq: mode_ref[node, comp * 4 + i, chunk] for i, pq in enumerate(PLANE)}
            for comp in range(3)
        ]

    def store_modes(node, comp, field):
        for i, plane in enumerate(to_modes_xy(field)):
            for chunk, a in zip(chunks, plane):
                mode_ref[node, comp * 4 + i, chunk] = a

    def one_case(case, carry):
        for at in range(nodes):
            for comp in range(3):
                field = []
                for chunk, force in zip(chunks, packed(at - SWEEPS, case, comp)):
                    step = inv_ref[at, chunk] * force * (1.0 / theta)
                    field.append(step)
                    if 1 <= at < nodes - 1:
                        step_ref[comp, at, chunk] = step
                    if SWEEPS <= at <= SWEEPS + layers:
                        sol_ref[comp, at - SWEEPS, chunk] = step
                store_modes(at, comp, field)

        factor = 1.0 / sigma
        for sweep in range(1, SWEEPS + 1):
            factor_next = 1.0 / (2.0 * sigma - factor)
            keep, take = factor_next * factor, 2.0 * factor_next / delta
            first, end = sweep - 1, nodes - sweep
            if sweep > 1:
                for node in range(first, end + 1):
                    for comp in range(3):
                        store_modes(node, comp, [step_ref[comp, node, chunk] for chunk in chunks])
            for chunk in chunks:
                low = load_modes(first, chunk)
                up = None
                for element in range(first, end):
                    high = load_modes(element + 1, chunk)
                    stiff = [stiff_ref[kind, element, chunk] for kind in range(4)]
                    f = mode_forces(modes_z(low, high), *stiff)
                    ups = []
                    for comp in range(3):
                        for i, pq in enumerate(PLANE):
                            diff = f[comp][pq + "d"]
                            at = comp * 4 + i
                            if pq == "ss":
                                ups.append(diff)
                                if up:
                                    node_ref[element, at, chunk] = up[at] - diff
                            else:
                                both = f[comp][pq + "s"]
                                ups.append(both + diff)
                                if up:
                                    node_ref[element, at, chunk] = up[at] + (both - diff)
                    low, up = high, ups
            for node in range(first + 1, end):
                for comp in range(3):
                    g = [[node_ref[node, comp * 4 + i, chunk] for chunk in chunks] for i in range(4)]
                    if sweep == 1:
                        before = packed(node - SWEEPS, case, comp)
                    else:
                        before = [res_ref[comp, node, chunk] for chunk in chunks]
                    for chunk, res in zip(chunks, sub(before, from_modes_xy(*g))):
                        step = keep * step_ref[comp, node, chunk] + take * (inv_ref[node, chunk] * res)
                        if sweep < SWEEPS:
                            res_ref[comp, node, chunk] = res
                            step_ref[comp, node, chunk] = step
                        if SWEEPS <= node <= SWEEPS + layers:
                            sol = sol_ref[comp, node - SWEEPS, chunk] + step
                            sol_ref[comp, node - SWEEPS, chunk] = sol
                            if sweep == SWEEPS and node < SWEEPS + layers:
                                disp_ref[case, comp, node - SWEEPS, chunk] = sol
            factor = factor_next
        pltpu.make_async_copy(disp_ref.at[case], disp_hbm.at[case], disp_sem.at[case]).start()

        weight = weights_ref[load * cases + case].astype(jnp.float32)
        for node in range(layers + 1):
            for comp in range(3):
                store_modes(node, comp, [sol_ref[comp, node, chunk] for chunk in chunks])
        for chunk in chunks:
            low = load_modes(0, chunk)
            for layer in range(layers):
                high = load_modes(layer + 1, chunk)
                energy = weight * mode_energy(modes_z(low, high))
                before = jnp.where(case == 0, 0.0, energy_ref[layer, chunk])
                energy_ref[layer, chunk] = before + energy
                low = high
        return carry

    lax.fori_loop(0, cases, one_case, 0)
    weight_sum = weights_ref[0]
    for at in range(1, weights_ref.shape[0]):
        weight_sum = weight_sum + weights_ref[at]
    weight_sum = jnp.full((8, columns), weight_sum.astype(jnp.float32))
    scale = (SHEAR / 48) / weight_sum

    spans = filter_layers([packed(layer, cases, 0) for layer in range(-2, layers + 2)])
    recs = [
        [jnp.where(inside(layer), 1.0 / jnp.where(inside(layer), a, 1.0), 0.0) for a in span]
        for layer, span in zip(range(-1, layers + 1), spans)
    ]
    shares = filter_layers(recs)
    total = jnp.zeros((8, columns), jnp.float32)
    own_rows = own_ref.shape[2]
    own = pl.ds(pl.multiple_of(load * own_rows, own_rows), own_rows)
    for layer in range(layers):
        for kind in range(2):
            own_ref[1 + kind, layer] = pack_refs[0][pack_plane(cases, layers, cases, kind, layer), own]
        for at, chunk in enumerate(chunks):
            inner = pl.ds(8 + 8 * at, 8)
            sens = weight_ref[layer, inner] * (energy_ref[layer, chunk] * scale)
            weight_ref[layer, inner] = sens
            total = total + sens * shares[layer][at]
            energy_ref[layer, chunk] = recs[layer + 1][at]
        own_ref[0, layer] = energy_ref[layer, own]
        weight_ref[layer, :8] = jnp.zeros((8, columns), jnp.float32)
        weight_ref[layer, 8 + rows :] = jnp.zeros((8, columns), jnp.float32)
    share = jnp.sum(total, axis=0, keepdims=True)
    wide = own_rows + 2
    count_load = rows // own_rows
    for step in range(count_load):
        start = pl.multiple_of(partner(load, step) * own_rows, own_rows)
        slot_ref, base = (keep_ref, 0) if step < count_load // 2 else (send_ref, count_load // 2)
        at = (step - base) * (slot_ref.shape[0] * 2 // count_load)
        for layer in range(layers):
            window = weight_ref[layer, pl.ds(start, own_rows + 16)]
            slot_ref[at + layer * wide : at + (layer + 1) * wide] = window[7 : 7 + wide]
        slot_ref[at + layers * wide : at + layers * wide + 1] = share
    for case in range(cases):
        pltpu.make_async_copy(disp_ref.at[case], disp_hbm.at[case], disp_sem.at[case]).wait()


def pack_plane(cases, layers, group, kind, layer):
    return (group * 3 + kind) * layers + layer


def stage_kernel(labels_ref, forces_ref, pack_ref):
    cases, _, layers, _, _ = forces_ref.shape
    for case in range(cases):
        for comp in range(3):
            for layer in range(layers):
                pack_ref[pack_plane(cases, layers, case, comp, layer)] = forces_ref[case, comp, layer]
    for layer in range(layers):
        marks = labels_ref[layer].astype(jnp.float32)
        pack_ref[pack_plane(cases, layers, cases, 1, layer)] = marks


def join_kernel(one_ref, other_ref, out_ref):
    count = one_ref.shape[0]
    out_ref[:count] = one_ref[...]
    out_ref[count:] = other_ref[...]


def design_kernel(cases, pack_in_ref, near_ref, far_ref, pack_ref):
    count, layers, own_rows, _ = near_ref.shape
    load = lax.axis_index("load")
    for step in range(2 * count):
        start = pl.multiple_of(partner(load, step) * own_rows, own_rows)
        density_ref = near_ref if step < count else far_ref
        for layer in range(layers):
            plane = pack_plane(cases, layers, cases, 0, layer)
            pack_ref[plane, pl.ds(start, own_rows)] = density_ref[step % count, layer]


def halve_kernel(keep_ref, other_ref, keep_out_ref, send_out_ref):
    half = keep_out_ref.shape[0]
    keep_out_ref[...] = keep_ref[:half] + other_ref[:half]
    send_out_ref[...] = keep_ref[half:] + other_ref[half:]


def sum_kernel(keep_ref, other_ref, out_ref):
    out_ref[...] = keep_ref[...] + other_ref[...]


def forward_kernel(layers, wide, sum_ref, beside_ref, out_ref):
    even = lax.axis_index("gz") % 2 == 0
    end = layers * wide
    out_ref[:wide] = jnp.where(even, beside_ref[end - wide : end], beside_ref[:wide])
    out_ref[wide : wide + 1] = sum_ref[end : end + 1] + beside_ref[end : end + 1]


def share_kernel(wide, mine_ref, *refs):
    out_ref = refs[-1]
    out_ref[...] = mine_ref[...]
    out_ref[wide : wide + 1] = share_sum(wide, mine_ref, *refs[:-1])


def share_sum(wide, *refs):
    total = refs[0][wide : wide + 1]
    for ref in refs[1:]:
        total = total + ref[wide : wide + 1]
    return total


def chip_rounds(count_gz):
    edges = []
    while 2 ** (len(edges) + 1) < count_gz:
        edges.append(2 ** (len(edges) + 1) - 1)
    pairs = [edges[at : at + 2] for at in range(0, len(edges), 2)]
    return [pair + [pair[0] ^ pair[1]] if len(pair) == 2 else pair for pair in pairs]


def update_kernel(cells, rounds, *refs):
    sum_ref, beside_ref, mine_ref = refs[:3]
    other_refs = refs[3:-2]
    own_ref, new_ref = refs[-2:]
    _, layers, own_rows, columns = own_ref.shape
    wide = own_rows + 2
    gz = lax.axis_index("gz")
    even, chip = gz % 2 == 0, gz // 2
    beside = jnp.where(even, beside_ref[:wide], beside_ref[(layers - 1) * wide : layers * wide])
    across = jnp.zeros((wide, columns), jnp.float32)
    for mask, other_ref in zip(sum(rounds, []), other_refs):
        borders = (chip ^ mask) == jnp.where(even, chip - 1, chip + 1)
        across = jnp.where(borders, other_ref[:wide], across)
    numers = [jnp.where(even, across, beside)]
    numers += [sum_ref[layer * wide : (layer + 1) * wide] for layer in range(layers)]
    numers += [jnp.where(even, beside, across)]
    near, far = [], []
    for numer in numers:
        back, mid, front = (numer[at : at + own_rows] for at in range(3))
        sides = back + front
        cross = sides + (last_x(mid) + next_x(mid))
        near.append(1.5 * mid + 0.5 * cross + EDGE * (last_x(sides) + next_x(sides)))
        far.append(0.5 * mid + EDGE * cross)
    total = share_sum(wide, mine_ref, *other_refs[-len(rounds[-1]) :])
    mean = jnp.sum(total, keepdims=True) * (1.0 / cells)
    mean = jnp.broadcast_to(mean, (own_rows, columns))
    for layer in range(layers):
        numer = near[layer + 1] + (far[layer] + far[layer + 2])
        filtered = numer * own_ref[0, layer]
        density = own_ref[1, layer]
        candidate = density * jnp.sqrt(filtered / mean)
        lower = jnp.maximum(density - MOVE_LIMIT, FLOOR_DENSITY)
        upper = jnp.minimum(density + MOVE_LIMIT, 1.0)
        updated = jnp.minimum(jnp.maximum(candidate, lower), upper)
        new_ref[layer] = jnp.where(own_ref[2, layer] == 2.0, 1.0, updated)


def met(block, axis, step):
    count = lax.axis_size(axis)
    return lax.ppermute(block, axis, [(partner(i, step), i) for i in range(count)])


def swapped_across(block, count):
    low = range(1, count - 1, 2)
    return lax.ppermute(block, "gz", [(i, i + 1) for i in low] + [(i + 1, i) for i in low])


def from_neighbours(pack, hops, count):
    beside, across = met(pack, "gz", 1), swapped_across(pack, count)
    blocks = [beside, across]
    for far in range(2, hops + 1):
        beside = met(across, "gz", 1)
        up = [(i - far, i) for i in range(0, count, 2) if i - far >= 0]
        down = [(i + far, i) for i in range(1, count, 2) if i + far < count]
        across = lax.ppermute(pack, "gz", up + down)
        blocks += [beside, across]
    return blocks


def on_device(density, labels, forces, case_weights):
    count_gz, count_load = lax.axis_size("gz"), lax.axis_size("load")
    cases, _, layers, rows, columns = forces.shape
    own_rows = density.shape[1]
    nodes = layers + 2 * SWEEPS + 1
    hops = -(-(SWEEPS + 1) // layers)
    wide = own_rows + 2
    f32 = jnp.float32
    plane = (rows, columns)
    plane_bytes = rows * columns * 4
    vmem = pl.BlockSpec(memory_space=pltpu.VMEM)
    smem = pl.BlockSpec(memory_space=pltpu.SMEM)

    def shape(*dims):
        return jax.ShapeDtypeStruct(dims, f32)

    def call(kernel, out, args, planes, flops, in_specs=None, scratch=(), **more):
        limit = planes * plane_bytes + (2 << 20)
        return pl.pallas_call(
            kernel,
            out_shape=out,
            in_specs=in_specs or [vmem] * len(args),
            out_specs=more.pop("out_specs", vmem),
            scratch_shapes=scratch,
            compiler_params=pltpu.CompilerParams(vmem_limit_bytes=limit),
            cost_estimate=pl.CostEstimate(flops=flops, bytes_accessed=flops // 10, transcendentals=0),
            **more,
        )(*args)

    planes = (cases * 3 + 2) * layers
    pack = call(stage_kernel, shape(planes, rows, columns), (labels, forces), 2 * planes, 1_000_000)
    near = density[None]
    far = met(near, "load", 1)
    while 2 * near.shape[0] < count_load:
        count = near.shape[0]
        near = call(join_kernel, shape(2 * count, *density.shape), (near, far), 8 * layers, 10_000)
        far = met(near, "load", 2 * count)
    pack = call(
        functools.partial(design_kernel, cases),
        shape(planes, rows, columns),
        (pack, near, far),
        2 * planes + 2 * layers,
        100_000,
        input_output_aliases={0: 0},
    )
    packs = [pack] + from_neighbours(pack, hops, count_gz)

    slot_rows = -(-(layers * wide + 1) // 8) * 8
    scratch = [
        pltpu.VMEM((4, nodes - 1) + plane, f32),
        pltpu.VMEM((nodes,) + plane, f32),
        pltpu.VMEM((3, nodes) + plane, f32),
        pltpu.VMEM((3, nodes) + plane, f32),
        pltpu.VMEM((3, layers + 1) + plane, f32),
        pltpu.VMEM((nodes, 12) + plane, f32),
        pltpu.VMEM((nodes, 12) + plane, f32),
        pltpu.VMEM(forces.shape, f32),
        pltpu.VMEM((layers, rows + 16, columns), f32),
        pltpu.VMEM((layers,) + plane, f32),
        pltpu.SemaphoreType.DMA((cases,)),
    ]
    smooth_planes = nodes * 35 + 3 * (layers + 1) + 4 * layers
    smooth_planes += len(packs) * planes + cases * 3 * layers + 8 * layers
    displacement, own, kept, sent = call(
        functools.partial(smooth_kernel, hops, count_gz),
        (shape(*forces.shape), shape(3, layers, own_rows, columns))
        + (shape(count_load // 2 * slot_rows, columns),) * 2,
        (case_weights, *packs),
        smooth_planes,
        60_000_000,
        in_specs=[smem] + [vmem] * len(packs),
        out_specs=(pl.BlockSpec(memory_space=pltpu.HBM),) + (vmem,) * 3,
        scratch=scratch,
    )

    step = count_load // 2
    other = met(sent, "load", step)
    while step > 1:
        step //= 2
        kept, sent = call(
            halve_kernel,
            (shape(step * slot_rows, columns),) * 2,
            (kept, other),
            2 * count_load,
            10_000,
            out_specs=(vmem, vmem),
        )
        other = met(sent, "load", step)
    whole = call(sum_kernel, shape(slot_rows, columns), (kept, other), 4, 10_000)
    beside = met(whole, "gz", 1)
    forward_rows = -(-(wide + 1) // 8) * 8
    mine = call(
        functools.partial(forward_kernel, layers, wide),
        shape(forward_rows, columns),
        (whole, beside),
        4 * layers,
        10_000,
    )
    others = []
    rounds = chip_rounds(count_gz)
    for at, masks in enumerate(rounds):
        if at > 0:
            mine = call(
                functools.partial(share_kernel, wide),
                shape(forward_rows, columns),
                (mine, *others[-len(rounds[at - 1]) :]),
                8,
                10_000,
            )
        others += [met(mine, "gz", 2 * mask) for mask in masks]
    new_density = call(
        functools.partial(update_kernel, float(count_gz * layers * rows * columns), rounds),
        shape(*density.shape),
        (whole, beside, mine, *others, own),
        8 * layers,
        100_000,
    )
    return (new_density, displacement)


def solution(mesh):
    return jax.shard_map(
        on_device,
        mesh=mesh,
        in_specs=(
            P("gz", "load", None),
            P("gz", None, None),
            P("load", None, "gz", None, None),
            P(),
        ),
        out_specs=(P("gz", "load", None), P("load", None, "gz", None, None)),
        check_vma=False,
    )
```

```python
import functools

import jax
import jax.numpy as jnp
from jax import lax
from jax.experimental import pallas as pl
from jax.experimental.pallas import tpu as pltpu
from jax.sharding import PartitionSpec as P

SWEEPS = 3
EMIN = 0.001
LOWER_EIG = 0.1
UPPER_EIG = 2.5
MOVE_LIMIT = 0.2
FLOOR_DENSITY = 0.001
POISSON = 0.3
LAME = POISSON / ((1 + POISSON) * (1 - 2 * POISSON))
SHEAR = 1.0 / (2 * (1 + POISSON))
KE_DIAG = (LAME + 4 * SHEAR) / 9
EDGE = 1.5 - 2.0**0.5
PLANE = ("ss", "sd", "ds", "dd")


def chunks_of(rows):
    return [pl.ds(at, 8) for at in range(0, rows, 8)]


def next_x(a):
    lanes = a.shape[1]
    lane = lax.broadcasted_iota(jnp.int32, a.shape, 1)
    return jnp.where(lane == lanes - 1, 0.0, pltpu.roll(a, lanes - 1, 1))


def last_x(a):
    lane = lax.broadcasted_iota(jnp.int32, a.shape, 1)
    return jnp.where(lane == 0, 0.0, pltpu.roll(a, 1, 1))


def next_y(plane):
    row = lax.broadcasted_iota(jnp.int32, plane[0].shape, 0)
    rolled = [pltpu.roll(a, 7, 0) for a in plane] + [jnp.zeros_like(plane[0])]
    return [jnp.where(row == 7, rolled[at + 1], rolled[at]) for at in range(len(plane))]


def last_y(plane):
    row = lax.broadcasted_iota(jnp.int32, plane[0].shape, 0)
    rolled = [jnp.zeros_like(plane[0])] + [pltpu.roll(a, 1, 0) for a in plane]
    return [jnp.where(row == 0, rolled[at], rolled[at + 1]) for at in range(len(plane))]


def add(*planes):
    return [sum(chunks[1:], chunks[0]) for chunks in zip(*planes)]


def sub(one, other):
    return [a - b for a, b in zip(one, other)]


def to_modes_xy(u):
    ux = [next_x(a) for a in u]
    s, d = add(ux, u), sub(ux, u)
    sy, dy = next_y(s), next_y(d)
    return add(sy, s), sub(sy, s), add(dy, d), sub(dy, d)


def from_modes_xy(ss, sd, ds, dd):
    s = add(sub(ss, sd), last_y(add(ss, sd)))
    d = add(sub(ds, dd), last_y(add(ds, dd)))
    return add(sub(s, d), [last_x(a) for a in add(s, d)])


def modes_z(low, high):
    modes = []
    for comp in range(3):
        one = {}
        for pq in PLANE:
            if pq != "ss":
                one[pq + "s"] = high[comp][pq] + low[comp][pq]
            one[pq + "d"] = high[comp][pq] - low[comp][pq]
        modes.append(one)
    return modes


NORMAL = ((0, "dss"), (1, "sds"), (2, "ssd"))
BENDS = (((1, "dds"), (2, "dsd")), ((0, "dds"), (2, "sdd")), ((0, "dsd"), (1, "sdd")))
SHEARS = (((0, "sds"), (1, "dss")), ((0, "ssd"), (2, "dss")), ((1, "ssd"), (2, "sds")))
STIFF = (SHEAR / 16, SHEAR / 48, (LAME + 4 * SHEAR) / 144, SHEAR / 8)
TWIST = ((0, "sdd"), (1, "dsd"), (2, "dds"))


def mode_forces(modes, e1, e2, e3, e4):
    m = lambda key: modes[key[0]][key[1]]
    out = [{}, {}, {}]

    def put(key, value):
        out[key[0]][key[1]] = value

    trace = (LAME / (2 * SHEAR)) * (m(NORMAL[0]) + m(NORMAL[1]) + m(NORMAL[2]))
    for key in NORMAL:
        put(key, e4 * (trace + m(key)))
    for a, b in BENDS:
        t = (LAME / (3 * SHEAR)) * (m(a) + m(b))
        put(a, e1 * (t + m(a)))
        put(b, e1 * (t + m(b)))
    for a, b in SHEARS:
        f = e1 * (m(a) + m(b))
        put(a, f)
        put(b, f)
    t = m(TWIST[0]) + m(TWIST[1]) + m(TWIST[2])
    for key in TWIST:
        put(key, e2 * (t + m(key)))
    for comp in range(3):
        put((comp, "ddd"), e3 * modes[comp]["ddd"])
    return out


def mode_energy(modes):
    m = lambda key: modes[key[0]][key[1]]
    sq = lambda v: v * v
    n = [m(key) for key in NORMAL]
    total = (3 * LAME / SHEAR) * sq(n[0] + n[1] + n[2]) + 6.0 * (sq(n[0]) + sq(n[1]) + sq(n[2]))
    shear = None
    for a, b in SHEARS:
        t = sq(m(a) + m(b))
        shear = t if shear is None else shear + t
    total = total + 3.0 * shear
    sums, own = None, None
    for a, b in BENDS:
        t = sq(m(a) + m(b))
        o = sq(m(a)) + sq(m(b))
        sums = t if sums is None else sums + t
        own = o if own is None else own + o
    total = total + (LAME / SHEAR) * sums + 3.0 * own
    a, b, c = (m(key) for key in TWIST)
    total = total + (sq(a + b) + sq(a + c) + sq(b + c))
    bulk = sq(modes[0]["ddd"]) + sq(modes[1]["ddd"]) + sq(modes[2]["ddd"])
    return total + ((LAME + 4 * SHEAR) / (3 * SHEAR)) * bulk


def filter_planes(plane):
    x = [last_x(a) + next_x(a) for a in plane]
    cross = add(x, add(last_y(plane), next_y(plane)))
    diagonal = add(last_y(x), next_y(x))
    near = [1.5 * a + 0.5 * c + EDGE * d for a, c, d in zip(plane, cross, diagonal)]
    return near, [0.5 * a + EDGE * c for a, c in zip(plane, cross)]


def filter_layers(layers):
    pairs = [filter_planes(plane) for plane in layers]
    return [
        add(pairs[at][0], add(pairs[at - 1][1], pairs[at + 1][1])) for at in range(1, len(layers) - 1)
    ]


def partner(index, step):
    return index ^ step


def smooth_kernel(hops, count_gz, *refs):
    blocks = 1 + 2 * hops
    weights_ref = refs[0]
    pack_refs = refs[1 : 1 + blocks]
    disp_hbm, own_ref = refs[1 + blocks : 3 + blocks]
    slot_refs = refs[3 + blocks : -11]
    stiff_ref, inv_ref, res_ref, step_ref, sol_ref, mode_ref, node_ref = refs[-11:-4]
    disp_ref, weight_ref, energy_ref, disp_sem = refs[-4:]

    cases, _, layers, rows, columns = disp_ref.shape
    nodes = layers + 2 * SWEEPS + 1
    chunks = chunks_of(rows)
    gz = lax.axis_index("gz")
    load = lax.axis_index("load")
    even = gz % 2 == 0

    def packed(layer, group, kind):
        hop = layer // layers
        plane = pack_plane(cases, layers, group, kind, layer - hop * layers)
        if hop == 0:
            return [pack_refs[0][plane, chunk] for chunk in chunks]
        far = abs(hop)
        beside, across = pack_refs[2 * far - 1], pack_refs[2 * far]
        by_sibling = even == (hop > 0)
        return [jnp.where(by_sibling, beside[plane, chunk], across[plane, chunk]) for chunk in chunks]

    def inside(layer):
        owner = gz + layer // layers
        return jnp.logical_and(owner >= 0, owner < count_gz)

    below = None
    for at in range(nodes + 1):
        layer = at - SWEEPS - 1
        live = jnp.where(inside(layer), 1.0, 0.0)
        marks = packed(layer, cases, 1)
        moduli = []
        for chunk_at, (dense, mark) in enumerate(zip(packed(layer, cases, 0), marks)):
            solid = jnp.where(mark == 2.0, 1.0, dense)
            modulus = (EMIN + (1.0 - EMIN) * solid * solid * solid) * live
            moduli.append(modulus)
            if 0 <= layer < layers:
                weight = (3.0 * (1.0 - EMIN)) * solid * solid * dense
                weight_ref[layer, pl.ds(8 + 8 * chunk_at, 8)] = weight
            if 1 <= at < nodes:
                for kind, factor in enumerate(STIFF):
                    stiff_ref[kind, at - 1, chunks[chunk_at]] = modulus * factor
        spread = add(moduli, [last_x(a) for a in moduli])
        spread = add(spread, last_y(spread))
        if at > 0:
            for chunk, mark, low, high in zip(chunks, marks, below, spread):
                free = jnp.logical_and(mark != 1.0, inside(layer))
                diag = jnp.where(free, KE_DIAG * (low + high), 1.0)
                inv_ref[at - 1, chunk] = jnp.where(free, 1.0 / diag, 0.0)
        below = spread

    theta = 0.5 * (UPPER_EIG + LOWER_EIG)
    delta = 0.5 * (UPPER_EIG - LOWER_EIG)
    sigma = theta / delta

    def load_modes(node, chunk):
        return [
            {pq: mode_ref[node, comp * 4 + i, chunk] for i, pq in enumerate(PLANE)}
            for comp in range(3)
        ]

    def store_modes(node, comp, field):
        for i, plane in enumerate(to_modes_xy(field)):
            for chunk, a in zip(chunks, plane):
                mode_ref[node, comp * 4 + i, chunk] = a

    def one_case(case, carry):
        for at in range(nodes):
            for comp in range(3):
                field = []
                for chunk, force in zip(chunks, packed(at - SWEEPS, case, comp)):
                    step = inv_ref[at, chunk] * force * (1.0 / theta)
                    field.append(step)
                    if 1 <= at < nodes - 1:
                        step_ref[comp, at, chunk] = step
                    if SWEEPS <= at <= SWEEPS + layers:
                        sol_ref[comp, at - SWEEPS, chunk] = step
                store_modes(at, comp, field)

        factor = 1.0 / sigma
        for sweep in range(1, SWEEPS + 1):
            factor_next = 1.0 / (2.0 * sigma - factor)
            keep, take = factor_next * factor, 2.0 * factor_next / delta
            first, end = sweep - 1, nodes - sweep
            if sweep > 1:
                for node in range(first, end + 1):
                    for comp in range(3):
                        store_modes(node, comp, [step_ref[comp, node, chunk] for chunk in chunks])
            for chunk in chunks:
                low = load_modes(first, chunk)
                up = None
                for element in range(first, end):
                    high = load_modes(element + 1, chunk)
                    stiff = [stiff_ref[kind, element, chunk] for kind in range(4)]
                    f = mode_forces(modes_z(low, high), *stiff)
                    ups = []
                    for comp in range(3):
                        for i, pq in enumerate(PLANE):
                            diff = f[comp][pq + "d"]
                            at = comp * 4 + i
                            if pq == "ss":
                                ups.append(diff)
                                if up:
                                    node_ref[element, at, chunk] = up[at] - diff
                            else:
                                both = f[comp][pq + "s"]
                                ups.append(both + diff)
                                if up:
                                    node_ref[element, at, chunk] = up[at] + (both - diff)
                    low, up = high, ups
            for node in range(first + 1, end):
                for comp in range(3):
                    g = [[node_ref[node, comp * 4 + i, chunk] for chunk in chunks] for i in range(4)]
                    if sweep == 1:
                        before = packed(node - SWEEPS, case, comp)
                    else:
                        before = [res_ref[comp, node, chunk] for chunk in chunks]
                    for chunk, res in zip(chunks, sub(before, from_modes_xy(*g))):
                        step = keep * step_ref[comp, node, chunk] + take * (inv_ref[node, chunk] * res)
                        if sweep < SWEEPS:
                            res_ref[comp, node, chunk] = res
                            step_ref[comp, node, chunk] = step
                        if SWEEPS <= node <= SWEEPS + layers:
                            sol = sol_ref[comp, node - SWEEPS, chunk] + step
                            sol_ref[comp, node - SWEEPS, chunk] = sol
                            if sweep == SWEEPS and node < SWEEPS + layers:
                                disp_ref[case, comp, node - SWEEPS, chunk] = sol
            factor = factor_next
        pltpu.make_async_copy(disp_ref.at[case], disp_hbm.at[case], disp_sem.at[case]).start()

        weight = weights_ref[load * cases + case].astype(jnp.float32)
        for node in range(layers + 1):
            for comp in range(3):
                store_modes(node, comp, [sol_ref[comp, node, chunk] for chunk in chunks])
        for chunk in chunks:
            low = load_modes(0, chunk)
            for layer in range(layers):
                high = load_modes(layer + 1, chunk)
                energy = weight * mode_energy(modes_z(low, high))
                before = jnp.where(case == 0, 0.0, energy_ref[layer, chunk])
                energy_ref[layer, chunk] = before + energy
                low = high
        return carry

    lax.fori_loop(0, cases, one_case, 0)
    weight_sum = weights_ref[0]
    for at in range(1, weights_ref.shape[0]):
        weight_sum = weight_sum + weights_ref[at]
    weight_sum = jnp.full((8, columns), weight_sum.astype(jnp.float32))
    scale = (SHEAR / 48) / weight_sum

    spans = filter_layers(
        [[jnp.where(inside(at), a, 0.0) for a in packed(at, cases, 0)] for at in range(-2, layers + 2)]
    )
    recs = [
        [jnp.where(inside(layer), 1.0 / jnp.where(inside(layer), a, 1.0), 0.0) for a in span]
        for layer, span in zip(range(-1, layers + 1), spans)
    ]
    shares = filter_layers(recs)
    total = jnp.zeros((8, columns), jnp.float32)
    own_rows = own_ref.shape[2]
    own = pl.ds(pl.multiple_of(load * own_rows, own_rows), own_rows)
    for layer in range(layers):
        for kind in range(2):
            own_ref[1 + kind, layer] = pack_refs[0][pack_plane(cases, layers, cases, kind, layer), own]
        for at, chunk in enumerate(chunks):
            inner = pl.ds(8 + 8 * at, 8)
            sens = weight_ref[layer, inner] * (energy_ref[layer, chunk] * scale)
            weight_ref[layer, inner] = sens
            total = total + sens * shares[layer][at]
            energy_ref[layer, chunk] = recs[layer + 1][at]
        own_ref[0, layer] = energy_ref[layer, own]
        weight_ref[layer, :8] = jnp.zeros((8, columns), jnp.float32)
        weight_ref[layer, 8 + rows :] = jnp.zeros((8, columns), jnp.float32)
    share = jnp.sum(total, axis=0, keepdims=True)
    wide = own_rows + 2
    for step, slot_ref in enumerate(slot_refs):
        start = pl.multiple_of(partner(load, step) * own_rows, own_rows)
        for layer in range(layers):
            window = weight_ref[layer, pl.ds(start, own_rows + 16)]
            slot_ref[layer * wide : (layer + 1) * wide] = window[7 : 7 + wide]
        slot_ref[layers * wide : layers * wide + 1] = share
    for case in range(cases):
        pltpu.make_async_copy(disp_ref.at[case], disp_hbm.at[case], disp_sem.at[case]).wait()


def pack_plane(cases, layers, group, kind, layer):
    return (group * 3 + kind) * layers + layer


def stage_kernel(labels_ref, forces_ref, pack_ref):
    cases, _, layers, _, _ = forces_ref.shape
    for case in range(cases):
        for comp in range(3):
            for layer in range(layers):
                pack_ref[pack_plane(cases, layers, case, comp, layer)] = forces_ref[case, comp, layer]
    for layer in range(layers):
        marks = labels_ref[layer].astype(jnp.float32)
        pack_ref[pack_plane(cases, layers, cases, 1, layer)] = marks


def design_kernel(cases, *refs):
    density_refs, pack_ref = refs[1:-1], refs[-1]
    layers, own_rows, _ = density_refs[0].shape
    load = lax.axis_index("load")
    for step, density_ref in enumerate(density_refs):
        start = pl.multiple_of(partner(load, step) * own_rows, own_rows)
        for layer in range(layers):
            plane = pack_plane(cases, layers, cases, 0, layer)
            pack_ref[plane, pl.ds(start, own_rows)] = density_ref[layer]


def sum_kernel(*refs):
    total = refs[0][...]
    for ref in refs[1:-1]:
        total = total + ref[...]
    refs[-1][...] = total


def forward_kernel(layers, wide, sum_ref, beside_ref, out_ref):
    even = lax.axis_index("gz") % 2 == 0
    end = layers * wide
    out_ref[:wide] = jnp.where(even, beside_ref[end - wide : end], beside_ref[:wide])
    out_ref[wide : wide + 1] = sum_ref[end : end + 1] + beside_ref[end : end + 1]


def share_kernel(wide, mine_ref, *refs):
    out_ref = refs[-1]
    out_ref[...] = mine_ref[...]
    out_ref[wide : wide + 1] = share_sum(wide, mine_ref, *refs[:-1])


def share_sum(wide, *refs):
    total = refs[0][wide : wide + 1]
    for ref in refs[1:]:
        total = total + ref[wide : wide + 1]
    return total


def chip_rounds(count_gz):
    edges = []
    while 2 ** (len(edges) + 1) < count_gz:
        edges.append(2 ** (len(edges) + 1) - 1)
    pairs = [edges[at : at + 2] for at in range(0, len(edges), 2)]
    return [pair + [pair[0] ^ pair[1]] if len(pair) == 2 else pair for pair in pairs]


def update_kernel(cells, rounds, *refs):
    sum_ref, beside_ref, mine_ref = refs[:3]
    other_refs = refs[3:-2]
    own_ref, new_ref = refs[-2:]
    _, layers, own_rows, columns = own_ref.shape
    wide = own_rows + 2
    gz = lax.axis_index("gz")
    even, chip = gz % 2 == 0, gz // 2
    beside = jnp.where(even, beside_ref[:wide], beside_ref[(layers - 1) * wide : layers * wide])
    across = jnp.zeros((wide, columns), jnp.float32)
    for mask, other_ref in zip(sum(rounds, []), other_refs):
        borders = (chip ^ mask) == jnp.where(even, chip - 1, chip + 1)
        across = jnp.where(borders, other_ref[:wide], across)
    numers = [jnp.where(even, across, beside)]
    numers += [sum_ref[layer * wide : (layer + 1) * wide] for layer in range(layers)]
    numers += [jnp.where(even, beside, across)]
    near, far = [], []
    for numer in numers:
        back, mid, front = (numer[at : at + own_rows] for at in range(3))
        sides = back + front
        cross = sides + (last_x(mid) + next_x(mid))
        near.append(1.5 * mid + 0.5 * cross + EDGE * (last_x(sides) + next_x(sides)))
        far.append(0.5 * mid + EDGE * cross)
    total = share_sum(wide, mine_ref, *other_refs[-len(rounds[-1]) :])
    mean = jnp.sum(total, keepdims=True) * (1.0 / cells)
    mean = jnp.broadcast_to(mean, (own_rows, columns))
    for layer in range(layers):
        numer = near[layer + 1] + (far[layer] + far[layer + 2])
        filtered = numer * own_ref[0, layer]
        density = own_ref[1, layer]
        candidate = density * jnp.sqrt(filtered / mean)
        lower = jnp.maximum(density - MOVE_LIMIT, FLOOR_DENSITY)
        upper = jnp.minimum(density + MOVE_LIMIT, 1.0)
        updated = jnp.minimum(jnp.maximum(candidate, lower), upper)
        new_ref[layer] = jnp.where(own_ref[2, layer] == 2.0, 1.0, updated)


def met(block, axis, step):
    count = lax.axis_size(axis)
    return lax.ppermute(block, axis, [(partner(i, step), i) for i in range(count)])


def from_neighbours(pack, hops, count):
    low = range(1, count - 1, 2)
    pairs = [(i, i + 1) for i in low] + [(i + 1, i) for i in low] + [(0, 0), (count - 1, count - 1)]
    beside, across = met(pack, "gz", 1), lax.ppermute(pack, "gz", pairs)
    blocks = [beside, across]
    for far in range(2, hops + 1):
        beside = met(across, "gz", 1)
        up = [(i - far, i) for i in range(0, count, 2) if i - far >= 0]
        down = [(i + far, i) for i in range(1, count, 2) if i + far < count]
        free = [i for i in range(count) if i not in dict(up + down)]
        empty = [i for i in range(count) if i not in dict(up + down).values()]
        across = lax.ppermute(pack, "gz", up + down + list(zip(free, empty)))
        blocks += [beside, across]
    return blocks


def on_device(density, labels, forces, case_weights):
    count_gz, count_load = lax.axis_size("gz"), lax.axis_size("load")
    cases, _, layers, rows, columns = forces.shape
    own_rows = density.shape[1]
    nodes = layers + 2 * SWEEPS + 1
    hops = -(-(SWEEPS + 1) // layers)
    wide = own_rows + 2
    f32 = jnp.float32
    plane = (rows, columns)
    plane_bytes = rows * columns * 4
    vmem = pl.BlockSpec(memory_space=pltpu.VMEM)
    smem = pl.BlockSpec(memory_space=pltpu.SMEM)

    def shape(*dims):
        return jax.ShapeDtypeStruct(dims, f32)

    def call(kernel, out, args, planes, flops, in_specs=None, scratch=(), **more):
        limit = planes * plane_bytes + (2 << 20)
        return pl.pallas_call(
            kernel,
            out_shape=out,
            in_specs=in_specs or [vmem] * len(args),
            out_specs=more.pop("out_specs", vmem),
            scratch_shapes=scratch,
            compiler_params=pltpu.CompilerParams(vmem_limit_bytes=limit),
            cost_estimate=pl.CostEstimate(flops=flops, bytes_accessed=flops // 10, transcendentals=0),
            **more,
        )(*args)

    planes = (cases * 3 + 2) * layers
    pack = call(stage_kernel, shape(planes, rows, columns), (labels, forces), 2 * planes, 1_000_000)
    densities = [density] + [met(density, "load", step) for step in range(1, count_load)]
    pack = call(
        functools.partial(design_kernel, cases),
        shape(planes, rows, columns),
        (pack, *densities),
        2 * planes + 2 * layers,
        100_000,
        input_output_aliases={0: 0},
    )
    packs = [pack] + from_neighbours(pack, hops, count_gz)

    slot_rows = -(-(layers * wide + 1) // 8) * 8
    scratch = [
        pltpu.VMEM((4, nodes - 1) + plane, f32),
        pltpu.VMEM((nodes,) + plane, f32),
        pltpu.VMEM((3, nodes) + plane, f32),
        pltpu.VMEM((3, nodes) + plane, f32),
        pltpu.VMEM((3, layers + 1) + plane, f32),
        pltpu.VMEM((nodes, 12) + plane, f32),
        pltpu.VMEM((nodes, 12) + plane, f32),
        pltpu.VMEM(forces.shape, f32),
        pltpu.VMEM((layers, rows + 16, columns), f32),
        pltpu.VMEM((layers,) + plane, f32),
        pltpu.SemaphoreType.DMA((cases,)),
    ]
    smooth_planes = nodes * 35 + 3 * (layers + 1) + 4 * layers
    smooth_planes += len(packs) * planes + cases * 3 * layers + 8 * layers
    displacement, own, *slots = call(
        functools.partial(smooth_kernel, hops, count_gz),
        (shape(*forces.shape), shape(3, layers, own_rows, columns))
        + (shape(slot_rows, columns),) * count_load,
        (case_weights, *packs),
        smooth_planes,
        60_000_000,
        in_specs=[smem] + [vmem] * len(packs),
        out_specs=(pl.BlockSpec(memory_space=pltpu.HBM),) + (vmem,) * (1 + count_load),
        scratch=scratch,
    )

    received = [met(slots[step], "load", step) for step in range(1, count_load)]
    whole = call(sum_kernel, shape(slot_rows, columns), (slots[0], *received), 2 * count_load, 100_000)
    beside = met(whole, "gz", 1)
    forward_rows = -(-(wide + 1) // 8) * 8
    mine = call(
        functools.partial(forward_kernel, layers, wide),
        shape(forward_rows, columns),
        (whole, beside),
        4 * layers,
        10_000,
    )
    others = []
    rounds = chip_rounds(count_gz)
    for at, masks in enumerate(rounds):
        if at > 0:
            mine = call(
                functools.partial(share_kernel, wide),
                shape(forward_rows, columns),
                (mine, *others[-len(rounds[at - 1]) :]),
                8,
                10_000,
            )
        others += [met(mine, "gz", 2 * mask) for mask in masks]
    new_density = call(
        functools.partial(update_kernel, float(count_gz * layers * rows * columns), rounds),
        shape(*density.shape),
        (whole, beside, mine, *others, own),
        8 * layers,
        100_000,
    )
    return (new_density, displacement)


def solution(mesh):
    return jax.shard_map(
        on_device,
        mesh=mesh,
        in_specs=(
            P("gz", "load", None),
            P("gz", None, None),
            P("load", None, "gz", None, None),
            P(),
        ),
        out_specs=(P("gz", "load", None), P("load", None, "gz", None, None)),
        check_vma=False,
    )
```

```python
import functools

import jax
import jax.numpy as jnp
from jax import lax
from jax.experimental import pallas as pl
from jax.experimental.pallas import tpu as pltpu
from jax.sharding import PartitionSpec as P

SWEEPS = 3
EMIN = 0.001
LOWER_EIG = 0.1
UPPER_EIG = 2.5
MOVE_LIMIT = 0.2
FLOOR_DENSITY = 0.001
POISSON = 0.3
LAME = POISSON / ((1 + POISSON) * (1 - 2 * POISSON))
SHEAR = 1.0 / (2 * (1 + POISSON))
KE_DIAG = (LAME + 4 * SHEAR) / 9
EDGE = 1.5 - 2.0**0.5
PLANE = ("ss", "sd", "ds", "dd")


def chunks_of(rows):
    return [pl.ds(at, 8) for at in range(0, rows, 8)]


def next_x(a):
    lanes = a.shape[1]
    lane = lax.broadcasted_iota(jnp.int32, a.shape, 1)
    return jnp.where(lane == lanes - 1, 0.0, pltpu.roll(a, lanes - 1, 1))


def last_x(a):
    lane = lax.broadcasted_iota(jnp.int32, a.shape, 1)
    return jnp.where(lane == 0, 0.0, pltpu.roll(a, 1, 1))


def next_y(plane):
    row = lax.broadcasted_iota(jnp.int32, plane[0].shape, 0)
    rolled = [pltpu.roll(a, 7, 0) for a in plane] + [jnp.zeros_like(plane[0])]
    return [jnp.where(row == 7, rolled[at + 1], rolled[at]) for at in range(len(plane))]


def last_y(plane):
    row = lax.broadcasted_iota(jnp.int32, plane[0].shape, 0)
    rolled = [jnp.zeros_like(plane[0])] + [pltpu.roll(a, 1, 0) for a in plane]
    return [jnp.where(row == 0, rolled[at], rolled[at + 1]) for at in range(len(plane))]


def add(*planes):
    return [sum(chunks[1:], chunks[0]) for chunks in zip(*planes)]


def sub(one, other):
    return [a - b for a, b in zip(one, other)]


def to_modes_xy(u):
    ux = [next_x(a) for a in u]
    s, d = add(ux, u), sub(ux, u)
    sy, dy = next_y(s), next_y(d)
    return add(sy, s), sub(sy, s), add(dy, d), sub(dy, d)


def from_modes_xy(ss, sd, ds, dd):
    s = add(sub(ss, sd), last_y(add(ss, sd)))
    d = add(sub(ds, dd), last_y(add(ds, dd)))
    return add(sub(s, d), [last_x(a) for a in add(s, d)])


def modes_z(low, high):
    modes = []
    for comp in range(3):
        one = {}
        for pq in PLANE:
            if pq != "ss":
                one[pq + "s"] = high[comp][pq] + low[comp][pq]
            one[pq + "d"] = high[comp][pq] - low[comp][pq]
        modes.append(one)
    return modes


NORMAL = ((0, "dss"), (1, "sds"), (2, "ssd"))
BENDS = (((1, "dds"), (2, "dsd")), ((0, "dds"), (2, "sdd")), ((0, "dsd"), (1, "sdd")))
SHEARS = (((0, "sds"), (1, "dss")), ((0, "ssd"), (2, "dss")), ((1, "ssd"), (2, "sds")))
STIFF = (SHEAR / 16, SHEAR / 48, (LAME + 4 * SHEAR) / 144, SHEAR / 8)
TWIST = ((0, "sdd"), (1, "dsd"), (2, "dds"))


def mode_forces(modes, e1, e2, e3, e4):
    m = lambda key: modes[key[0]][key[1]]
    out = [{}, {}, {}]

    def put(key, value):
        out[key[0]][key[1]] = value

    trace = (LAME / (2 * SHEAR)) * (m(NORMAL[0]) + m(NORMAL[1]) + m(NORMAL[2]))
    for key in NORMAL:
        put(key, e4 * (trace + m(key)))
    for a, b in BENDS:
        t = (LAME / (3 * SHEAR)) * (m(a) + m(b))
        put(a, e1 * (t + m(a)))
        put(b, e1 * (t + m(b)))
    for a, b in SHEARS:
        f = e1 * (m(a) + m(b))
        put(a, f)
        put(b, f)
    t = m(TWIST[0]) + m(TWIST[1]) + m(TWIST[2])
    for key in TWIST:
        put(key, e2 * (t + m(key)))
    for comp in range(3):
        put((comp, "ddd"), e3 * modes[comp]["ddd"])
    return out


def mode_energy(modes):
    m = lambda key: modes[key[0]][key[1]]
    sq = lambda v: v * v
    n = [m(key) for key in NORMAL]
    total = (3 * LAME / SHEAR) * sq(n[0] + n[1] + n[2]) + 6.0 * (sq(n[0]) + sq(n[1]) + sq(n[2]))
    shear = None
    for a, b in SHEARS:
        t = sq(m(a) + m(b))
        shear = t if shear is None else shear + t
    total = total + 3.0 * shear
    sums, own = None, None
    for a, b in BENDS:
        t = sq(m(a) + m(b))
        o = sq(m(a)) + sq(m(b))
        sums = t if sums is None else sums + t
        own = o if own is None else own + o
    total = total + (LAME / SHEAR) * sums + 3.0 * own
    a, b, c = (m(key) for key in TWIST)
    total = total + (sq(a + b) + sq(a + c) + sq(b + c))
    bulk = sq(modes[0]["ddd"]) + sq(modes[1]["ddd"]) + sq(modes[2]["ddd"])
    return total + ((LAME + 4 * SHEAR) / (3 * SHEAR)) * bulk


def filter_planes(plane):
    x = [last_x(a) + next_x(a) for a in plane]
    cross = add(x, add(last_y(plane), next_y(plane)))
    diagonal = add(last_y(x), next_y(x))
    near = [1.5 * a + 0.5 * c + EDGE * d for a, c, d in zip(plane, cross, diagonal)]
    return near, [0.5 * a + EDGE * c for a, c in zip(plane, cross)]


def filter_layers(layers):
    pairs = [filter_planes(plane) for plane in layers]
    return [
        add(pairs[at][0], add(pairs[at - 1][1], pairs[at + 1][1])) for at in range(1, len(layers) - 1)
    ]


def partner(index, step):
    return index ^ step


def smooth_kernel(hops, count_gz, *refs):
    blocks = 1 + 3 * hops
    weights_ref = refs[0]
    pack_refs = refs[1 : 1 + blocks]
    disp_hbm, own_ref = refs[1 + blocks : 3 + blocks]
    slot_refs = refs[3 + blocks : -11]
    stiff_ref, inv_ref, res_ref, step_ref, sol_ref, mode_ref, node_ref = refs[-11:-4]
    disp_ref, weight_ref, energy_ref, disp_sem = refs[-4:]

    cases, _, layers, rows, columns = disp_ref.shape
    nodes = layers + 2 * SWEEPS + 1
    chunks = chunks_of(rows)
    gz = lax.axis_index("gz")
    load = lax.axis_index("load")
    even = gz % 2 == 0

    def packed(layer, group, kind):
        hop = layer // layers
        plane = pack_plane(cases, layers, cases if group is None else group, kind, layer - hop * layers)
        if hop == 0:
            return [pack_refs[0][plane, chunk] for chunk in chunks]
        beside_ref, design_ref, force_ref = pack_refs[3 * abs(hop) - 2 : 3 * abs(hop) + 1]
        if group is not None:
            across = [force_ref[group, kind, layer - hop * layers, chunk] for chunk in chunks]
        else:
            across = [design_ref[kind * layers + layer - hop * layers, chunk] for chunk in chunks]
        by_sibling = even == (hop > 0)
        return [
            jnp.where(by_sibling, beside_ref[plane, chunk], a) for chunk, a in zip(chunks, across)
        ]

    def inside(layer):
        owner = gz + layer // layers
        return jnp.logical_and(owner >= 0, owner < count_gz)

    below = None
    for at in range(nodes + 1):
        layer = at - SWEEPS - 1
        live = jnp.where(inside(layer), 1.0, 0.0)
        marks = packed(layer, None, 1)
        moduli = []
        for chunk_at, (dense, mark) in enumerate(zip(packed(layer, None, 0), marks)):
            solid = jnp.where(mark == 2.0, 1.0, dense)
            modulus = (EMIN + (1.0 - EMIN) * solid * solid * solid) * live
            moduli.append(modulus)
            if 0 <= layer < layers:
                weight = (3.0 * (1.0 - EMIN)) * solid * solid * dense
                weight_ref[layer, pl.ds(8 + 8 * chunk_at, 8)] = weight
            if 1 <= at < nodes:
                for kind, factor in enumerate(STIFF):
                    stiff_ref[kind, at - 1, chunks[chunk_at]] = modulus * factor
        spread = add(moduli, [last_x(a) for a in moduli])
        spread = add(spread, last_y(spread))
        if at > 0:
            for chunk, mark, low, high in zip(chunks, marks, below, spread):
                free = jnp.logical_and(mark != 1.0, inside(layer))
                diag = jnp.where(free, KE_DIAG * (low + high), 1.0)
                inv_ref[at - 1, chunk] = jnp.where(free, 1.0 / diag, 0.0)
        below = spread

    theta = 0.5 * (UPPER_EIG + LOWER_EIG)
    delta = 0.5 * (UPPER_EIG - LOWER_EIG)
    sigma = theta / delta

    def load_modes(node, chunk):
        return [
            {pq: mode_ref[node, comp * 4 + i, chunk] for i, pq in enumerate(PLANE)}
            for comp in range(3)
        ]

    def store_modes(node, comp, field):
        for i, plane in enumerate(to_modes_xy(field)):
            for chunk, a in zip(chunks, plane):
                mode_ref[node, comp * 4 + i, chunk] = a

    def one_case(case, carry):
        for at in range(nodes):
            for comp in range(3):
                field = []
                for chunk, force in zip(chunks, packed(at - SWEEPS, case, comp)):
                    step = inv_ref[at, chunk] * force * (1.0 / theta)
                    field.append(step)
                    if 1 <= at < nodes - 1:
                        step_ref[comp, at, chunk] = step
                    if SWEEPS <= at <= SWEEPS + layers:
                        sol_ref[comp, at - SWEEPS, chunk] = step
                store_modes(at, comp, field)

        factor = 1.0 / sigma
        for sweep in range(1, SWEEPS + 1):
            factor_next = 1.0 / (2.0 * sigma - factor)
            keep, take = factor_next * factor, 2.0 * factor_next / delta
            first, end = sweep - 1, nodes - sweep
            if sweep > 1:
                for node in range(first, end + 1):
                    for comp in range(3):
                        store_modes(node, comp, [step_ref[comp, node, chunk] for chunk in chunks])
            for chunk in chunks:
                low = load_modes(first, chunk)
                up = None
                for element in range(first, end):
                    high = load_modes(element + 1, chunk)
                    stiff = [stiff_ref[kind, element, chunk] for kind in range(4)]
                    f = mode_forces(modes_z(low, high), *stiff)
                    ups = []
                    for comp in range(3):
                        for i, pq in enumerate(PLANE):
                            diff = f[comp][pq + "d"]
                            at = comp * 4 + i
                            if pq == "ss":
                                ups.append(diff)
                                if up:
                                    node_ref[element, at, chunk] = up[at] - diff
                            else:
                                both = f[comp][pq + "s"]
                                ups.append(both + diff)
                                if up:
                                    node_ref[element, at, chunk] = up[at] + (both - diff)
                    low, up = high, ups
            for node in range(first + 1, end):
                for comp in range(3):
                    g = [[node_ref[node, comp * 4 + i, chunk] for chunk in chunks] for i in range(4)]
                    if sweep == 1:
                        before = packed(node - SWEEPS, case, comp)
                    else:
                        before = [res_ref[comp, node, chunk] for chunk in chunks]
                    for chunk, res in zip(chunks, sub(before, from_modes_xy(*g))):
                        step = keep * step_ref[comp, node, chunk] + take * (inv_ref[node, chunk] * res)
                        if sweep < SWEEPS:
                            res_ref[comp, node, chunk] = res
                            step_ref[comp, node, chunk] = step
                        if SWEEPS <= node <= SWEEPS + layers:
                            sol = sol_ref[comp, node - SWEEPS, chunk] + step
                            sol_ref[comp, node - SWEEPS, chunk] = sol
                            if sweep == SWEEPS and node < SWEEPS + layers:
                                disp_ref[case, comp, node - SWEEPS, chunk] = sol
            factor = factor_next
        pltpu.make_async_copy(disp_ref.at[case], disp_hbm.at[case], disp_sem.at[case]).start()

        weight = weights_ref[load * cases + case].astype(jnp.float32)
        for node in range(layers + 1):
            for comp in range(3):
                store_modes(node, comp, [sol_ref[comp, node, chunk] for chunk in chunks])
        for chunk in chunks:
            low = load_modes(0, chunk)
            for layer in range(layers):
                high = load_modes(layer + 1, chunk)
                energy = weight * mode_energy(modes_z(low, high))
                before = jnp.where(case == 0, 0.0, energy_ref[layer, chunk])
                energy_ref[layer, chunk] = before + energy
                low = high
        return carry

    lax.fori_loop(0, cases, one_case, 0)
    weight_sum = weights_ref[0]
    for at in range(1, weights_ref.shape[0]):
        weight_sum = weight_sum + weights_ref[at]
    weight_sum = jnp.full((8, columns), weight_sum.astype(jnp.float32))
    scale = (SHEAR / 48) / weight_sum

    spans = filter_layers(
        [[jnp.where(inside(at), a, 0.0) for a in packed(at, None, 0)] for at in range(-2, layers + 2)]
    )
    recs = [
        [jnp.where(inside(layer), 1.0 / jnp.where(inside(layer), a, 1.0), 0.0) for a in span]
        for layer, span in zip(range(-1, layers + 1), spans)
    ]
    shares = filter_layers(recs)
    total = jnp.zeros((8, columns), jnp.float32)
    own_rows = own_ref.shape[2]
    own = pl.ds(pl.multiple_of(load * own_rows, own_rows), own_rows)
    for layer in range(layers):
        for kind in range(2):
            own_ref[1 + kind, layer] = pack_refs[0][pack_plane(cases, layers, cases, kind, layer), own]
        for at, chunk in enumerate(chunks):
            inner = pl.ds(8 + 8 * at, 8)
            sens = weight_ref[layer, inner] * (energy_ref[layer, chunk] * scale)
            weight_ref[layer, inner] = sens
            total = total + sens * shares[layer][at]
            energy_ref[layer, chunk] = recs[layer + 1][at]
        own_ref[0, layer] = energy_ref[layer, own]
        weight_ref[layer, :8] = jnp.zeros((8, columns), jnp.float32)
        weight_ref[layer, 8 + rows :] = jnp.zeros((8, columns), jnp.float32)
    share = jnp.sum(total, axis=0, keepdims=True)
    wide = own_rows + 2
    for step, slot_ref in enumerate(slot_refs):
        start = pl.multiple_of(partner(load, step) * own_rows, own_rows)
        for layer in range(layers):
            window = weight_ref[layer, pl.ds(start, own_rows + 16)]
            slot_ref[layer * wide : (layer + 1) * wide] = window[7 : 7 + wide]
        slot_ref[layers * wide : layers * wide + 1] = share
    for case in range(cases):
        pltpu.make_async_copy(disp_ref.at[case], disp_hbm.at[case], disp_sem.at[case]).wait()


def pack_plane(cases, layers, group, kind, layer):
    return (group * 3 + kind) * layers + layer


def stage_kernel(labels_ref, forces_ref, pack_ref):
    cases, _, layers, _, _ = forces_ref.shape
    for case in range(cases):
        for comp in range(3):
            for layer in range(layers):
                pack_ref[pack_plane(cases, layers, case, comp, layer)] = forces_ref[case, comp, layer]
    for layer in range(layers):
        marks = labels_ref[layer].astype(jnp.float32)
        pack_ref[pack_plane(cases, layers, cases, 1, layer)] = marks


def design_kernel(cases, count_load, *refs):
    density_refs = refs[1 : 1 + count_load]
    pack_ref, design_ref = refs[-2:]
    layers, own_rows, _ = density_refs[0].shape
    load = lax.axis_index("load")
    for step, density_ref in enumerate(density_refs):
        start = pl.multiple_of(partner(load, step) * own_rows, own_rows)
        for layer in range(layers):
            plane = pack_plane(cases, layers, cases, 0, layer)
            pack_ref[plane, pl.ds(start, own_rows)] = density_ref[layer]
    design_ref[...] = pack_ref[cases * 3 * layers :]


def join_kernel(force_ref, design_ref, *refs):
    pack_ref = refs[-1]
    cases, _, layers, _, _ = force_ref.shape
    for case in range(cases):
        for comp in range(3):
            for layer in range(layers):
                pack_ref[pack_plane(cases, layers, case, comp, layer)] = force_ref[case, comp, layer]
    pack_ref[cases * 3 * layers :] = design_ref[...]


def sum_kernel(*refs):
    total = refs[0][...]
    for ref in refs[1:-1]:
        total = total + ref[...]
    refs[-1][...] = total


def forward_kernel(layers, wide, sum_ref, beside_ref, out_ref):
    even = lax.axis_index("gz") % 2 == 0
    end = layers * wide
    out_ref[:wide] = jnp.where(even, beside_ref[end - wide : end], beside_ref[:wide])
    out_ref[wide : wide + 1] = sum_ref[end : end + 1] + beside_ref[end : end + 1]


def share_kernel(wide, mine_ref, *refs):
    out_ref = refs[-1]
    out_ref[...] = mine_ref[...]
    out_ref[wide : wide + 1] = share_sum(wide, mine_ref, *refs[:-1])


def share_sum(wide, *refs):
    total = refs[0][wide : wide + 1]
    for ref in refs[1:]:
        total = total + ref[wide : wide + 1]
    return total


def chip_rounds(count_gz):
    edges = []
    while 2 ** (len(edges) + 1) < count_gz:
        edges.append(2 ** (len(edges) + 1) - 1)
    pairs = [edges[at : at + 2] for at in range(0, len(edges), 2)]
    return [pair + [pair[0] ^ pair[1]] if len(pair) == 2 else pair for pair in pairs]


def update_kernel(cells, rounds, *refs):
    sum_ref, beside_ref, mine_ref = refs[:3]
    other_refs = refs[3:-2]
    own_ref, new_ref = refs[-2:]
    _, layers, own_rows, columns = own_ref.shape
    wide = own_rows + 2
    gz = lax.axis_index("gz")
    even, chip = gz % 2 == 0, gz // 2
    beside = jnp.where(even, beside_ref[:wide], beside_ref[(layers - 1) * wide : layers * wide])
    across = jnp.zeros((wide, columns), jnp.float32)
    for mask, other_ref in zip(sum(rounds, []), other_refs):
        borders = (chip ^ mask) == jnp.where(even, chip - 1, chip + 1)
        across = jnp.where(borders, other_ref[:wide], across)
    numers = [jnp.where(even, across, beside)]
    numers += [sum_ref[layer * wide : (layer + 1) * wide] for layer in range(layers)]
    numers += [jnp.where(even, beside, across)]
    near, far = [], []
    for numer in numers:
        back, mid, front = (numer[at : at + own_rows] for at in range(3))
        sides = back + front
        cross = sides + (last_x(mid) + next_x(mid))
        near.append(1.5 * mid + 0.5 * cross + EDGE * (last_x(sides) + next_x(sides)))
        far.append(0.5 * mid + EDGE * cross)
    total = share_sum(wide, mine_ref, *other_refs[-len(rounds[-1]) :])
    mean = jnp.sum(total, keepdims=True) * (1.0 / cells)
    mean = jnp.broadcast_to(mean, (own_rows, columns))
    for layer in range(layers):
        numer = near[layer + 1] + (far[layer] + far[layer + 2])
        filtered = numer * own_ref[0, layer]
        density = own_ref[1, layer]
        candidate = density * jnp.sqrt(filtered / mean)
        lower = jnp.maximum(density - MOVE_LIMIT, FLOOR_DENSITY)
        upper = jnp.minimum(density + MOVE_LIMIT, 1.0)
        updated = jnp.minimum(jnp.maximum(candidate, lower), upper)
        new_ref[layer] = jnp.where(own_ref[2, layer] == 2.0, 1.0, updated)


def met(block, axis, step):
    count = lax.axis_size(axis)
    return lax.ppermute(block, axis, [(partner(i, step), i) for i in range(count)])


def across_pairs(far, count):
    up = [(i - far, i) for i in range(0, count, 2) if i - far >= 0]
    down = [(i + far, i) for i in range(1, count, 2) if i + far < count]
    free = [i for i in range(count) if i not in dict(up + down)]
    empty = [i for i in range(count) if i not in dict(up + down).values()]
    return up + down + list(zip(free, empty))


def on_device(density, labels, forces, case_weights):
    count_gz, count_load = lax.axis_size("gz"), lax.axis_size("load")
    cases, _, layers, rows, columns = forces.shape
    own_rows = density.shape[1]
    nodes = layers + 2 * SWEEPS + 1
    hops = -(-(SWEEPS + 1) // layers)
    wide = own_rows + 2
    f32 = jnp.float32
    plane = (rows, columns)
    plane_bytes = rows * columns * 4
    vmem = pl.BlockSpec(memory_space=pltpu.VMEM)
    smem = pl.BlockSpec(memory_space=pltpu.SMEM)

    def shape(*dims):
        return jax.ShapeDtypeStruct(dims, f32)

    def call(kernel, out, args, planes, flops, in_specs=None, scratch=(), **more):
        limit = planes * plane_bytes + (2 << 20)
        return pl.pallas_call(
            kernel,
            out_shape=out,
            in_specs=in_specs or [vmem] * len(args),
            out_specs=more.pop("out_specs", vmem),
            scratch_shapes=scratch,
            compiler_params=pltpu.CompilerParams(vmem_limit_bytes=limit),
            cost_estimate=pl.CostEstimate(flops=flops, bytes_accessed=flops // 10, transcendentals=0),
            **more,
        )(*args)

    planes = (cases * 3 + 2) * layers
    far_forces = [
        lax.ppermute(forces, "gz", across_pairs(far, count_gz)) for far in range(1, hops + 1)
    ]
    pack = call(stage_kernel, shape(planes, rows, columns), (labels, forces), 2 * planes, 1_000_000)
    densities = [density] + [met(density, "load", step) for step in range(1, count_load)]
    pack, design = call(
        functools.partial(design_kernel, cases, count_load),
        (shape(planes, rows, columns), shape(2 * layers, rows, columns)),
        (pack, *densities, *far_forces),
        2 * planes + 6 * layers,
        100_000,
        in_specs=[vmem] * (1 + count_load) + [pl.BlockSpec(memory_space=pl.ANY)] * hops,
        out_specs=(vmem, vmem),
        input_output_aliases={0: 0},
    )
    far_designs = [
        lax.ppermute(design, "gz", across_pairs(far, count_gz)) for far in range(1, hops + 1)
    ]
    beside, packs = pack, [pack]
    for at in range(hops):
        packs += [met(beside, "gz", 1), far_designs[at], far_forces[at]]
        if at < hops - 1:
            later = far_designs[at + 1 :]
            beside = call(
                join_kernel,
                shape(planes, rows, columns),
                (far_forces[at], far_designs[at], *later),
                2 * planes,
                100_000,
                in_specs=[vmem] * 2 + [pl.BlockSpec(memory_space=pl.ANY)] * len(later),
            )

    slot_rows = -(-(layers * wide + 1) // 8) * 8
    scratch = [
        pltpu.VMEM((4, nodes - 1) + plane, f32),
        pltpu.VMEM((nodes,) + plane, f32),
        pltpu.VMEM((3, nodes) + plane, f32),
        pltpu.VMEM((3, nodes) + plane, f32),
        pltpu.VMEM((3, layers + 1) + plane, f32),
        pltpu.VMEM((nodes, 12) + plane, f32),
        pltpu.VMEM((nodes, 12) + plane, f32),
        pltpu.VMEM(forces.shape, f32),
        pltpu.VMEM((layers, rows + 16, columns), f32),
        pltpu.VMEM((layers,) + plane, f32),
        pltpu.SemaphoreType.DMA((cases,)),
    ]
    smooth_planes = nodes * 35 + 3 * (layers + 1) + 4 * layers
    smooth_planes += (1 + 2 * hops) * planes + cases * 3 * layers + 8 * layers
    displacement, own, *slots = call(
        functools.partial(smooth_kernel, hops, count_gz),
        (shape(*forces.shape), shape(3, layers, own_rows, columns))
        + (shape(slot_rows, columns),) * count_load,
        (case_weights, *packs),
        smooth_planes,
        60_000_000,
        in_specs=[smem] + [vmem] * len(packs),
        out_specs=(pl.BlockSpec(memory_space=pltpu.HBM),) + (vmem,) * (1 + count_load),
        scratch=scratch,
    )

    received = [met(slots[step], "load", step) for step in range(1, count_load)]
    whole = call(sum_kernel, shape(slot_rows, columns), (slots[0], *received), 2 * count_load, 100_000)
    beside = met(whole, "gz", 1)
    forward_rows = -(-(wide + 1) // 8) * 8
    mine = call(
        functools.partial(forward_kernel, layers, wide),
        shape(forward_rows, columns),
        (whole, beside),
        4 * layers,
        10_000,
    )
    others = []
    rounds = chip_rounds(count_gz)
    for at, masks in enumerate(rounds):
        if at > 0:
            mine = call(
                functools.partial(share_kernel, wide),
                shape(forward_rows, columns),
                (mine, *others[-len(rounds[at - 1]) :]),
                8,
                10_000,
            )
        others += [met(mine, "gz", 2 * mask) for mask in masks]
    new_density = call(
        functools.partial(update_kernel, float(count_gz * layers * rows * columns), rounds),
        shape(*density.shape),
        (whole, beside, mine, *others, own),
        8 * layers,
        100_000,
    )
    return (new_density, displacement)


def solution(mesh):
    return jax.shard_map(
        on_device,
        mesh=mesh,
        in_specs=(
            P("gz", "load", None),
            P("gz", None, None),
            P("load", None, "gz", None, None),
            P(),
        ),
        out_specs=(P("gz", "load", None), P("load", None, "gz", None, None)),
        check_vma=False,
    )
```

```python
import functools

import jax
import jax.numpy as jnp
from jax import lax
from jax.experimental import pallas as pl
from jax.experimental.pallas import tpu as pltpu
from jax.sharding import PartitionSpec as P

SWEEPS = 3
EMIN = 0.001
LOWER_EIG = 0.1
UPPER_EIG = 2.5
MOVE_LIMIT = 0.2
FLOOR_DENSITY = 0.001
POISSON = 0.3
LAME = POISSON / ((1 + POISSON) * (1 - 2 * POISSON))
SHEAR = 1.0 / (2 * (1 + POISSON))
KE_DIAG = (LAME + 4 * SHEAR) / 9
EDGE = 1.5 - 2.0**0.5
PLANE = ("ss", "sd", "ds", "dd")


def chunks_of(rows):
    return [pl.ds(at, 8) for at in range(0, rows, 8)]


def next_x(a):
    lanes = a.shape[1]
    lane = lax.broadcasted_iota(jnp.int32, a.shape, 1)
    return jnp.where(lane == lanes - 1, 0.0, pltpu.roll(a, lanes - 1, 1))


def last_x(a):
    lane = lax.broadcasted_iota(jnp.int32, a.shape, 1)
    return jnp.where(lane == 0, 0.0, pltpu.roll(a, 1, 1))


def next_y(plane):
    row = lax.broadcasted_iota(jnp.int32, plane[0].shape, 0)
    rolled = [pltpu.roll(a, 7, 0) for a in plane] + [jnp.zeros_like(plane[0])]
    return [jnp.where(row == 7, rolled[at + 1], rolled[at]) for at in range(len(plane))]


def last_y(plane):
    row = lax.broadcasted_iota(jnp.int32, plane[0].shape, 0)
    rolled = [jnp.zeros_like(plane[0])] + [pltpu.roll(a, 1, 0) for a in plane]
    return [jnp.where(row == 0, rolled[at], rolled[at + 1]) for at in range(len(plane))]


def add(*planes):
    return [sum(chunks[1:], chunks[0]) for chunks in zip(*planes)]


def sub(one, other):
    return [a - b for a, b in zip(one, other)]


def to_modes_xy(u):
    ux = [next_x(a) for a in u]
    s, d = add(ux, u), sub(ux, u)
    sy, dy = next_y(s), next_y(d)
    return add(sy, s), sub(sy, s), add(dy, d), sub(dy, d)


def from_modes_xy(ss, sd, ds, dd):
    s = add(sub(ss, sd), last_y(add(ss, sd)))
    d = add(sub(ds, dd), last_y(add(ds, dd)))
    return add(sub(s, d), [last_x(a) for a in add(s, d)])


def modes_z(low, high):
    modes = []
    for comp in range(3):
        one = {}
        for pq in PLANE:
            if pq != "ss":
                one[pq + "s"] = high[comp][pq] + low[comp][pq]
            one[pq + "d"] = high[comp][pq] - low[comp][pq]
        modes.append(one)
    return modes


NORMAL = ((0, "dss"), (1, "sds"), (2, "ssd"))
BENDS = (((1, "dds"), (2, "dsd")), ((0, "dds"), (2, "sdd")), ((0, "dsd"), (1, "sdd")))
SHEARS = (((0, "sds"), (1, "dss")), ((0, "ssd"), (2, "dss")), ((1, "ssd"), (2, "sds")))
STIFF = (SHEAR / 16, SHEAR / 48, (LAME + 4 * SHEAR) / 144, SHEAR / 8)
TWIST = ((0, "sdd"), (1, "dsd"), (2, "dds"))


def mode_forces(modes, e1, e2, e3, e4):
    m = lambda key: modes[key[0]][key[1]]
    out = [{}, {}, {}]

    def put(key, value):
        out[key[0]][key[1]] = value

    trace = (LAME / (2 * SHEAR)) * (m(NORMAL[0]) + m(NORMAL[1]) + m(NORMAL[2]))
    for key in NORMAL:
        put(key, e4 * (trace + m(key)))
    for a, b in BENDS:
        t = (LAME / (3 * SHEAR)) * (m(a) + m(b))
        put(a, e1 * (t + m(a)))
        put(b, e1 * (t + m(b)))
    for a, b in SHEARS:
        f = e1 * (m(a) + m(b))
        put(a, f)
        put(b, f)
    t = m(TWIST[0]) + m(TWIST[1]) + m(TWIST[2])
    for key in TWIST:
        put(key, e2 * (t + m(key)))
    for comp in range(3):
        put((comp, "ddd"), e3 * modes[comp]["ddd"])
    return out


def mode_energy(modes):
    m = lambda key: modes[key[0]][key[1]]
    sq = lambda v: v * v
    n = [m(key) for key in NORMAL]
    total = (3 * LAME / SHEAR) * sq(n[0] + n[1] + n[2]) + 6.0 * (sq(n[0]) + sq(n[1]) + sq(n[2]))
    shear = None
    for a, b in SHEARS:
        t = sq(m(a) + m(b))
        shear = t if shear is None else shear + t
    total = total + 3.0 * shear
    sums, own = None, None
    for a, b in BENDS:
        t = sq(m(a) + m(b))
        o = sq(m(a)) + sq(m(b))
        sums = t if sums is None else sums + t
        own = o if own is None else own + o
    total = total + (LAME / SHEAR) * sums + 3.0 * own
    a, b, c = (m(key) for key in TWIST)
    total = total + (sq(a + b) + sq(a + c) + sq(b + c))
    bulk = sq(modes[0]["ddd"]) + sq(modes[1]["ddd"]) + sq(modes[2]["ddd"])
    return total + ((LAME + 4 * SHEAR) / (3 * SHEAR)) * bulk


def filter_planes(plane):
    x = [last_x(a) + next_x(a) for a in plane]
    cross = add(x, add(last_y(plane), next_y(plane)))
    diagonal = add(last_y(x), next_y(x))
    near = [1.5 * a + 0.5 * c + EDGE * d for a, c, d in zip(plane, cross, diagonal)]
    return near, [0.5 * a + EDGE * c for a, c in zip(plane, cross)]


def filter_layers(layers):
    pairs = [filter_planes(plane) for plane in layers]
    return [
        add(pairs[at][0], add(pairs[at - 1][1], pairs[at + 1][1])) for at in range(1, len(layers) - 1)
    ]


def partner(index, step):
    return index ^ step


def smooth_kernel(hops, count_gz, *refs):
    blocks = 1 + 2 * hops
    weights_ref = refs[0]
    pack_refs = refs[1 : 1 + blocks]
    disp_hbm, own_ref = refs[1 + blocks : 3 + blocks]
    slot_refs = refs[3 + blocks : -11]
    stiff_ref, inv_ref, res_ref, step_ref, sol_ref, mode_ref, node_ref = refs[-11:-4]
    disp_ref, weight_ref, energy_ref, disp_sem = refs[-4:]

    cases, _, layers, rows, columns = disp_ref.shape
    nodes = layers + 2 * SWEEPS + 1
    chunks = chunks_of(rows)
    gz = lax.axis_index("gz")
    load = lax.axis_index("load")
    even = gz % 2 == 0

    def packed(layer, group, kind):
        hop = layer // layers
        plane = pack_plane(cases, layers, group, kind, layer - hop * layers)
        if hop == 0:
            return [pack_refs[0][plane, chunk] for chunk in chunks]
        far = abs(hop)
        beside, across = pack_refs[2 * far - 1], pack_refs[2 * far]
        by_sibling = even == (hop > 0)
        return [jnp.where(by_sibling, beside[plane, chunk], across[plane, chunk]) for chunk in chunks]

    def inside(layer):
        owner = gz + layer // layers
        return jnp.logical_and(owner >= 0, owner < count_gz)

    below = None
    for at in range(nodes + 1):
        layer = at - SWEEPS - 1
        live = jnp.where(inside(layer), 1.0, 0.0)
        marks = packed(layer, cases, 1)
        moduli = []
        for chunk_at, (dense, mark) in enumerate(zip(packed(layer, cases, 0), marks)):
            solid = jnp.where(mark == 2.0, 1.0, dense)
            modulus = (EMIN + (1.0 - EMIN) * solid * solid * solid) * live
            moduli.append(modulus)
            if 0 <= layer < layers:
                weight = (3.0 * (1.0 - EMIN)) * solid * solid * dense
                weight_ref[layer, pl.ds(8 + 8 * chunk_at, 8)] = weight
            if 1 <= at < nodes:
                for kind, factor in enumerate(STIFF):
                    stiff_ref[kind, at - 1, chunks[chunk_at]] = modulus * factor
        spread = add(moduli, [last_x(a) for a in moduli])
        spread = add(spread, last_y(spread))
        if at > 0:
            for chunk, mark, low, high in zip(chunks, marks, below, spread):
                free = jnp.logical_and(mark != 1.0, inside(layer))
                diag = jnp.where(free, KE_DIAG * (low + high), 1.0)
                inv_ref[at - 1, chunk] = jnp.where(free, 1.0 / diag, 0.0)
        below = spread

    theta = 0.5 * (UPPER_EIG + LOWER_EIG)
    delta = 0.5 * (UPPER_EIG - LOWER_EIG)
    sigma = theta / delta

    def load_modes(node, chunk):
        return [
            {pq: mode_ref[node, comp * 4 + i, chunk] for i, pq in enumerate(PLANE)}
            for comp in range(3)
        ]

    def store_modes(node, comp, field):
        for i, plane in enumerate(to_modes_xy(field)):
            for chunk, a in zip(chunks, plane):
                mode_ref[node, comp * 4 + i, chunk] = a

    def one_case(case, carry):
        for at in range(nodes):
            for comp in range(3):
                field = []
                for chunk, force in zip(chunks, packed(at - SWEEPS, case, comp)):
                    step = inv_ref[at, chunk] * force * (1.0 / theta)
                    field.append(step)
                    if 1 <= at < nodes - 1:
                        step_ref[comp, at, chunk] = step
                    if SWEEPS <= at <= SWEEPS + layers:
                        sol_ref[comp, at - SWEEPS, chunk] = step
                store_modes(at, comp, field)

        factor = 1.0 / sigma
        for sweep in range(1, SWEEPS + 1):
            factor_next = 1.0 / (2.0 * sigma - factor)
            keep, take = factor_next * factor, 2.0 * factor_next / delta
            first, end = sweep - 1, nodes - sweep
            for chunk in chunks:
                low = load_modes(first, chunk)
                up = None
                for element in range(first, end):
                    high = load_modes(element + 1, chunk)
                    stiff = [stiff_ref[kind, element, chunk] for kind in range(4)]
                    f = mode_forces(modes_z(low, high), *stiff)
                    ups = []
                    for comp in range(3):
                        for i, pq in enumerate(PLANE):
                            diff = f[comp][pq + "d"]
                            at = comp * 4 + i
                            if pq == "ss":
                                ups.append(diff)
                                if up:
                                    node_ref[element, at, chunk] = up[at] - diff
                            else:
                                both = f[comp][pq + "s"]
                                ups.append(both + diff)
                                if up:
                                    node_ref[element, at, chunk] = up[at] + (both - diff)
                    low, up = high, ups
            for node in range(first + 1, end):
                for comp in range(3):
                    g = [[node_ref[node, comp * 4 + i, chunk] for chunk in chunks] for i in range(4)]
                    if sweep == 1:
                        before = packed(node - SWEEPS, case, comp)
                    else:
                        before = [res_ref[comp, node, chunk] for chunk in chunks]
                    steps, sols = [], []
                    for chunk, res in zip(chunks, sub(before, from_modes_xy(*g))):
                        step = keep * step_ref[comp, node, chunk] + take * (inv_ref[node, chunk] * res)
                        steps.append(step)
                        if sweep < SWEEPS:
                            res_ref[comp, node, chunk] = res
                            step_ref[comp, node, chunk] = step
                        if SWEEPS <= node <= SWEEPS + layers:
                            sol = sol_ref[comp, node - SWEEPS, chunk] + step
                            sols.append(sol)
                            if sweep < SWEEPS:
                                sol_ref[comp, node - SWEEPS, chunk] = sol
                            elif node < SWEEPS + layers:
                                disp_ref[case, comp, node - SWEEPS, chunk] = sol
                    store_modes(node, comp, steps if sweep < SWEEPS else sols)
            factor = factor_next
        pltpu.make_async_copy(disp_ref.at[case], disp_hbm.at[case], disp_sem.at[case]).start()

        weight = weights_ref[load * cases + case].astype(jnp.float32)
        for chunk in chunks:
            low = load_modes(SWEEPS, chunk)
            for layer in range(layers):
                high = load_modes(SWEEPS + layer + 1, chunk)
                energy = weight * mode_energy(modes_z(low, high))
                before = jnp.where(case == 0, 0.0, energy_ref[layer, chunk])
                energy_ref[layer, chunk] = before + energy
                low = high
        return carry

    lax.fori_loop(0, cases, one_case, 0)
    weight_sum = weights_ref[0]
    for at in range(1, weights_ref.shape[0]):
        weight_sum = weight_sum + weights_ref[at]
    weight_sum = jnp.full((8, columns), weight_sum.astype(jnp.float32))
    scale = (SHEAR / 48) / weight_sum

    spans = filter_layers(
        [[jnp.where(inside(at), a, 0.0) for a in packed(at, cases, 0)] for at in range(-2, layers + 2)]
    )
    recs = [
        [jnp.where(inside(layer), 1.0 / jnp.where(inside(layer), a, 1.0), 0.0) for a in span]
        for layer, span in zip(range(-1, layers + 1), spans)
    ]
    shares = filter_layers(recs)
    total = jnp.zeros((8, columns), jnp.float32)
    own_rows = own_ref.shape[2]
    own = pl.ds(pl.multiple_of(load * own_rows, own_rows), own_rows)
    for layer in range(layers):
        for kind in range(2):
            own_ref[1 + kind, layer] = pack_refs[0][pack_plane(cases, layers, cases, kind, layer), own]
        for at, chunk in enumerate(chunks):
            inner = pl.ds(8 + 8 * at, 8)
            sens = weight_ref[layer, inner] * (energy_ref[layer, chunk] * scale)
            weight_ref[layer, inner] = sens
            total = total + sens * shares[layer][at]
            energy_ref[layer, chunk] = recs[layer + 1][at]
        own_ref[0, layer] = energy_ref[layer, own]
        weight_ref[layer, :8] = jnp.zeros((8, columns), jnp.float32)
        weight_ref[layer, 8 + rows :] = jnp.zeros((8, columns), jnp.float32)
    share = jnp.sum(total, axis=0, keepdims=True)
    wide = own_rows + 2
    for step, slot_ref in enumerate(slot_refs):
        start = pl.multiple_of(partner(load, step) * own_rows, own_rows)
        for layer in range(layers):
            window = weight_ref[layer, pl.ds(start, own_rows + 16)]
            slot_ref[layer * wide : (layer + 1) * wide] = window[7 : 7 + wide]
        slot_ref[layers * wide : layers * wide + 1] = share
    for case in range(cases):
        pltpu.make_async_copy(disp_ref.at[case], disp_hbm.at[case], disp_sem.at[case]).wait()


def pack_plane(cases, layers, group, kind, layer):
    return (group * 3 + kind) * layers + layer


def stage_kernel(labels_ref, forces_ref, pack_ref):
    cases, _, layers, _, _ = forces_ref.shape
    for case in range(cases):
        for comp in range(3):
            for layer in range(layers):
                pack_ref[pack_plane(cases, layers, case, comp, layer)] = forces_ref[case, comp, layer]
    for layer in range(layers):
        marks = labels_ref[layer].astype(jnp.float32)
        pack_ref[pack_plane(cases, layers, cases, 1, layer)] = marks


def design_kernel(cases, steps, *refs):
    density_refs, pack_ref = refs[1:-1], refs[-1]
    layers, own_rows, _ = density_refs[0].shape
    load = lax.axis_index("load")
    for step, density_ref in zip(steps, density_refs):
        start = pl.multiple_of(partner(load, step) * own_rows, own_rows)
        for layer in range(layers):
            plane = pack_plane(cases, layers, cases, 0, layer)
            pack_ref[plane, pl.ds(start, own_rows)] = density_ref[layer]


def sum_kernel(*refs):
    total = refs[0][...]
    for ref in refs[1:-1]:
        total = total + ref[...]
    refs[-1][...] = total


def forward_kernel(layers, wide, sum_ref, beside_ref, out_ref):
    even = lax.axis_index("gz") % 2 == 0
    end = layers * wide
    out_ref[:wide] = jnp.where(even, beside_ref[end - wide : end], beside_ref[:wide])
    out_ref[wide : wide + 1] = sum_ref[end : end + 1] + beside_ref[end : end + 1]


def share_kernel(wide, mine_ref, *refs):
    out_ref = refs[-1]
    out_ref[...] = mine_ref[...]
    out_ref[wide : wide + 1] = share_sum(wide, mine_ref, *refs[:-1])


def share_sum(wide, *refs):
    total = refs[0][wide : wide + 1]
    for ref in refs[1:]:
        total = total + ref[wide : wide + 1]
    return total


def chip_rounds(count_gz):
    edges = []
    while 2 ** (len(edges) + 1) < count_gz:
        edges.append(2 ** (len(edges) + 1) - 1)
    pairs = [edges[at : at + 2] for at in range(0, len(edges), 2)]
    return [[pair[0], pair[0] ^ pair[1], pair[1]] if len(pair) == 2 else pair for pair in pairs]


def update_kernel(cells, rounds, *refs):
    sum_ref, beside_ref, mine_ref = refs[:3]
    other_refs = refs[3:-2]
    own_ref, new_ref = refs[-2:]
    _, layers, own_rows, columns = own_ref.shape
    wide = own_rows + 2
    gz = lax.axis_index("gz")
    even, chip = gz % 2 == 0, gz // 2
    beside = jnp.where(even, beside_ref[:wide], beside_ref[(layers - 1) * wide : layers * wide])
    across = jnp.zeros((wide, columns), jnp.float32)
    for mask, other_ref in zip(sum(rounds, []), other_refs):
        borders = (chip ^ mask) == jnp.where(even, chip - 1, chip + 1)
        across = jnp.where(borders, other_ref[:wide], across)
    numers = [jnp.where(even, across, beside)]
    numers += [sum_ref[layer * wide : (layer + 1) * wide] for layer in range(layers)]
    numers += [jnp.where(even, beside, across)]
    near, far = [], []
    for numer in numers:
        back, mid, front = (numer[at : at + own_rows] for at in range(3))
        sides = back + front
        cross = sides + (last_x(mid) + next_x(mid))
        near.append(1.5 * mid + 0.5 * cross + EDGE * (last_x(sides) + next_x(sides)))
        far.append(0.5 * mid + EDGE * cross)
    total = share_sum(wide, mine_ref, *other_refs[-len(rounds[-1]) :])
    mean = jnp.sum(total, keepdims=True) * (1.0 / cells)
    mean = jnp.broadcast_to(mean, (own_rows, columns))
    for layer in range(layers):
        numer = near[layer + 1] + (far[layer] + far[layer + 2])
        filtered = numer * own_ref[0, layer]
        density = own_ref[1, layer]
        candidate = density * jnp.sqrt(filtered / mean)
        lower = jnp.maximum(density - MOVE_LIMIT, FLOOR_DENSITY)
        upper = jnp.minimum(density + MOVE_LIMIT, 1.0)
        updated = jnp.minimum(jnp.maximum(candidate, lower), upper)
        new_ref[layer] = jnp.where(own_ref[2, layer] == 2.0, 1.0, updated)


def met(block, axis, step):
    count = lax.axis_size(axis)
    return lax.ppermute(block, axis, [(partner(i, step), i) for i in range(count)])


def from_neighbours(pack, hops, count):
    low = range(1, count - 1, 2)
    pairs = [(i, i + 1) for i in low] + [(i + 1, i) for i in low] + [(0, 0), (count - 1, count - 1)]
    beside, across = met(pack, "gz", 1), lax.ppermute(pack, "gz", pairs)
    blocks = [beside, across]
    for far in range(2, hops + 1):
        beside = met(across, "gz", 1)
        up = [(i - far, i) for i in range(0, count, 2) if i - far >= 0]
        down = [(i + far, i) for i in range(1, count, 2) if i + far < count]
        free = [i for i in range(count) if i not in dict(up + down)]
        empty = [i for i in range(count) if i not in dict(up + down).values()]
        across = lax.ppermute(pack, "gz", up + down + list(zip(free, empty)))
        blocks += [beside, across]
    return blocks


def on_device(density, labels, forces, case_weights):
    count_gz, count_load = lax.axis_size("gz"), lax.axis_size("load")
    cases, _, layers, rows, columns = forces.shape
    own_rows = density.shape[1]
    nodes = layers + 2 * SWEEPS + 1
    hops = -(-(SWEEPS + 1) // layers)
    wide = own_rows + 2
    f32 = jnp.float32
    plane = (rows, columns)
    plane_bytes = rows * columns * 4
    vmem = pl.BlockSpec(memory_space=pltpu.VMEM)
    smem = pl.BlockSpec(memory_space=pltpu.SMEM)

    def shape(*dims):
        return jax.ShapeDtypeStruct(dims, f32)

    def call(kernel, out, args, planes, flops, in_specs=None, scratch=(), **more):
        limit = planes * plane_bytes + (2 << 20)
        return pl.pallas_call(
            kernel,
            out_shape=out,
            in_specs=in_specs or [vmem] * len(args),
            out_specs=more.pop("out_specs", vmem),
            scratch_shapes=scratch,
            compiler_params=pltpu.CompilerParams(vmem_limit_bytes=limit),
            cost_estimate=pl.CostEstimate(flops=flops, bytes_accessed=flops // 10, transcendentals=0),
            **more,
        )(*args)

    planes = (cases * 3 + 2) * layers
    pack = call(stage_kernel, shape(planes, rows, columns), (labels, forces), 2 * planes, 1_000_000)
    steps = [0] + list(range(2, count_load)) + [1]
    densities = [density] + [met(density, "load", step) for step in steps[1:]]
    pack = call(
        functools.partial(design_kernel, cases, steps),
        shape(planes, rows, columns),
        (pack, *densities),
        2 * planes + 2 * layers,
        100_000,
        input_output_aliases={0: 0},
    )
    packs = [pack] + from_neighbours(pack, hops, count_gz)

    slot_rows = -(-(layers * wide + 1) // 8) * 8
    scratch = [
        pltpu.VMEM((4, nodes - 1) + plane, f32),
        pltpu.VMEM((nodes,) + plane, f32),
        pltpu.VMEM((3, nodes) + plane, f32),
        pltpu.VMEM((3, nodes) + plane, f32),
        pltpu.VMEM((3, layers + 1) + plane, f32),
        pltpu.VMEM((nodes, 12) + plane, f32),
        pltpu.VMEM((nodes, 12) + plane, f32),
        pltpu.VMEM(forces.shape, f32),
        pltpu.VMEM((layers, rows + 16, columns), f32),
        pltpu.VMEM((layers,) + plane, f32),
        pltpu.SemaphoreType.DMA((cases,)),
    ]
    smooth_planes = nodes * 35 + 3 * (layers + 1) + 4 * layers
    smooth_planes += len(packs) * planes + cases * 3 * layers + 8 * layers
    displacement, own, *slots = call(
        functools.partial(smooth_kernel, hops, count_gz),
        (shape(*forces.shape), shape(3, layers, own_rows, columns))
        + (shape(slot_rows, columns),) * count_load,
        (case_weights, *packs),
        smooth_planes,
        60_000_000,
        in_specs=[smem] + [vmem] * len(packs),
        out_specs=(pl.BlockSpec(memory_space=pltpu.HBM),) + (vmem,) * (1 + count_load),
        scratch=scratch,
    )

    received = [met(slots[step], "load", step) for step in range(count_load - 1, 0, -1)]
    whole = call(sum_kernel, shape(slot_rows, columns), (slots[0], *received), 2 * count_load, 100_000)
    beside = met(whole, "gz", 1)
    forward_rows = -(-(wide + 1) // 8) * 8
    mine = call(
        functools.partial(forward_kernel, layers, wide),
        shape(forward_rows, columns),
        (whole, beside),
        4 * layers,
        10_000,
    )
    others = []
    rounds = chip_rounds(count_gz)
    for at, masks in enumerate(rounds):
        if at > 0:
            mine = call(
                functools.partial(share_kernel, wide),
                shape(forward_rows, columns),
                (mine, *others[-len(rounds[at - 1]) :]),
                8,
                10_000,
            )
        others += [met(mine, "gz", 2 * mask) for mask in masks]
    new_density = call(
        functools.partial(update_kernel, float(count_gz * layers * rows * columns), rounds),
        shape(*density.shape),
        (whole, beside, mine, *others, own),
        8 * layers,
        100_000,
    )
    return (new_density, displacement)


def solution(mesh):
    return jax.shard_map(
        on_device,
        mesh=mesh,
        in_specs=(
            P("gz", "load", None),
            P("gz", None, None),
            P("load", None, "gz", None, None),
            P(),
        ),
        out_specs=(P("gz", "load", None), P("load", None, "gz", None, None)),
        check_vma=False,
    )
```

```python
import functools

import jax
import jax.numpy as jnp
from jax import lax
from jax.experimental import pallas as pl
from jax.experimental.pallas import tpu as pltpu
from jax.sharding import PartitionSpec as P

SWEEPS = 3
EMIN = 0.001
LOWER_EIG = 0.1
UPPER_EIG = 2.5
MOVE_LIMIT = 0.2
FLOOR_DENSITY = 0.001
POISSON = 0.3
LAME = POISSON / ((1 + POISSON) * (1 - 2 * POISSON))
SHEAR = 1.0 / (2 * (1 + POISSON))
KE_DIAG = (LAME + 4 * SHEAR) / 9
EDGE = 1.5 - 2.0**0.5
PLANE = ("ss", "sd", "ds", "dd")


def chunks_of(rows):
    return [pl.ds(at, 8) for at in range(0, rows, 8)]


def next_x(a):
    lanes = a.shape[1]
    lane = lax.broadcasted_iota(jnp.int32, a.shape, 1)
    return jnp.where(lane == lanes - 1, 0.0, pltpu.roll(a, lanes - 1, 1))


def last_x(a):
    lane = lax.broadcasted_iota(jnp.int32, a.shape, 1)
    return jnp.where(lane == 0, 0.0, pltpu.roll(a, 1, 1))


def next_y(plane):
    row = lax.broadcasted_iota(jnp.int32, plane[0].shape, 0)
    rolled = [pltpu.roll(a, 7, 0) for a in plane] + [jnp.zeros_like(plane[0])]
    return [jnp.where(row == 7, rolled[at + 1], rolled[at]) for at in range(len(plane))]


def last_y(plane):
    row = lax.broadcasted_iota(jnp.int32, plane[0].shape, 0)
    rolled = [jnp.zeros_like(plane[0])] + [pltpu.roll(a, 1, 0) for a in plane]
    return [jnp.where(row == 0, rolled[at], rolled[at + 1]) for at in range(len(plane))]


def add(*planes):
    return [sum(chunks[1:], chunks[0]) for chunks in zip(*planes)]


def sub(one, other):
    return [a - b for a, b in zip(one, other)]


def to_modes_xy(u):
    ux = [next_x(a) for a in u]
    s, d = add(ux, u), sub(ux, u)
    sy, dy = next_y(s), next_y(d)
    return add(sy, s), sub(sy, s), add(dy, d), sub(dy, d)


def from_modes_xy(ss, sd, ds, dd):
    s = add(sub(ss, sd), last_y(add(ss, sd)))
    d = add(sub(ds, dd), last_y(add(ds, dd)))
    return add(sub(s, d), [last_x(a) for a in add(s, d)])


def modes_z(low, high):
    modes = []
    for comp in range(3):
        one = {}
        for pq in PLANE:
            if pq != "ss":
                one[pq + "s"] = high[comp][pq] + low[comp][pq]
            one[pq + "d"] = high[comp][pq] - low[comp][pq]
        modes.append(one)
    return modes


NORMAL = ((0, "dss"), (1, "sds"), (2, "ssd"))
BENDS = (((1, "dds"), (2, "dsd")), ((0, "dds"), (2, "sdd")), ((0, "dsd"), (1, "sdd")))
SHEARS = (((0, "sds"), (1, "dss")), ((0, "ssd"), (2, "dss")), ((1, "ssd"), (2, "sds")))
STIFF = (SHEAR / 16, SHEAR / 48, (LAME + 4 * SHEAR) / 144, SHEAR / 8)
TWIST = ((0, "sdd"), (1, "dsd"), (2, "dds"))


def mode_forces(modes, e1, e2, e3, e4):
    m = lambda key: modes[key[0]][key[1]]
    out = [{}, {}, {}]

    def put(key, value):
        out[key[0]][key[1]] = value

    trace = (LAME / (2 * SHEAR)) * (m(NORMAL[0]) + m(NORMAL[1]) + m(NORMAL[2]))
    for key in NORMAL:
        put(key, e4 * (trace + m(key)))
    for a, b in BENDS:
        t = (LAME / (3 * SHEAR)) * (m(a) + m(b))
        put(a, e1 * (t + m(a)))
        put(b, e1 * (t + m(b)))
    for a, b in SHEARS:
        f = e1 * (m(a) + m(b))
        put(a, f)
        put(b, f)
    t = m(TWIST[0]) + m(TWIST[1]) + m(TWIST[2])
    for key in TWIST:
        put(key, e2 * (t + m(key)))
    for comp in range(3):
        put((comp, "ddd"), e3 * modes[comp]["ddd"])
    return out


def mode_energy(modes):
    m = lambda key: modes[key[0]][key[1]]
    sq = lambda v: v * v
    n = [m(key) for key in NORMAL]
    total = (3 * LAME / SHEAR) * sq(n[0] + n[1] + n[2]) + 6.0 * (sq(n[0]) + sq(n[1]) + sq(n[2]))
    shear = None
    for a, b in SHEARS:
        t = sq(m(a) + m(b))
        shear = t if shear is None else shear + t
    total = total + 3.0 * shear
    sums, own = None, None
    for a, b in BENDS:
        t = sq(m(a) + m(b))
        o = sq(m(a)) + sq(m(b))
        sums = t if sums is None else sums + t
        own = o if own is None else own + o
    total = total + (LAME / SHEAR) * sums + 3.0 * own
    a, b, c = (m(key) for key in TWIST)
    total = total + (sq(a + b) + sq(a + c) + sq(b + c))
    bulk = sq(modes[0]["ddd"]) + sq(modes[1]["ddd"]) + sq(modes[2]["ddd"])
    return total + ((LAME + 4 * SHEAR) / (3 * SHEAR)) * bulk


def filter_planes(plane):
    x = [last_x(a) + next_x(a) for a in plane]
    cross = add(x, add(last_y(plane), next_y(plane)))
    diagonal = add(last_y(x), next_y(x))
    near = [1.5 * a + 0.5 * c + EDGE * d for a, c, d in zip(plane, cross, diagonal)]
    return near, [0.5 * a + EDGE * c for a, c in zip(plane, cross)]


def filter_layers(layers):
    pairs = [filter_planes(plane) for plane in layers]
    return [
        add(pairs[at][0], add(pairs[at - 1][1], pairs[at + 1][1])) for at in range(1, len(layers) - 1)
    ]


def partner(index, step):
    return index ^ step


def smooth_kernel(hops, count_gz, *refs):
    blocks = 1 + 3 * hops
    weights_ref = refs[0]
    pack_refs = refs[1 : 1 + blocks]
    disp_hbm, own_ref = refs[1 + blocks : 3 + blocks]
    slot_refs = refs[3 + blocks : -11]
    stiff_ref, inv_ref, res_ref, step_ref, sol_ref, mode_ref, node_ref = refs[-11:-4]
    disp_ref, weight_ref, energy_ref, disp_sem = refs[-4:]

    cases, _, layers, rows, columns = disp_ref.shape
    nodes = layers + 2 * SWEEPS + 1
    chunks = chunks_of(rows)
    gz = lax.axis_index("gz")
    load = lax.axis_index("load")
    even = gz % 2 == 0

    def packed(layer, group, kind):
        hop = layer // layers
        plane = pack_plane(cases, layers, cases if group is None else group, kind, layer - hop * layers)
        if hop == 0:
            return [pack_refs[0][plane, chunk] for chunk in chunks]
        beside_ref, design_ref, force_ref = pack_refs[3 * abs(hop) - 2 : 3 * abs(hop) + 1]
        if group is not None:
            across = [force_ref[group, kind, layer - hop * layers, chunk] for chunk in chunks]
        else:
            across = [design_ref[kind * layers + layer - hop * layers, chunk] for chunk in chunks]
        by_sibling = even == (hop > 0)
        return [
            jnp.where(by_sibling, beside_ref[plane, chunk], a) for chunk, a in zip(chunks, across)
        ]

    def inside(layer):
        owner = gz + layer // layers
        return jnp.logical_and(owner >= 0, owner < count_gz)

    below = None
    for at in range(nodes + 1):
        layer = at - SWEEPS - 1
        live = jnp.where(inside(layer), 1.0, 0.0)
        marks = packed(layer, None, 1)
        moduli = []
        for chunk_at, (dense, mark) in enumerate(zip(packed(layer, None, 0), marks)):
            solid = jnp.where(mark == 2.0, 1.0, dense)
            modulus = (EMIN + (1.0 - EMIN) * solid * solid * solid) * live
            moduli.append(modulus)
            if 0 <= layer < layers:
                weight = (3.0 * (1.0 - EMIN)) * solid * solid * dense
                weight_ref[layer, pl.ds(8 + 8 * chunk_at, 8)] = weight
            if 1 <= at < nodes:
                for kind, factor in enumerate(STIFF):
                    stiff_ref[kind, at - 1, chunks[chunk_at]] = modulus * factor
        spread = add(moduli, [last_x(a) for a in moduli])
        spread = add(spread, last_y(spread))
        if at > 0:
            for chunk, mark, low, high in zip(chunks, marks, below, spread):
                free = jnp.logical_and(mark != 1.0, inside(layer))
                diag = jnp.where(free, KE_DIAG * (low + high), 1.0)
                inv_ref[at - 1, chunk] = jnp.where(free, 1.0 / diag, 0.0)
        below = spread

    theta = 0.5 * (UPPER_EIG + LOWER_EIG)
    delta = 0.5 * (UPPER_EIG - LOWER_EIG)
    sigma = theta / delta

    def load_modes(node, chunk):
        return [
            {pq: mode_ref[node, comp * 4 + i, chunk] for i, pq in enumerate(PLANE)}
            for comp in range(3)
        ]

    def store_modes(node, comp, field):
        for i, plane in enumerate(to_modes_xy(field)):
            for chunk, a in zip(chunks, plane):
                mode_ref[node, comp * 4 + i, chunk] = a

    def one_case(case, carry):
        for at in range(nodes):
            for comp in range(3):
                field = []
                for chunk, force in zip(chunks, packed(at - SWEEPS, case, comp)):
                    step = inv_ref[at, chunk] * force * (1.0 / theta)
                    field.append(step)
                    if 1 <= at < nodes - 1:
                        step_ref[comp, at, chunk] = step
                    if SWEEPS <= at <= SWEEPS + layers:
                        sol_ref[comp, at - SWEEPS, chunk] = step
                store_modes(at, comp, field)

        factor = 1.0 / sigma
        for sweep in range(1, SWEEPS + 1):
            factor_next = 1.0 / (2.0 * sigma - factor)
            keep, take = factor_next * factor, 2.0 * factor_next / delta
            first, end = sweep - 1, nodes - sweep
            if sweep > 1:
                for node in range(first, end + 1):
                    for comp in range(3):
                        store_modes(node, comp, [step_ref[comp, node, chunk] for chunk in chunks])
            for chunk in chunks:
                low = load_modes(first, chunk)
                up = None
                for element in range(first, end):
                    high = load_modes(element + 1, chunk)
                    stiff = [stiff_ref[kind, element, chunk] for kind in range(4)]
                    f = mode_forces(modes_z(low, high), *stiff)
                    ups = []
                    for comp in range(3):
                        for i, pq in enumerate(PLANE):
                            diff = f[comp][pq + "d"]
                            at = comp * 4 + i
                            if pq == "ss":
                                ups.append(diff)
                                if up:
                                    node_ref[element, at, chunk] = up[at] - diff
                            else:
                                both = f[comp][pq + "s"]
                                ups.append(both + diff)
                                if up:
                                    node_ref[element, at, chunk] = up[at] + (both - diff)
                    low, up = high, ups
            for node in range(first + 1, end):
                for comp in range(3):
                    g = [[node_ref[node, comp * 4 + i, chunk] for chunk in chunks] for i in range(4)]
                    if sweep == 1:
                        before = packed(node - SWEEPS, case, comp)
                    else:
                        before = [res_ref[comp, node, chunk] for chunk in chunks]
                    for chunk, res in zip(chunks, sub(before, from_modes_xy(*g))):
                        step = keep * step_ref[comp, node, chunk] + take * (inv_ref[node, chunk] * res)
                        if sweep < SWEEPS:
                            res_ref[comp, node, chunk] = res
                            step_ref[comp, node, chunk] = step
                        if SWEEPS <= node <= SWEEPS + layers:
                            sol = sol_ref[comp, node - SWEEPS, chunk] + step
                            sol_ref[comp, node - SWEEPS, chunk] = sol
                            if sweep == SWEEPS and node < SWEEPS + layers:
                                disp_ref[case, comp, node - SWEEPS, chunk] = sol
            factor = factor_next
        pltpu.make_async_copy(disp_ref.at[case], disp_hbm.at[case], disp_sem.at[case]).start()

        weight = weights_ref[load * cases + case].astype(jnp.float32)
        for node in range(layers + 1):
            for comp in range(3):
                store_modes(node, comp, [sol_ref[comp, node, chunk] for chunk in chunks])
        for chunk in chunks:
            low = load_modes(0, chunk)
            for layer in range(layers):
                high = load_modes(layer + 1, chunk)
                energy = weight * mode_energy(modes_z(low, high))
                before = jnp.where(case == 0, 0.0, energy_ref[layer, chunk])
                energy_ref[layer, chunk] = before + energy
                low = high
        return carry

    lax.fori_loop(0, cases, one_case, 0)
    weight_sum = weights_ref[0]
    for at in range(1, weights_ref.shape[0]):
        weight_sum = weight_sum + weights_ref[at]
    weight_sum = jnp.full((8, columns), weight_sum.astype(jnp.float32))
    scale = (SHEAR / 48) / weight_sum

    spans = filter_layers(
        [[jnp.where(inside(at), a, 0.0) for a in packed(at, None, 0)] for at in range(-2, layers + 2)]
    )
    recs = [
        [jnp.where(inside(layer), 1.0 / jnp.where(inside(layer), a, 1.0), 0.0) for a in span]
        for layer, span in zip(range(-1, layers + 1), spans)
    ]
    shares = filter_layers(recs)
    total = jnp.zeros((8, columns), jnp.float32)
    own_rows = own_ref.shape[2]
    own = pl.ds(pl.multiple_of(load * own_rows, own_rows), own_rows)
    for layer in range(layers):
        for kind in range(2):
            own_ref[1 + kind, layer] = pack_refs[0][pack_plane(cases, layers, cases, kind, layer), own]
        for at, chunk in enumerate(chunks):
            inner = pl.ds(8 + 8 * at, 8)
            sens = weight_ref[layer, inner] * (energy_ref[layer, chunk] * scale)
            weight_ref[layer, inner] = sens
            total = total + sens * shares[layer][at]
            energy_ref[layer, chunk] = recs[layer + 1][at]
        own_ref[0, layer] = energy_ref[layer, own]
        weight_ref[layer, :8] = jnp.zeros((8, columns), jnp.float32)
        weight_ref[layer, 8 + rows :] = jnp.zeros((8, columns), jnp.float32)
    share = jnp.sum(total, axis=0, keepdims=True)
    wide = own_rows + 2
    for step, slot_ref in enumerate(slot_refs):
        start = pl.multiple_of(partner(load, step) * own_rows, own_rows)
        for layer in range(layers):
            window = weight_ref[layer, pl.ds(start, own_rows + 16)]
            slot_ref[layer * wide : (layer + 1) * wide] = window[7 : 7 + wide]
        slot_ref[layers * wide : layers * wide + 1] = share
    for case in range(cases):
        pltpu.make_async_copy(disp_ref.at[case], disp_hbm.at[case], disp_sem.at[case]).wait()


def pack_plane(cases, layers, group, kind, layer):
    return (group * 3 + kind) * layers + layer


def stage_kernel(labels_ref, forces_ref, pack_ref):
    cases, _, layers, _, _ = forces_ref.shape
    for case in range(cases):
        for comp in range(3):
            for layer in range(layers):
                pack_ref[pack_plane(cases, layers, case, comp, layer)] = forces_ref[case, comp, layer]
    for layer in range(layers):
        marks = labels_ref[layer].astype(jnp.float32)
        pack_ref[pack_plane(cases, layers, cases, 1, layer)] = marks


def design_kernel(cases, steps, *refs):
    density_refs = refs[1 : 1 + len(steps)]
    pack_ref, design_ref = refs[-2:]
    layers, own_rows, _ = density_refs[0].shape
    load = lax.axis_index("load")
    for step, density_ref in zip(steps, density_refs):
        start = pl.multiple_of(partner(load, step) * own_rows, own_rows)
        for layer in range(layers):
            plane = pack_plane(cases, layers, cases, 0, layer)
            pack_ref[plane, pl.ds(start, own_rows)] = density_ref[layer]
    design_ref[...] = pack_ref[cases * 3 * layers :]


def join_kernel(force_ref, design_ref, *refs):
    pack_ref = refs[-1]
    cases, _, layers, _, _ = force_ref.shape
    for case in range(cases):
        for comp in range(3):
            for layer in range(layers):
                pack_ref[pack_plane(cases, layers, case, comp, layer)] = force_ref[case, comp, layer]
    pack_ref[cases * 3 * layers :] = design_ref[...]


def sum_kernel(*refs):
    total = refs[0][...]
    for ref in refs[1:-1]:
        total = total + ref[...]
    refs[-1][...] = total


def forward_kernel(layers, wide, sum_ref, beside_ref, out_ref):
    even = lax.axis_index("gz") % 2 == 0
    end = layers * wide
    out_ref[:wide] = jnp.where(even, beside_ref[end - wide : end], beside_ref[:wide])
    out_ref[wide : wide + 1] = sum_ref[end : end + 1] + beside_ref[end : end + 1]


def share_kernel(wide, mine_ref, *refs):
    out_ref = refs[-1]
    out_ref[...] = mine_ref[...]
    out_ref[wide : wide + 1] = share_sum(wide, mine_ref, *refs[:-1])


def share_sum(wide, *refs):
    total = refs[0][wide : wide + 1]
    for ref in refs[1:]:
        total = total + ref[wide : wide + 1]
    return total


def chip_rounds(count_gz):
    edges = []
    while 2 ** (len(edges) + 1) < count_gz:
        edges.append(2 ** (len(edges) + 1) - 1)
    pairs = [edges[at : at + 2] for at in range(0, len(edges), 2)]
    return [[pair[0], pair[0] ^ pair[1], pair[1]] if len(pair) == 2 else pair for pair in pairs]


def update_kernel(cells, rounds, *refs):
    sum_ref, beside_ref, mine_ref = refs[:3]
    other_refs = refs[3:-2]
    own_ref, new_ref = refs[-2:]
    _, layers, own_rows, columns = own_ref.shape
    wide = own_rows + 2
    gz = lax.axis_index("gz")
    even, chip = gz % 2 == 0, gz // 2
    beside = jnp.where(even, beside_ref[:wide], beside_ref[(layers - 1) * wide : layers * wide])
    across = jnp.zeros((wide, columns), jnp.float32)
    for mask, other_ref in zip(sum(rounds, []), other_refs):
        borders = (chip ^ mask) == jnp.where(even, chip - 1, chip + 1)
        across = jnp.where(borders, other_ref[:wide], across)
    numers = [jnp.where(even, across, beside)]
    numers += [sum_ref[layer * wide : (layer + 1) * wide] for layer in range(layers)]
    numers += [jnp.where(even, beside, across)]
    near, far = [], []
    for numer in numers:
        back, mid, front = (numer[at : at + own_rows] for at in range(3))
        sides = back + front
        cross = sides + (last_x(mid) + next_x(mid))
        near.append(1.5 * mid + 0.5 * cross + EDGE * (last_x(sides) + next_x(sides)))
        far.append(0.5 * mid + EDGE * cross)
    total = share_sum(wide, mine_ref, *other_refs[-len(rounds[-1]) :])
    mean = jnp.sum(total, keepdims=True) * (1.0 / cells)
    mean = jnp.broadcast_to(mean, (own_rows, columns))
    for layer in range(layers):
        numer = near[layer + 1] + (far[layer] + far[layer + 2])
        filtered = numer * own_ref[0, layer]
        density = own_ref[1, layer]
        candidate = density * jnp.sqrt(filtered / mean)
        lower = jnp.maximum(density - MOVE_LIMIT, FLOOR_DENSITY)
        upper = jnp.minimum(density + MOVE_LIMIT, 1.0)
        updated = jnp.minimum(jnp.maximum(candidate, lower), upper)
        new_ref[layer] = jnp.where(own_ref[2, layer] == 2.0, 1.0, updated)


def met(block, axis, step):
    count = lax.axis_size(axis)
    return lax.ppermute(block, axis, [(partner(i, step), i) for i in range(count)])


def across_pairs(far, count):
    up = [(i - far, i) for i in range(0, count, 2) if i - far >= 0]
    down = [(i + far, i) for i in range(1, count, 2) if i + far < count]
    free = [i for i in range(count) if i not in dict(up + down)]
    empty = [i for i in range(count) if i not in dict(up + down).values()]
    return up + down + list(zip(free, empty))


def on_device(density, labels, forces, case_weights):
    count_gz, count_load = lax.axis_size("gz"), lax.axis_size("load")
    cases, _, layers, rows, columns = forces.shape
    own_rows = density.shape[1]
    nodes = layers + 2 * SWEEPS + 1
    hops = -(-(SWEEPS + 1) // layers)
    wide = own_rows + 2
    f32 = jnp.float32
    plane = (rows, columns)
    plane_bytes = rows * columns * 4
    vmem = pl.BlockSpec(memory_space=pltpu.VMEM)
    smem = pl.BlockSpec(memory_space=pltpu.SMEM)

    def shape(*dims):
        return jax.ShapeDtypeStruct(dims, f32)

    def call(kernel, out, args, planes, flops, in_specs=None, scratch=(), **more):
        limit = planes * plane_bytes + (2 << 20)
        return pl.pallas_call(
            kernel,
            out_shape=out,
            in_specs=in_specs or [vmem] * len(args),
            out_specs=more.pop("out_specs", vmem),
            scratch_shapes=scratch,
            compiler_params=pltpu.CompilerParams(vmem_limit_bytes=limit),
            cost_estimate=pl.CostEstimate(flops=flops, bytes_accessed=flops // 10, transcendentals=0),
            **more,
        )(*args)

    planes = (cases * 3 + 2) * layers
    far_forces = [
        lax.ppermute(forces, "gz", across_pairs(far, count_gz)) for far in range(1, hops + 1)
    ]
    pack = call(stage_kernel, shape(planes, rows, columns), (labels, forces), 2 * planes, 1_000_000)
    steps = [0] + list(range(2, count_load)) + [1]
    densities = [density] + [met(density, "load", step) for step in steps[1:]]
    pack, design = call(
        functools.partial(design_kernel, cases, steps),
        (shape(planes, rows, columns), shape(2 * layers, rows, columns)),
        (pack, *densities, *far_forces),
        2 * planes + 6 * layers,
        100_000,
        in_specs=[vmem] * (1 + count_load) + [pl.BlockSpec(memory_space=pl.ANY)] * hops,
        out_specs=(vmem, vmem),
        input_output_aliases={0: 0},
    )
    far_designs = [
        lax.ppermute(design, "gz", across_pairs(far, count_gz)) for far in range(1, hops + 1)
    ]
    beside, packs = pack, [pack]
    for at in range(hops):
        packs += [met(beside, "gz", 1), far_designs[at], far_forces[at]]
        if at < hops - 1:
            later = far_designs[at + 1 :]
            beside = call(
                join_kernel,
                shape(planes, rows, columns),
                (far_forces[at], far_designs[at], *later),
                2 * planes,
                100_000,
                in_specs=[vmem] * 2 + [pl.BlockSpec(memory_space=pl.ANY)] * len(later),
            )

    slot_rows = -(-(layers * wide + 1) // 8) * 8
    scratch = [
        pltpu.VMEM((4, nodes - 1) + plane, f32),
        pltpu.VMEM((nodes,) + plane, f32),
        pltpu.VMEM((3, nodes) + plane, f32),
        pltpu.VMEM((3, nodes) + plane, f32),
        pltpu.VMEM((3, layers + 1) + plane, f32),
        pltpu.VMEM((nodes, 12) + plane, f32),
        pltpu.VMEM((nodes, 12) + plane, f32),
        pltpu.VMEM(forces.shape, f32),
        pltpu.VMEM((layers, rows + 16, columns), f32),
        pltpu.VMEM((layers,) + plane, f32),
        pltpu.SemaphoreType.DMA((cases,)),
    ]
    smooth_planes = nodes * 35 + 3 * (layers + 1) + 4 * layers
    smooth_planes += (1 + 2 * hops) * planes + cases * 3 * layers + 8 * layers
    displacement, own, *slots = call(
        functools.partial(smooth_kernel, hops, count_gz),
        (shape(*forces.shape), shape(3, layers, own_rows, columns))
        + (shape(slot_rows, columns),) * count_load,
        (case_weights, *packs),
        smooth_planes,
        60_000_000,
        in_specs=[smem] + [vmem] * len(packs),
        out_specs=(pl.BlockSpec(memory_space=pltpu.HBM),) + (vmem,) * (1 + count_load),
        scratch=scratch,
    )

    received = [met(slots[step], "load", step) for step in range(count_load - 1, 0, -1)]
    whole = call(sum_kernel, shape(slot_rows, columns), (slots[0], *received), 2 * count_load, 100_000)
    beside = met(whole, "gz", 1)
    forward_rows = -(-(wide + 1) // 8) * 8
    mine = call(
        functools.partial(forward_kernel, layers, wide),
        shape(forward_rows, columns),
        (whole, beside),
        4 * layers,
        10_000,
    )
    others = []
    rounds = chip_rounds(count_gz)
    for at, masks in enumerate(rounds):
        if at > 0:
            mine = call(
                functools.partial(share_kernel, wide),
                shape(forward_rows, columns),
                (mine, *others[-len(rounds[at - 1]) :]),
                8,
                10_000,
            )
        others += [met(mine, "gz", 2 * mask) for mask in masks]
    new_density = call(
        functools.partial(update_kernel, float(count_gz * layers * rows * columns), rounds),
        shape(*density.shape),
        (whole, beside, mine, *others, own),
        8 * layers,
        100_000,
    )
    return (new_density, displacement)


def solution(mesh):
    return jax.shard_map(
        on_device,
        mesh=mesh,
        in_specs=(
            P("gz", "load", None),
            P("gz", None, None),
            P("load", None, "gz", None, None),
            P(),
        ),
        out_specs=(P("gz", "load", None), P("load", None, "gz", None, None)),
        check_vma=False,
    )
```

```python
import functools

import jax
import jax.numpy as jnp
from jax import lax
from jax.experimental import pallas as pl
from jax.experimental.pallas import tpu as pltpu
from jax.sharding import PartitionSpec as P

SWEEPS = 3
EMIN = 0.001
LOWER_EIG = 0.1
UPPER_EIG = 2.5
MOVE_LIMIT = 0.2
FLOOR_DENSITY = 0.001
POISSON = 0.3
LAME = POISSON / ((1 + POISSON) * (1 - 2 * POISSON))
SHEAR = 1.0 / (2 * (1 + POISSON))
KE_DIAG = (LAME + 4 * SHEAR) / 9
EDGE = 1.5 - 2.0**0.5
PLANE = ("ss", "sd", "ds", "dd")


def chunks_of(rows):
    return [pl.ds(at, 8) for at in range(0, rows, 8)]


def next_x(a):
    lanes = a.shape[1]
    lane = lax.broadcasted_iota(jnp.int32, a.shape, 1)
    return jnp.where(lane == lanes - 1, 0.0, pltpu.roll(a, lanes - 1, 1))


def last_x(a):
    lane = lax.broadcasted_iota(jnp.int32, a.shape, 1)
    return jnp.where(lane == 0, 0.0, pltpu.roll(a, 1, 1))


def next_y(plane):
    row = lax.broadcasted_iota(jnp.int32, plane[0].shape, 0)
    rolled = [pltpu.roll(a, 7, 0) for a in plane] + [jnp.zeros_like(plane[0])]
    return [jnp.where(row == 7, rolled[at + 1], rolled[at]) for at in range(len(plane))]


def last_y(plane):
    row = lax.broadcasted_iota(jnp.int32, plane[0].shape, 0)
    rolled = [jnp.zeros_like(plane[0])] + [pltpu.roll(a, 1, 0) for a in plane]
    return [jnp.where(row == 0, rolled[at], rolled[at + 1]) for at in range(len(plane))]


def add(*planes):
    return [sum(chunks[1:], chunks[0]) for chunks in zip(*planes)]


def sub(one, other):
    return [a - b for a, b in zip(one, other)]


def to_modes_xy(u):
    ux = [next_x(a) for a in u]
    s, d = add(ux, u), sub(ux, u)
    sy, dy = next_y(s), next_y(d)
    return add(sy, s), sub(sy, s), add(dy, d), sub(dy, d)


def from_modes_xy(ss, sd, ds, dd):
    s = add(sub(ss, sd), last_y(add(ss, sd)))
    d = add(sub(ds, dd), last_y(add(ds, dd)))
    return add(sub(s, d), [last_x(a) for a in add(s, d)])


def modes_z(low, high):
    modes = []
    for comp in range(3):
        one = {}
        for pq in PLANE:
            if pq != "ss":
                one[pq + "s"] = high[comp][pq] + low[comp][pq]
            one[pq + "d"] = high[comp][pq] - low[comp][pq]
        modes.append(one)
    return modes


NORMAL = ((0, "dss"), (1, "sds"), (2, "ssd"))
BENDS = (((1, "dds"), (2, "dsd")), ((0, "dds"), (2, "sdd")), ((0, "dsd"), (1, "sdd")))
SHEARS = (((0, "sds"), (1, "dss")), ((0, "ssd"), (2, "dss")), ((1, "ssd"), (2, "sds")))
STIFF = (SHEAR / 16, SHEAR / 48, (LAME + 4 * SHEAR) / 144, SHEAR / 8)
TWIST = ((0, "sdd"), (1, "dsd"), (2, "dds"))


def mode_forces(modes, e1, e2, e3, e4):
    m = lambda key: modes[key[0]][key[1]]
    out = [{}, {}, {}]

    def put(key, value):
        out[key[0]][key[1]] = value

    trace = (LAME / (2 * SHEAR)) * (m(NORMAL[0]) + m(NORMAL[1]) + m(NORMAL[2]))
    for key in NORMAL:
        put(key, e4 * (trace + m(key)))
    for a, b in BENDS:
        t = (LAME / (3 * SHEAR)) * (m(a) + m(b))
        put(a, e1 * (t + m(a)))
        put(b, e1 * (t + m(b)))
    for a, b in SHEARS:
        f = e1 * (m(a) + m(b))
        put(a, f)
        put(b, f)
    t = m(TWIST[0]) + m(TWIST[1]) + m(TWIST[2])
    for key in TWIST:
        put(key, e2 * (t + m(key)))
    for comp in range(3):
        put((comp, "ddd"), e3 * modes[comp]["ddd"])
    return out


def mode_energy(modes):
    m = lambda key: modes[key[0]][key[1]]
    sq = lambda v: v * v
    n = [m(key) for key in NORMAL]
    total = (3 * LAME / SHEAR) * sq(n[0] + n[1] + n[2]) + 6.0 * (sq(n[0]) + sq(n[1]) + sq(n[2]))
    shear = None
    for a, b in SHEARS:
        t = sq(m(a) + m(b))
        shear = t if shear is None else shear + t
    total = total + 3.0 * shear
    sums, own = None, None
    for a, b in BENDS:
        t = sq(m(a) + m(b))
        o = sq(m(a)) + sq(m(b))
        sums = t if sums is None else sums + t
        own = o if own is None else own + o
    total = total + (LAME / SHEAR) * sums + 3.0 * own
    a, b, c = (m(key) for key in TWIST)
    total = total + (sq(a + b) + sq(a + c) + sq(b + c))
    bulk = sq(modes[0]["ddd"]) + sq(modes[1]["ddd"]) + sq(modes[2]["ddd"])
    return total + ((LAME + 4 * SHEAR) / (3 * SHEAR)) * bulk


def filter_planes(plane):
    x = [last_x(a) + next_x(a) for a in plane]
    cross = add(x, add(last_y(plane), next_y(plane)))
    diagonal = add(last_y(x), next_y(x))
    near = [1.5 * a + 0.5 * c + EDGE * d for a, c, d in zip(plane, cross, diagonal)]
    return near, [0.5 * a + EDGE * c for a, c in zip(plane, cross)]


def filter_layers(layers):
    pairs = [filter_planes(plane) for plane in layers]
    return [
        add(pairs[at][0], add(pairs[at - 1][1], pairs[at + 1][1])) for at in range(1, len(layers) - 1)
    ]


def partner(index, step):
    return index ^ step


def smooth_kernel(hops, count_gz, *refs):
    blocks = 4 * hops
    weights_ref = refs[0]
    pack_refs = refs[1 : 1 + blocks]
    disp_hbm, own_ref = refs[1 + blocks : 3 + blocks]
    slot_refs = refs[3 + blocks : -11]
    stiff_ref, inv_ref, res_ref, step_ref, sol_ref, mode_ref, node_ref = refs[-11:-4]
    disp_ref, weight_ref, energy_ref, disp_sem = refs[-4:]

    cases, _, layers, rows, columns = disp_ref.shape
    nodes = layers + 2 * SWEEPS + 1
    chunks = chunks_of(rows)
    gz = lax.axis_index("gz")
    load = lax.axis_index("load")
    even = gz % 2 == 0

    def packed(layer, group, kind):
        hop = layer // layers
        inner = layer - hop * layers
        plane = pack_plane(cases, layers, cases if group is None else group, kind, inner)
        if hop == 0:
            return [pack_refs[0][plane, chunk] for chunk in chunks]

        def pick(design_ref, force_ref):
            if group is None:
                return [design_ref[kind * layers + inner, chunk] for chunk in chunks]
            return [force_ref[group, kind, inner, chunk] for chunk in chunks]

        at = 4 * abs(hop) - 2
        across = pick(*pack_refs[at : at + 2])
        if abs(hop) == 1:
            beside = [pack_refs[1][plane, chunk] for chunk in chunks]
        else:
            beside = pick(*pack_refs[at - 2 : at])
        by_sibling = even == (hop > 0)
        return [jnp.where(by_sibling, one, other) for one, other in zip(beside, across)]

    def inside(layer):
        owner = gz + layer // layers
        return jnp.logical_and(owner >= 0, owner < count_gz)

    below = None
    for at in range(nodes + 1):
        layer = at - SWEEPS - 1
        live = jnp.where(inside(layer), 1.0, 0.0)
        marks = packed(layer, None, 1)
        moduli = []
        for chunk_at, (dense, mark) in enumerate(zip(packed(layer, None, 0), marks)):
            solid = jnp.where(mark == 2.0, 1.0, dense)
            modulus = (EMIN + (1.0 - EMIN) * solid * solid * solid) * live
            moduli.append(modulus)
            if 0 <= layer < layers:
                weight = (3.0 * (1.0 - EMIN)) * solid * solid * dense
                weight_ref[layer, pl.ds(8 + 8 * chunk_at, 8)] = weight
            if 1 <= at < nodes:
                for kind, factor in enumerate(STIFF):
                    stiff_ref[kind, at - 1, chunks[chunk_at]] = modulus * factor
        spread = add(moduli, [last_x(a) for a in moduli])
        spread = add(spread, last_y(spread))
        if at > 0:
            for chunk, mark, low, high in zip(chunks, marks, below, spread):
                free = jnp.logical_and(mark != 1.0, inside(layer))
                diag = jnp.where(free, KE_DIAG * (low + high), 1.0)
                inv_ref[at - 1, chunk] = jnp.where(free, 1.0 / diag, 0.0)
        below = spread

    theta = 0.5 * (UPPER_EIG + LOWER_EIG)
    delta = 0.5 * (UPPER_EIG - LOWER_EIG)
    sigma = theta / delta

    def load_modes(node, chunk):
        return [
            {pq: mode_ref[node, comp * 4 + i, chunk] for i, pq in enumerate(PLANE)}
            for comp in range(3)
        ]

    def store_modes(node, comp, field):
        for i, plane in enumerate(to_modes_xy(field)):
            for chunk, a in zip(chunks, plane):
                mode_ref[node, comp * 4 + i, chunk] = a

    def one_case(case, carry):
        for at in range(nodes):
            for comp in range(3):
                field = []
                for chunk, force in zip(chunks, packed(at - SWEEPS, case, comp)):
                    step = inv_ref[at, chunk] * force * (1.0 / theta)
                    field.append(step)
                    if 1 <= at < nodes - 1:
                        step_ref[comp, at, chunk] = step
                    if SWEEPS <= at <= SWEEPS + layers:
                        sol_ref[comp, at - SWEEPS, chunk] = step
                store_modes(at, comp, field)

        factor = 1.0 / sigma
        for sweep in range(1, SWEEPS + 1):
            factor_next = 1.0 / (2.0 * sigma - factor)
            keep, take = factor_next * factor, 2.0 * factor_next / delta
            first, end = sweep - 1, nodes - sweep
            if sweep > 1:
                for node in range(first, end + 1):
                    for comp in range(3):
                        store_modes(node, comp, [step_ref[comp, node, chunk] for chunk in chunks])
            for chunk in chunks:
                low = load_modes(first, chunk)
                up = None
                for element in range(first, end):
                    high = load_modes(element + 1, chunk)
                    stiff = [stiff_ref[kind, element, chunk] for kind in range(4)]
                    f = mode_forces(modes_z(low, high), *stiff)
                    ups = []
                    for comp in range(3):
                        for i, pq in enumerate(PLANE):
                            diff = f[comp][pq + "d"]
                            at = comp * 4 + i
                            if pq == "ss":
                                ups.append(diff)
                                if up:
                                    node_ref[element, at, chunk] = up[at] - diff
                            else:
                                both = f[comp][pq + "s"]
                                ups.append(both + diff)
                                if up:
                                    node_ref[element, at, chunk] = up[at] + (both - diff)
                    low, up = high, ups
            for node in range(first + 1, end):
                for comp in range(3):
                    g = [[node_ref[node, comp * 4 + i, chunk] for chunk in chunks] for i in range(4)]
                    if sweep == 1:
                        before = packed(node - SWEEPS, case, comp)
                    else:
                        before = [res_ref[comp, node, chunk] for chunk in chunks]
                    for chunk, res in zip(chunks, sub(before, from_modes_xy(*g))):
                        step = keep * step_ref[comp, node, chunk] + take * (inv_ref[node, chunk] * res)
                        if sweep < SWEEPS:
                            res_ref[comp, node, chunk] = res
                            step_ref[comp, node, chunk] = step
                        if SWEEPS <= node <= SWEEPS + layers:
                            sol = sol_ref[comp, node - SWEEPS, chunk] + step
                            sol_ref[comp, node - SWEEPS, chunk] = sol
                            if sweep == SWEEPS and node < SWEEPS + layers:
                                disp_ref[case, comp, node - SWEEPS, chunk] = sol
            factor = factor_next
        pltpu.make_async_copy(disp_ref.at[case], disp_hbm.at[case], disp_sem.at[case]).start()

        weight = weights_ref[load * cases + case].astype(jnp.float32)
        for node in range(layers + 1):
            for comp in range(3):
                store_modes(node, comp, [sol_ref[comp, node, chunk] for chunk in chunks])
        for chunk in chunks:
            low = load_modes(0, chunk)
            for layer in range(layers):
                high = load_modes(layer + 1, chunk)
                energy = weight * mode_energy(modes_z(low, high))
                before = jnp.where(case == 0, 0.0, energy_ref[layer, chunk])
                energy_ref[layer, chunk] = before + energy
                low = high
        return carry

    lax.fori_loop(0, cases, one_case, 0)
    weight_sum = weights_ref[0]
    for at in range(1, weights_ref.shape[0]):
        weight_sum = weight_sum + weights_ref[at]
    weight_sum = jnp.full((8, columns), weight_sum.astype(jnp.float32))
    scale = (SHEAR / 48) / weight_sum

    spans = filter_layers(
        [[jnp.where(inside(at), a, 0.0) for a in packed(at, None, 0)] for at in range(-2, layers + 2)]
    )
    recs = [
        [jnp.where(inside(layer), 1.0 / jnp.where(inside(layer), a, 1.0), 0.0) for a in span]
        for layer, span in zip(range(-1, layers + 1), spans)
    ]
    shares = filter_layers(recs)
    total = jnp.zeros((8, columns), jnp.float32)
    own_rows = own_ref.shape[2]
    own = pl.ds(pl.multiple_of(load * own_rows, own_rows), own_rows)
    for layer in range(layers):
        for kind in range(2):
            own_ref[1 + kind, layer] = pack_refs[0][pack_plane(cases, layers, cases, kind, layer), own]
        for at, chunk in enumerate(chunks):
            inner = pl.ds(8 + 8 * at, 8)
            sens = weight_ref[layer, inner] * (energy_ref[layer, chunk] * scale)
            weight_ref[layer, inner] = sens
            total = total + sens * shares[layer][at]
            energy_ref[layer, chunk] = recs[layer + 1][at]
        own_ref[0, layer] = energy_ref[layer, own]
        weight_ref[layer, :8] = jnp.zeros((8, columns), jnp.float32)
        weight_ref[layer, 8 + rows :] = jnp.zeros((8, columns), jnp.float32)
    share = jnp.sum(total, axis=0, keepdims=True)
    wide = own_rows + 2
    for step, slot_ref in enumerate(slot_refs):
        start = pl.multiple_of(partner(load, step) * own_rows, own_rows)
        for layer in range(layers):
            window = weight_ref[layer, pl.ds(start, own_rows + 16)]
            slot_ref[layer * wide : (layer + 1) * wide] = window[7 : 7 + wide]
        slot_ref[layers * wide : layers * wide + 1] = share
    for case in range(cases):
        pltpu.make_async_copy(disp_ref.at[case], disp_hbm.at[case], disp_sem.at[case]).wait()


def pack_plane(cases, layers, group, kind, layer):
    return (group * 3 + kind) * layers + layer


def stage_kernel(labels_ref, forces_ref, pack_ref):
    cases, _, layers, _, _ = forces_ref.shape
    for case in range(cases):
        for comp in range(3):
            for layer in range(layers):
                pack_ref[pack_plane(cases, layers, case, comp, layer)] = forces_ref[case, comp, layer]
    for layer in range(layers):
        marks = labels_ref[layer].astype(jnp.float32)
        pack_ref[pack_plane(cases, layers, cases, 1, layer)] = marks


def design_kernel(cases, steps, *refs):
    density_refs = refs[1 : 1 + len(steps)]
    pack_ref, design_ref = refs[-2:]
    layers, own_rows, _ = density_refs[0].shape
    load = lax.axis_index("load")
    for step, density_ref in zip(steps, density_refs):
        start = pl.multiple_of(partner(load, step) * own_rows, own_rows)
        for layer in range(layers):
            plane = pack_plane(cases, layers, cases, 0, layer)
            pack_ref[plane, pl.ds(start, own_rows)] = density_ref[layer]
    design_ref[...] = pack_ref[cases * 3 * layers :]


def sum_kernel(*refs):
    total = refs[0][...]
    for ref in refs[1:-1]:
        total = total + ref[...]
    refs[-1][...] = total


def forward_kernel(layers, wide, sum_ref, beside_ref, out_ref):
    even = lax.axis_index("gz") % 2 == 0
    end = layers * wide
    out_ref[:wide] = jnp.where(even, beside_ref[end - wide : end], beside_ref[:wide])
    out_ref[wide : wide + 1] = sum_ref[end : end + 1] + beside_ref[end : end + 1]


def share_kernel(wide, mine_ref, *refs):
    out_ref = refs[-1]
    out_ref[...] = mine_ref[...]
    out_ref[wide : wide + 1] = share_sum(wide, mine_ref, *refs[:-1])


def share_sum(wide, *refs):
    total = refs[0][wide : wide + 1]
    for ref in refs[1:]:
        total = total + ref[wide : wide + 1]
    return total


def chip_rounds(count_gz):
    edges = []
    while 2 ** (len(edges) + 1) < count_gz:
        edges.append(2 ** (len(edges) + 1) - 1)
    pairs = [edges[at : at + 2] for at in range(0, len(edges), 2)]
    return [[pair[0], pair[0] ^ pair[1], pair[1]] if len(pair) == 2 else pair for pair in pairs]


def update_kernel(cells, rounds, *refs):
    sum_ref, beside_ref, mine_ref = refs[:3]
    other_refs = refs[3:-2]
    own_ref, new_ref = refs[-2:]
    _, layers, own_rows, columns = own_ref.shape
    wide = own_rows + 2
    gz = lax.axis_index("gz")
    even, chip = gz % 2 == 0, gz // 2
    beside = jnp.where(even, beside_ref[:wide], beside_ref[(layers - 1) * wide : layers * wide])
    across = jnp.zeros((wide, columns), jnp.float32)
    for mask, other_ref in zip(sum(rounds, []), other_refs):
        borders = (chip ^ mask) == jnp.where(even, chip - 1, chip + 1)
        across = jnp.where(borders, other_ref[:wide], across)
    numers = [jnp.where(even, across, beside)]
    numers += [sum_ref[layer * wide : (layer + 1) * wide] for layer in range(layers)]
    numers += [jnp.where(even, beside, across)]
    near, far = [], []
    for numer in numers:
        back, mid, front = (numer[at : at + own_rows] for at in range(3))
        sides = back + front
        cross = sides + (last_x(mid) + next_x(mid))
        near.append(1.5 * mid + 0.5 * cross + EDGE * (last_x(sides) + next_x(sides)))
        far.append(0.5 * mid + EDGE * cross)
    total = share_sum(wide, mine_ref, *other_refs[-len(rounds[-1]) :])
    mean = jnp.sum(total, keepdims=True) * (1.0 / cells)
    mean = jnp.broadcast_to(mean, (own_rows, columns))
    for layer in range(layers):
        numer = near[layer + 1] + (far[layer] + far[layer + 2])
        filtered = numer * own_ref[0, layer]
        density = own_ref[1, layer]
        candidate = density * jnp.sqrt(filtered / mean)
        lower = jnp.maximum(density - MOVE_LIMIT, FLOOR_DENSITY)
        upper = jnp.minimum(density + MOVE_LIMIT, 1.0)
        updated = jnp.minimum(jnp.maximum(candidate, lower), upper)
        new_ref[layer] = jnp.where(own_ref[2, layer] == 2.0, 1.0, updated)


def met(block, axis, step):
    count = lax.axis_size(axis)
    return lax.ppermute(block, axis, [(partner(i, step), i) for i in range(count)])


def far_pairs(far, count, across):
    pairs = [(i - far if (i % 2 == 0) == across else i + far, i) for i in range(count)]
    pairs = [(source, i) for source, i in pairs if 0 <= source < count]
    free = [i for i in range(count) if i not in dict(pairs)]
    empty = [i for i in range(count) if i not in dict(pairs).values()]
    return pairs + list(zip(free, empty))


def on_device(density, labels, forces, case_weights):
    count_gz, count_load = lax.axis_size("gz"), lax.axis_size("load")
    cases, _, layers, rows, columns = forces.shape
    own_rows = density.shape[1]
    nodes = layers + 2 * SWEEPS + 1
    hops = -(-(SWEEPS + 1) // layers)
    wide = own_rows + 2
    f32 = jnp.float32
    plane = (rows, columns)
    plane_bytes = rows * columns * 4
    vmem = pl.BlockSpec(memory_space=pltpu.VMEM)
    smem = pl.BlockSpec(memory_space=pltpu.SMEM)

    def shape(*dims):
        return jax.ShapeDtypeStruct(dims, f32)

    def call(kernel, out, args, planes, flops, in_specs=None, scratch=(), **more):
        limit = planes * plane_bytes + (2 << 20)
        return pl.pallas_call(
            kernel,
            out_shape=out,
            in_specs=in_specs or [vmem] * len(args),
            out_specs=more.pop("out_specs", vmem),
            scratch_shapes=scratch,
            compiler_params=pltpu.CompilerParams(vmem_limit_bytes=limit),
            cost_estimate=pl.CostEstimate(flops=flops, bytes_accessed=flops // 10, transcendentals=0),
            **more,
        )(*args)

    planes = (cases * 3 + 2) * layers
    far_forces = [
        lax.ppermute(forces, "gz", far_pairs(far, count_gz, True)) for far in range(1, hops + 1)
    ]
    pack = call(stage_kernel, shape(planes, rows, columns), (labels, forces), 2 * planes, 1_000_000)
    steps = [0] + list(range(2, count_load)) + [1]
    densities = [density] + [met(density, "load", step) for step in steps[1:]]
    pack, design = call(
        functools.partial(design_kernel, cases, steps),
        (shape(planes, rows, columns), shape(2 * layers, rows, columns)),
        (pack, *densities, *far_forces),
        2 * planes + 6 * layers,
        100_000,
        in_specs=[vmem] * (1 + count_load) + [pl.BlockSpec(memory_space=pl.ANY)] * hops,
        out_specs=(vmem, vmem),
        input_output_aliases={0: 0},
    )
    packs = [pack, met(pack, "gz", 1)]
    for far, forces_far in enumerate(far_forces, 1):
        if far > 1:
            packs.append(lax.ppermute(design, "gz", far_pairs(far, count_gz, False)))
            packs.append(met(far_forces[far - 2], "gz", 1))
        packs += [lax.ppermute(design, "gz", far_pairs(far, count_gz, True)), forces_far]

    slot_rows = -(-(layers * wide + 1) // 8) * 8
    scratch = [
        pltpu.VMEM((4, nodes - 1) + plane, f32),
        pltpu.VMEM((nodes,) + plane, f32),
        pltpu.VMEM((3, nodes) + plane, f32),
        pltpu.VMEM((3, nodes) + plane, f32),
        pltpu.VMEM((3, layers + 1) + plane, f32),
        pltpu.VMEM((nodes, 12) + plane, f32),
        pltpu.VMEM((nodes, 12) + plane, f32),
        pltpu.VMEM(forces.shape, f32),
        pltpu.VMEM((layers, rows + 16, columns), f32),
        pltpu.VMEM((layers,) + plane, f32),
        pltpu.SemaphoreType.DMA((cases,)),
    ]
    smooth_planes = nodes * 35 + 3 * (layers + 1) + 4 * layers
    smooth_planes += (1 + 2 * hops) * planes + cases * 3 * layers + 8 * layers
    displacement, own, *slots = call(
        functools.partial(smooth_kernel, hops, count_gz),
        (shape(*forces.shape), shape(3, layers, own_rows, columns))
        + (shape(slot_rows, columns),) * count_load,
        (case_weights, *packs),
        smooth_planes,
        60_000_000,
        in_specs=[smem] + [vmem] * len(packs),
        out_specs=(pl.BlockSpec(memory_space=pltpu.HBM),) + (vmem,) * (1 + count_load),
        scratch=scratch,
    )

    received = [met(slots[step], "load", step) for step in range(count_load - 1, 0, -1)]
    whole = call(sum_kernel, shape(slot_rows, columns), (slots[0], *received), 2 * count_load, 100_000)
    beside = met(whole, "gz", 1)
    forward_rows = -(-(wide + 1) // 8) * 8
    mine = call(
        functools.partial(forward_kernel, layers, wide),
        shape(forward_rows, columns),
        (whole, beside),
        4 * layers,
        10_000,
    )
    others = []
    rounds = chip_rounds(count_gz)
    for at, masks in enumerate(rounds):
        if at > 0:
            mine = call(
                functools.partial(share_kernel, wide),
                shape(forward_rows, columns),
                (mine, *others[-len(rounds[at - 1]) :]),
                8,
                10_000,
            )
        others += [met(mine, "gz", 2 * mask) for mask in masks]
    new_density = call(
        functools.partial(update_kernel, float(count_gz * layers * rows * columns), rounds),
        shape(*density.shape),
        (whole, beside, mine, *others, own),
        8 * layers,
        100_000,
    )
    return (new_density, displacement)


def solution(mesh):
    return jax.shard_map(
        on_device,
        mesh=mesh,
        in_specs=(
            P("gz", "load", None),
            P("gz", None, None),
            P("load", None, "gz", None, None),
            P(),
        ),
        out_specs=(P("gz", "load", None), P("load", None, "gz", None, None)),
        check_vma=False,
    )
```

```python
import functools

import jax
import jax.numpy as jnp
from jax import lax
from jax.experimental import pallas as pl
from jax.experimental.pallas import tpu as pltpu
from jax.sharding import PartitionSpec as P

SWEEPS = 3
EMIN = 0.001
LOWER_EIG = 0.1
UPPER_EIG = 2.5
MOVE_LIMIT = 0.2
FLOOR_DENSITY = 0.001
POISSON = 0.3
LAME = POISSON / ((1 + POISSON) * (1 - 2 * POISSON))
SHEAR = 1.0 / (2 * (1 + POISSON))
KE_DIAG = (LAME + 4 * SHEAR) / 9
EDGE = 1.5 - 2.0**0.5
PLANE = ("ss", "sd", "ds", "dd")


def chunks_of(rows):
    return [pl.ds(at, 8) for at in range(0, rows, 8)]


def next_x(a):
    lanes = a.shape[1]
    lane = lax.broadcasted_iota(jnp.int32, a.shape, 1)
    return jnp.where(lane == lanes - 1, 0.0, pltpu.roll(a, lanes - 1, 1))


def last_x(a):
    lane = lax.broadcasted_iota(jnp.int32, a.shape, 1)
    return jnp.where(lane == 0, 0.0, pltpu.roll(a, 1, 1))


def next_y(plane):
    row = lax.broadcasted_iota(jnp.int32, plane[0].shape, 0)
    rolled = [pltpu.roll(a, 7, 0) for a in plane] + [jnp.zeros_like(plane[0])]
    return [jnp.where(row == 7, rolled[at + 1], rolled[at]) for at in range(len(plane))]


def last_y(plane):
    row = lax.broadcasted_iota(jnp.int32, plane[0].shape, 0)
    rolled = [jnp.zeros_like(plane[0])] + [pltpu.roll(a, 1, 0) for a in plane]
    return [jnp.where(row == 0, rolled[at], rolled[at + 1]) for at in range(len(plane))]


def add(*planes):
    return [sum(chunks[1:], chunks[0]) for chunks in zip(*planes)]


def sub(one, other):
    return [a - b for a, b in zip(one, other)]


def to_modes_xy(u):
    ux = [next_x(a) for a in u]
    s, d = add(ux, u), sub(ux, u)
    sy, dy = next_y(s), next_y(d)
    return add(sy, s), sub(sy, s), add(dy, d), sub(dy, d)


def from_modes_xy(ss, sd, ds, dd):
    s = add(sub(ss, sd), last_y(add(ss, sd)))
    d = add(sub(ds, dd), last_y(add(ds, dd)))
    return add(sub(s, d), [last_x(a) for a in add(s, d)])


def modes_z(low, high):
    modes = []
    for comp in range(3):
        one = {}
        for pq in PLANE:
            if pq != "ss":
                one[pq + "s"] = high[comp][pq] + low[comp][pq]
            one[pq + "d"] = high[comp][pq] - low[comp][pq]
        modes.append(one)
    return modes


NORMAL = ((0, "dss"), (1, "sds"), (2, "ssd"))
BENDS = (((1, "dds"), (2, "dsd")), ((0, "dds"), (2, "sdd")), ((0, "dsd"), (1, "sdd")))
SHEARS = (((0, "sds"), (1, "dss")), ((0, "ssd"), (2, "dss")), ((1, "ssd"), (2, "sds")))
STIFF = (SHEAR / 16, SHEAR / 48, (LAME + 4 * SHEAR) / 144, SHEAR / 8)
TWIST = ((0, "sdd"), (1, "dsd"), (2, "dds"))


def mode_forces(mode, e1, e2, e3, e4, give):
    def normal():
        m = [mode(*key) for key in NORMAL]
        trace = (LAME / (2 * SHEAR)) * (m[0] + m[1] + m[2])
        for key, a in zip(NORMAL, m):
            give(*key, e4 * (trace + a))

    def bend(at):
        m = [mode(*key) for key in BENDS[at]]
        t = (LAME / (3 * SHEAR)) * (m[0] + m[1])
        for key, a in zip(BENDS[at], m):
            give(*key, e1 * (t + a))

    def shear(at):
        m = [mode(*key) for key in SHEARS[at]]
        f = e1 * (m[0] + m[1])
        for key in SHEARS[at]:
            give(*key, f)

    def twist():
        m = [mode(*key) for key in TWIST]
        t = m[0] + m[1] + m[2]
        for key, a in zip(TWIST, m):
            give(*key, e2 * (t + a))

    def bulk(comp):
        give(comp, "ddd", e3 * mode(comp, "ddd"))

    shear(0)
    twist()
    normal()
    bend(2)
    bend(0)
    bulk(1)
    shear(1)
    bend(1)
    bulk(0)
    shear(2)
    bulk(2)


def mode_energy(modes):
    m = lambda key: modes[key[0]][key[1]]
    sq = lambda v: v * v
    n = [m(key) for key in NORMAL]
    total = (3 * LAME / SHEAR) * sq(n[0] + n[1] + n[2]) + 6.0 * (sq(n[0]) + sq(n[1]) + sq(n[2]))
    shear = None
    for a, b in SHEARS:
        t = sq(m(a) + m(b))
        shear = t if shear is None else shear + t
    total = total + 3.0 * shear
    sums, own = None, None
    for a, b in BENDS:
        t = sq(m(a) + m(b))
        o = sq(m(a)) + sq(m(b))
        sums = t if sums is None else sums + t
        own = o if own is None else own + o
    total = total + (LAME / SHEAR) * sums + 3.0 * own
    a, b, c = (m(key) for key in TWIST)
    total = total + (sq(a + b) + sq(a + c) + sq(b + c))
    bulk = sq(modes[0]["ddd"]) + sq(modes[1]["ddd"]) + sq(modes[2]["ddd"])
    return total + ((LAME + 4 * SHEAR) / (3 * SHEAR)) * bulk


def filter_planes(plane):
    x = [last_x(a) + next_x(a) for a in plane]
    cross = add(x, add(last_y(plane), next_y(plane)))
    diagonal = add(last_y(x), next_y(x))
    near = [1.5 * a + 0.5 * c + EDGE * d for a, c, d in zip(plane, cross, diagonal)]
    return near, [0.5 * a + EDGE * c for a, c in zip(plane, cross)]


def filter_layers(layers):
    pairs = [filter_planes(plane) for plane in layers]
    return [
        add(pairs[at][0], add(pairs[at - 1][1], pairs[at + 1][1])) for at in range(1, len(layers) - 1)
    ]


def partner(index, step):
    return index ^ step


def smooth_kernel(hops, count_gz, *refs):
    blocks = 4 * hops
    weights_ref = refs[0]
    pack_refs = refs[1 : 1 + blocks]
    disp_hbm, own_ref = refs[1 + blocks : 3 + blocks]
    slot_refs = refs[3 + blocks : -11]
    stiff_ref, inv_ref, res_ref, step_ref, sol_ref, mode_ref, node_ref = refs[-11:-4]
    disp_ref, weight_ref, energy_ref, disp_sem = refs[-4:]

    cases, _, layers, rows, columns = disp_ref.shape
    nodes = layers + 2 * SWEEPS + 1
    chunks = chunks_of(rows)
    gz = lax.axis_index("gz")
    load = lax.axis_index("load")
    even = gz % 2 == 0

    def packed(layer, group, kind):
        hop = layer // layers
        inner = layer - hop * layers
        plane = pack_plane(cases, layers, cases if group is None else group, kind, inner)
        if hop == 0:
            return [pack_refs[0][plane, chunk] for chunk in chunks]

        def pick(design_ref, force_ref):
            if group is None:
                return [design_ref[kind * layers + inner, chunk] for chunk in chunks]
            return [force_ref[group, kind, inner, chunk] for chunk in chunks]

        at = 4 * abs(hop) - 2
        across = pick(*pack_refs[at : at + 2])
        if abs(hop) == 1:
            beside = [pack_refs[1][plane, chunk] for chunk in chunks]
        else:
            beside = pick(*pack_refs[at - 2 : at])
        by_sibling = even == (hop > 0)
        return [jnp.where(by_sibling, one, other) for one, other in zip(beside, across)]

    def inside(layer):
        owner = gz + layer // layers
        return jnp.logical_and(owner >= 0, owner < count_gz)

    below = None
    for at in range(nodes + 1):
        layer = at - SWEEPS - 1
        live = jnp.where(inside(layer), 1.0, 0.0)
        marks = packed(layer, None, 1)
        moduli = []
        for chunk_at, (dense, mark) in enumerate(zip(packed(layer, None, 0), marks)):
            solid = jnp.where(mark == 2.0, 1.0, dense)
            modulus = (EMIN + (1.0 - EMIN) * solid * solid * solid) * live
            moduli.append(modulus)
            if 0 <= layer < layers:
                weight = (3.0 * (1.0 - EMIN)) * solid * solid * dense
                weight_ref[layer, pl.ds(8 + 8 * chunk_at, 8)] = weight
            if 1 <= at < nodes:
                for kind, factor in enumerate(STIFF):
                    stiff_ref[kind, at - 1, chunks[chunk_at]] = modulus * factor
        spread = add(moduli, [last_x(a) for a in moduli])
        spread = add(spread, last_y(spread))
        if at > 0:
            for chunk, mark, low, high in zip(chunks, marks, below, spread):
                free = jnp.logical_and(mark != 1.0, inside(layer))
                diag = jnp.where(free, KE_DIAG * (low + high), 1.0)
                inv_ref[at - 1, chunk] = jnp.where(free, 1.0 / diag, 0.0)
        below = spread

    theta = 0.5 * (UPPER_EIG + LOWER_EIG)
    delta = 0.5 * (UPPER_EIG - LOWER_EIG)
    sigma = theta / delta

    def load_modes(node, chunk):
        return [
            {pq: mode_ref[node, comp * 4 + i, chunk] for i, pq in enumerate(PLANE)}
            for comp in range(3)
        ]

    def store_modes(node, comp, field):
        for i, plane in enumerate(to_modes_xy(field)):
            for chunk, a in zip(chunks, plane):
                mode_ref[node, comp * 4 + i, chunk] = a

    def one_case(case, carry):
        for at in range(nodes):
            for comp in range(3):
                field = []
                for chunk, force in zip(chunks, packed(at - SWEEPS, case, comp)):
                    step = inv_ref[at, chunk] * force * (1.0 / theta)
                    field.append(step)
                    if 1 <= at < nodes - 1:
                        step_ref[comp, at, chunk] = step
                    if SWEEPS <= at <= SWEEPS + layers:
                        sol_ref[comp, at - SWEEPS, chunk] = step
                store_modes(at, comp, field)

        factor = 1.0 / sigma
        for sweep in range(1, SWEEPS + 1):
            factor_next = 1.0 / (2.0 * sigma - factor)
            keep, take = factor_next * factor, 2.0 * factor_next / delta
            first, end = sweep - 1, nodes - sweep
            if sweep > 1:
                for node in range(first, end + 1):
                    for comp in range(3):
                        store_modes(node, comp, [step_ref[comp, node, chunk] for chunk in chunks])
            for chunk in chunks:
                up = {}
                for element in range(first, end):
                    carried, up = up, {}
                    forces = {}

                    def mode(comp, name):
                        at = comp * 4 + PLANE.index(name[:2])
                        low, high = mode_ref[element, at, chunk], mode_ref[element + 1, at, chunk]
                        return high + low if name[2] == "s" else high - low

                    def give(comp, name, force):
                        pq, at = name[:2], comp * 4 + PLANE.index(name[:2])
                        forces[comp, name] = force
                        diff, both = forces.get((comp, pq + "d")), forces.get((comp, pq + "s"))
                        if pq == "ss":
                            up[at] = diff
                            if carried:
                                node_ref[element, at, chunk] = carried[at] - diff
                        elif diff is not None and both is not None:
                            up[at] = both + diff
                            if carried:
                                node_ref[element, at, chunk] = carried[at] + (both - diff)

                    stiff = [stiff_ref[kind, element, chunk] for kind in range(4)]
                    mode_forces(mode, *stiff, give)
            for node in range(first + 1, end):
                for comp in range(3):
                    g = [[node_ref[node, comp * 4 + i, chunk] for chunk in chunks] for i in range(4)]
                    if sweep == 1:
                        before = packed(node - SWEEPS, case, comp)
                    else:
                        before = [res_ref[comp, node, chunk] for chunk in chunks]
                    for chunk, res in zip(chunks, sub(before, from_modes_xy(*g))):
                        step = keep * step_ref[comp, node, chunk] + take * (inv_ref[node, chunk] * res)
                        if sweep < SWEEPS:
                            res_ref[comp, node, chunk] = res
                            step_ref[comp, node, chunk] = step
                        if SWEEPS <= node <= SWEEPS + layers:
                            sol = sol_ref[comp, node - SWEEPS, chunk] + step
                            sol_ref[comp, node - SWEEPS, chunk] = sol
                            if sweep == SWEEPS and node < SWEEPS + layers:
                                disp_ref[case, comp, node - SWEEPS, chunk] = sol
            factor = factor_next
        pltpu.make_async_copy(disp_ref.at[case], disp_hbm.at[case], disp_sem.at[case]).start()

        weight = weights_ref[load * cases + case].astype(jnp.float32)
        for node in range(layers + 1):
            for comp in range(3):
                store_modes(node, comp, [sol_ref[comp, node, chunk] for chunk in chunks])
        for chunk in chunks:
            low = load_modes(0, chunk)
            for layer in range(layers):
                high = load_modes(layer + 1, chunk)
                energy = weight * mode_energy(modes_z(low, high))
                before = jnp.where(case == 0, 0.0, energy_ref[layer, chunk])
                energy_ref[layer, chunk] = before + energy
                low = high
        return carry

    lax.fori_loop(0, cases, one_case, 0)
    weight_sum = weights_ref[0]
    for at in range(1, weights_ref.shape[0]):
        weight_sum = weight_sum + weights_ref[at]
    weight_sum = jnp.full((8, columns), weight_sum.astype(jnp.float32))
    scale = (SHEAR / 48) / weight_sum

    spans = filter_layers(
        [[jnp.where(inside(at), a, 0.0) for a in packed(at, None, 0)] for at in range(-2, layers + 2)]
    )
    recs = [
        [jnp.where(inside(layer), 1.0 / jnp.where(inside(layer), a, 1.0), 0.0) for a in span]
        for layer, span in zip(range(-1, layers + 1), spans)
    ]
    shares = filter_layers(recs)
    total = jnp.zeros((8, columns), jnp.float32)
    own_rows = own_ref.shape[2]
    own = pl.ds(pl.multiple_of(load * own_rows, own_rows), own_rows)
    for layer in range(layers):
        for kind in range(2):
            own_ref[1 + kind, layer] = pack_refs[0][pack_plane(cases, layers, cases, kind, layer), own]
        for at, chunk in enumerate(chunks):
            inner = pl.ds(8 + 8 * at, 8)
            sens = weight_ref[layer, inner] * (energy_ref[layer, chunk] * scale)
            weight_ref[layer, inner] = sens
            total = total + sens * shares[layer][at]
            energy_ref[layer, chunk] = recs[layer + 1][at]
        own_ref[0, layer] = energy_ref[layer, own]
        weight_ref[layer, :8] = jnp.zeros((8, columns), jnp.float32)
        weight_ref[layer, 8 + rows :] = jnp.zeros((8, columns), jnp.float32)
    share = jnp.sum(total, axis=0, keepdims=True)
    wide = own_rows + 2
    for step, slot_ref in enumerate(slot_refs):
        start = pl.multiple_of(partner(load, step) * own_rows, own_rows)
        for layer in range(layers):
            window = weight_ref[layer, pl.ds(start, own_rows + 16)]
            slot_ref[layer * wide : (layer + 1) * wide] = window[7 : 7 + wide]
        slot_ref[layers * wide : layers * wide + 1] = share
    for case in range(cases):
        pltpu.make_async_copy(disp_ref.at[case], disp_hbm.at[case], disp_sem.at[case]).wait()


def pack_plane(cases, layers, group, kind, layer):
    return (group * 3 + kind) * layers + layer


def stage_kernel(labels_ref, forces_ref, pack_ref):
    cases, _, layers, _, _ = forces_ref.shape
    for case in range(cases):
        for comp in range(3):
            for layer in range(layers):
                pack_ref[pack_plane(cases, layers, case, comp, layer)] = forces_ref[case, comp, layer]
    for layer in range(layers):
        marks = labels_ref[layer].astype(jnp.float32)
        pack_ref[pack_plane(cases, layers, cases, 1, layer)] = marks


def design_kernel(cases, steps, *refs):
    density_refs = refs[1 : 1 + len(steps)]
    pack_ref, design_ref = refs[-2:]
    layers, own_rows, _ = density_refs[0].shape
    load = lax.axis_index("load")
    for step, density_ref in zip(steps, density_refs):
        start = pl.multiple_of(partner(load, step) * own_rows, own_rows)
        for layer in range(layers):
            plane = pack_plane(cases, layers, cases, 0, layer)
            pack_ref[plane, pl.ds(start, own_rows)] = density_ref[layer]
    design_ref[...] = pack_ref[cases * 3 * layers :]


def sum_kernel(*refs):
    total = refs[0][...]
    for ref in refs[1:-1]:
        total = total + ref[...]
    refs[-1][...] = total


def forward_kernel(layers, wide, sum_ref, beside_ref, out_ref):
    even = lax.axis_index("gz") % 2 == 0
    end = layers * wide
    out_ref[:wide] = jnp.where(even, beside_ref[end - wide : end], beside_ref[:wide])
    out_ref[wide : wide + 1] = sum_ref[end : end + 1] + beside_ref[end : end + 1]


def share_kernel(wide, mine_ref, *refs):
    out_ref = refs[-1]
    out_ref[...] = mine_ref[...]
    out_ref[wide : wide + 1] = share_sum(wide, mine_ref, *refs[:-1])


def share_sum(wide, *refs):
    total = refs[0][wide : wide + 1]
    for ref in refs[1:]:
        total = total + ref[wide : wide + 1]
    return total


def chip_rounds(count_gz):
    edges = []
    while 2 ** (len(edges) + 1) < count_gz:
        edges.append(2 ** (len(edges) + 1) - 1)
    pairs = [edges[at : at + 2] for at in range(0, len(edges), 2)]
    return [[pair[0], pair[0] ^ pair[1], pair[1]] if len(pair) == 2 else pair for pair in pairs]


def update_kernel(cells, rounds, *refs):
    sum_ref, beside_ref, mine_ref = refs[:3]
    other_refs = refs[3:-2]
    own_ref, new_ref = refs[-2:]
    _, layers, own_rows, columns = own_ref.shape
    wide = own_rows + 2
    gz = lax.axis_index("gz")
    even, chip = gz % 2 == 0, gz // 2
    beside = jnp.where(even, beside_ref[:wide], beside_ref[(layers - 1) * wide : layers * wide])
    across = jnp.zeros((wide, columns), jnp.float32)
    for mask, other_ref in zip(sum(rounds, []), other_refs):
        borders = (chip ^ mask) == jnp.where(even, chip - 1, chip + 1)
        across = jnp.where(borders, other_ref[:wide], across)
    numers = [jnp.where(even, across, beside)]
    numers += [sum_ref[layer * wide : (layer + 1) * wide] for layer in range(layers)]
    numers += [jnp.where(even, beside, across)]
    near, far = [], []
    for numer in numers:
        back, mid, front = (numer[at : at + own_rows] for at in range(3))
        sides = back + front
        cross = sides + (last_x(mid) + next_x(mid))
        near.append(1.5 * mid + 0.5 * cross + EDGE * (last_x(sides) + next_x(sides)))
        far.append(0.5 * mid + EDGE * cross)
    total = share_sum(wide, mine_ref, *other_refs[-len(rounds[-1]) :])
    mean = jnp.sum(total, keepdims=True) * (1.0 / cells)
    mean = jnp.broadcast_to(mean, (own_rows, columns))
    for layer in range(layers):
        numer = near[layer + 1] + (far[layer] + far[layer + 2])
        filtered = numer * own_ref[0, layer]
        density = own_ref[1, layer]
        candidate = density * jnp.sqrt(filtered / mean)
        lower = jnp.maximum(density - MOVE_LIMIT, FLOOR_DENSITY)
        upper = jnp.minimum(density + MOVE_LIMIT, 1.0)
        updated = jnp.minimum(jnp.maximum(candidate, lower), upper)
        new_ref[layer] = jnp.where(own_ref[2, layer] == 2.0, 1.0, updated)


def met(block, axis, step):
    count = lax.axis_size(axis)
    return lax.ppermute(block, axis, [(partner(i, step), i) for i in range(count)])


def far_pairs(far, count, across):
    pairs = [(i - far if (i % 2 == 0) == across else i + far, i) for i in range(count)]
    pairs = [(source, i) for source, i in pairs if 0 <= source < count]
    free = [i for i in range(count) if i not in dict(pairs)]
    empty = [i for i in range(count) if i not in dict(pairs).values()]
    return pairs + list(zip(free, empty))


def on_device(density, labels, forces, case_weights):
    count_gz, count_load = lax.axis_size("gz"), lax.axis_size("load")
    cases, _, layers, rows, columns = forces.shape
    own_rows = density.shape[1]
    nodes = layers + 2 * SWEEPS + 1
    hops = -(-(SWEEPS + 1) // layers)
    wide = own_rows + 2
    f32 = jnp.float32
    plane = (rows, columns)
    plane_bytes = rows * columns * 4
    vmem = pl.BlockSpec(memory_space=pltpu.VMEM)
    smem = pl.BlockSpec(memory_space=pltpu.SMEM)

    def shape(*dims):
        return jax.ShapeDtypeStruct(dims, f32)

    def call(kernel, out, args, planes, flops, in_specs=None, scratch=(), **more):
        limit = planes * plane_bytes + (2 << 20)
        return pl.pallas_call(
            kernel,
            out_shape=out,
            in_specs=in_specs or [vmem] * len(args),
            out_specs=more.pop("out_specs", vmem),
            scratch_shapes=scratch,
            compiler_params=pltpu.CompilerParams(vmem_limit_bytes=limit),
            cost_estimate=pl.CostEstimate(flops=flops, bytes_accessed=flops // 10, transcendentals=0),
            **more,
        )(*args)

    planes = (cases * 3 + 2) * layers
    far_forces = [
        lax.ppermute(forces, "gz", far_pairs(far, count_gz, True)) for far in range(1, hops + 1)
    ]
    pack = call(stage_kernel, shape(planes, rows, columns), (labels, forces), 2 * planes, 1_000_000)
    steps = [0] + list(range(2, count_load)) + [1]
    densities = [density] + [met(density, "load", step) for step in steps[1:]]
    pack, design = call(
        functools.partial(design_kernel, cases, steps),
        (shape(planes, rows, columns), shape(2 * layers, rows, columns)),
        (pack, *densities, *far_forces),
        2 * planes + 6 * layers,
        100_000,
        in_specs=[vmem] * (1 + count_load) + [pl.BlockSpec(memory_space=pl.ANY)] * hops,
        out_specs=(vmem, vmem),
        input_output_aliases={0: 0},
    )
    packs = [pack, met(pack, "gz", 1)]
    for far, forces_far in enumerate(far_forces, 1):
        if far > 1:
            packs.append(lax.ppermute(design, "gz", far_pairs(far, count_gz, False)))
            packs.append(met(far_forces[far - 2], "gz", 1))
        packs += [lax.ppermute(design, "gz", far_pairs(far, count_gz, True)), forces_far]

    slot_rows = -(-(layers * wide + 1) // 8) * 8
    scratch = [
        pltpu.VMEM((4, nodes - 1) + plane, f32),
        pltpu.VMEM((nodes,) + plane, f32),
        pltpu.VMEM((3, nodes) + plane, f32),
        pltpu.VMEM((3, nodes) + plane, f32),
        pltpu.VMEM((3, layers + 1) + plane, f32),
        pltpu.VMEM((nodes, 12) + plane, f32),
        pltpu.VMEM((nodes, 12) + plane, f32),
        pltpu.VMEM(forces.shape, f32),
        pltpu.VMEM((layers, rows + 16, columns), f32),
        pltpu.VMEM((layers,) + plane, f32),
        pltpu.SemaphoreType.DMA((cases,)),
    ]
    smooth_planes = nodes * 35 + 3 * (layers + 1) + 4 * layers
    smooth_planes += (1 + 2 * hops) * planes + cases * 3 * layers + 8 * layers
    displacement, own, *slots = call(
        functools.partial(smooth_kernel, hops, count_gz),
        (shape(*forces.shape), shape(3, layers, own_rows, columns))
        + (shape(slot_rows, columns),) * count_load,
        (case_weights, *packs),
        smooth_planes,
        60_000_000,
        in_specs=[smem] + [vmem] * len(packs),
        out_specs=(pl.BlockSpec(memory_space=pltpu.HBM),) + (vmem,) * (1 + count_load),
        scratch=scratch,
    )

    received = [met(slots[step], "load", step) for step in range(count_load - 1, 0, -1)]
    whole = call(sum_kernel, shape(slot_rows, columns), (slots[0], *received), 2 * count_load, 100_000)
    beside = met(whole, "gz", 1)
    forward_rows = -(-(wide + 1) // 8) * 8
    mine = call(
        functools.partial(forward_kernel, layers, wide),
        shape(forward_rows, columns),
        (whole, beside),
        4 * layers,
        10_000,
    )
    others = []
    rounds = chip_rounds(count_gz)
    for at, masks in enumerate(rounds):
        if at > 0:
            mine = call(
                functools.partial(share_kernel, wide),
                shape(forward_rows, columns),
                (mine, *others[-len(rounds[at - 1]) :]),
                8,
                10_000,
            )
        others += [met(mine, "gz", 2 * mask) for mask in masks]
    new_density = call(
        functools.partial(update_kernel, float(count_gz * layers * rows * columns), rounds),
        shape(*density.shape),
        (whole, beside, mine, *others, own),
        8 * layers,
        100_000,
    )
    return (new_density, displacement)


def solution(mesh):
    return jax.shard_map(
        on_device,
        mesh=mesh,
        in_specs=(
            P("gz", "load", None),
            P("gz", None, None),
            P("load", None, "gz", None, None),
            P(),
        ),
        out_specs=(P("gz", "load", None), P("load", None, "gz", None, None)),
        check_vma=False,
    )
```

```python
import functools

import jax
import jax.numpy as jnp
from jax import lax
from jax.experimental import pallas as pl
from jax.experimental.pallas import tpu as pltpu
from jax.sharding import PartitionSpec as P

SWEEPS = 3
EMIN = 0.001
LOWER_EIG = 0.1
UPPER_EIG = 2.5
MOVE_LIMIT = 0.2
FLOOR_DENSITY = 0.001
POISSON = 0.3
LAME = POISSON / ((1 + POISSON) * (1 - 2 * POISSON))
SHEAR = 1.0 / (2 * (1 + POISSON))
KE_DIAG = (LAME + 4 * SHEAR) / 9
EDGE = 1.5 - 2.0**0.5
PLANE = ("ss", "sd", "ds", "dd")


def chunks_of(rows):
    return [pl.ds(at, 8) for at in range(0, rows, 8)]


def next_x(a):
    lanes = a.shape[1]
    lane = lax.broadcasted_iota(jnp.int32, a.shape, 1)
    return jnp.where(lane == lanes - 1, 0.0, pltpu.roll(a, lanes - 1, 1))


def last_x(a):
    lane = lax.broadcasted_iota(jnp.int32, a.shape, 1)
    return jnp.where(lane == 0, 0.0, pltpu.roll(a, 1, 1))


def next_y(plane):
    row = lax.broadcasted_iota(jnp.int32, plane[0].shape, 0)
    rolled = [pltpu.roll(a, 7, 0) for a in plane] + [jnp.zeros_like(plane[0])]
    return [jnp.where(row == 7, rolled[at + 1], rolled[at]) for at in range(len(plane))]


def last_y(plane):
    row = lax.broadcasted_iota(jnp.int32, plane[0].shape, 0)
    rolled = [jnp.zeros_like(plane[0])] + [pltpu.roll(a, 1, 0) for a in plane]
    return [jnp.where(row == 0, rolled[at], rolled[at + 1]) for at in range(len(plane))]


def add(*planes):
    return [sum(chunks[1:], chunks[0]) for chunks in zip(*planes)]


def sub(one, other):
    return [a - b for a, b in zip(one, other)]


def to_modes_xy(u):
    ux = [next_x(a) for a in u]
    s, d = add(ux, u), sub(ux, u)
    sy, dy = next_y(s), next_y(d)
    return add(sy, s), sub(sy, s), add(dy, d), sub(dy, d)


def from_modes_xy(ss, sd, ds, dd):
    s = add(sub(ss, sd), last_y(add(ss, sd)))
    d = add(sub(ds, dd), last_y(add(ds, dd)))
    return add(sub(s, d), [last_x(a) for a in add(s, d)])


def modes_z(low, high):
    modes = []
    for comp in range(3):
        one = {}
        for pq in PLANE:
            if pq != "ss":
                one[pq + "s"] = high[comp][pq] + low[comp][pq]
            one[pq + "d"] = high[comp][pq] - low[comp][pq]
        modes.append(one)
    return modes


NORMAL = ((0, "dss"), (1, "sds"), (2, "ssd"))
BENDS = (((1, "dds"), (2, "dsd")), ((0, "dds"), (2, "sdd")), ((0, "dsd"), (1, "sdd")))
SHEARS = (((0, "sds"), (1, "dss")), ((0, "ssd"), (2, "dss")), ((1, "ssd"), (2, "sds")))
STIFF = (SHEAR / 16, SHEAR / 48, (LAME + 4 * SHEAR) / 144, SHEAR / 8)
TWIST = ((0, "sdd"), (1, "dsd"), (2, "dds"))


def mode_forces(modes, e1, e2, e3, e4):
    m = lambda key: modes[key[0]][key[1]]
    out = [{}, {}, {}]

    def put(key, value):
        out[key[0]][key[1]] = value

    trace = (LAME / (2 * SHEAR)) * (m(NORMAL[0]) + m(NORMAL[1]) + m(NORMAL[2]))
    for key in NORMAL:
        put(key, e4 * (trace + m(key)))
    for a, b in BENDS:
        t = (LAME / (3 * SHEAR)) * (m(a) + m(b))
        put(a, e1 * (t + m(a)))
        put(b, e1 * (t + m(b)))
    for a, b in SHEARS:
        f = e1 * (m(a) + m(b))
        put(a, f)
        put(b, f)
    t = m(TWIST[0]) + m(TWIST[1]) + m(TWIST[2])
    for key in TWIST:
        put(key, e2 * (t + m(key)))
    for comp in range(3):
        put((comp, "ddd"), e3 * modes[comp]["ddd"])
    return out


def mode_energy(modes):
    m = lambda key: modes[key[0]][key[1]]
    sq = lambda v: v * v
    n = [m(key) for key in NORMAL]
    total = (3 * LAME / SHEAR) * sq(n[0] + n[1] + n[2]) + 6.0 * (sq(n[0]) + sq(n[1]) + sq(n[2]))
    shear = None
    for a, b in SHEARS:
        t = sq(m(a) + m(b))
        shear = t if shear is None else shear + t
    total = total + 3.0 * shear
    sums, own = None, None
    for a, b in BENDS:
        t = sq(m(a) + m(b))
        o = sq(m(a)) + sq(m(b))
        sums = t if sums is None else sums + t
        own = o if own is None else own + o
    total = total + (LAME / SHEAR) * sums + 3.0 * own
    a, b, c = (m(key) for key in TWIST)
    total = total + (sq(a + b) + sq(a + c) + sq(b + c))
    bulk = sq(modes[0]["ddd"]) + sq(modes[1]["ddd"]) + sq(modes[2]["ddd"])
    return total + ((LAME + 4 * SHEAR) / (3 * SHEAR)) * bulk


def filter_planes(plane):
    x = [last_x(a) + next_x(a) for a in plane]
    cross = add(x, add(last_y(plane), next_y(plane)))
    diagonal = add(last_y(x), next_y(x))
    near = [1.5 * a + 0.5 * c + EDGE * d for a, c, d in zip(plane, cross, diagonal)]
    return near, [0.5 * a + EDGE * c for a, c in zip(plane, cross)]


def filter_layers(layers):
    pairs = [filter_planes(plane) for plane in layers]
    return [
        add(pairs[at][0], add(pairs[at - 1][1], pairs[at + 1][1])) for at in range(1, len(layers) - 1)
    ]


def partner(index, step):
    return index ^ step


def smooth_kernel(hops, count_gz, *refs):
    blocks = 4 * hops
    weights_ref = refs[0]
    pack_refs = refs[1 : 1 + blocks]
    disp_hbm, own_ref = refs[1 + blocks : 3 + blocks]
    slot_refs = refs[3 + blocks : -11]
    stiff_ref, inv_ref, res_ref, step_ref, sol_ref, mode_ref, node_ref = refs[-11:-4]
    disp_ref, weight_ref, energy_ref, disp_sem = refs[-4:]

    cases, _, layers, rows, columns = disp_ref.shape
    nodes = layers + 2 * SWEEPS + 1
    chunks = chunks_of(rows)
    gz = lax.axis_index("gz")
    load = lax.axis_index("load")
    even = gz % 2 == 0

    def packed(layer, group, kind):
        hop = layer // layers
        inner = layer - hop * layers
        plane = pack_plane(cases, layers, cases if group is None else group, kind, inner)
        if hop == 0:
            return [pack_refs[0][plane, chunk] for chunk in chunks]

        def pick(design_ref, force_ref):
            if group is None:
                return [design_ref[kind * layers + inner, chunk] for chunk in chunks]
            return [force_ref[group, kind, inner, chunk] for chunk in chunks]

        at = 4 * abs(hop) - 2
        across = pick(*pack_refs[at : at + 2])
        if abs(hop) == 1:
            beside = [pack_refs[1][plane, chunk] for chunk in chunks]
        else:
            beside = pick(*pack_refs[at - 2 : at])
        by_sibling = even == (hop > 0)
        return [jnp.where(by_sibling, one, other) for one, other in zip(beside, across)]

    def inside(layer):
        owner = gz + layer // layers
        return jnp.logical_and(owner >= 0, owner < count_gz)

    below = None
    for at in range(nodes + 1):
        layer = at - SWEEPS - 1
        live = jnp.where(inside(layer), 1.0, 0.0)
        marks = packed(layer, None, 1)
        moduli = []
        for chunk_at, (dense, mark) in enumerate(zip(packed(layer, None, 0), marks)):
            solid = jnp.where(mark == 2.0, 1.0, dense)
            modulus = (EMIN + (1.0 - EMIN) * solid * solid * solid) * live
            moduli.append(modulus)
            if 0 <= layer < layers:
                weight = (3.0 * (1.0 - EMIN)) * solid * solid * dense
                weight_ref[layer, pl.ds(8 + 8 * chunk_at, 8)] = weight
            if 1 <= at < nodes:
                for kind, factor in enumerate(STIFF):
                    stiff_ref[kind, at - 1, chunks[chunk_at]] = modulus * factor
        spread = add(moduli, [last_x(a) for a in moduli])
        spread = add(spread, last_y(spread))
        if at > 0:
            for chunk, mark, low, high in zip(chunks, marks, below, spread):
                free = jnp.logical_and(mark != 1.0, inside(layer))
                diag = jnp.where(free, KE_DIAG * (low + high), 1.0)
                inv_ref[at - 1, chunk] = jnp.where(free, 1.0 / diag, 0.0)
        below = spread

    theta = 0.5 * (UPPER_EIG + LOWER_EIG)
    delta = 0.5 * (UPPER_EIG - LOWER_EIG)
    sigma = theta / delta

    def load_modes(node, chunk):
        return [
            {pq: mode_ref[node, comp * 4 + i, chunk] for i, pq in enumerate(PLANE)}
            for comp in range(3)
        ]

    def store_modes(node, comp, field):
        for i, plane in enumerate(to_modes_xy(field)):
            for chunk, a in zip(chunks, plane):
                mode_ref[node, comp * 4 + i, chunk] = a

    def one_case(case, carry):
        for at in range(nodes):
            for comp in range(3):
                field = []
                for chunk, force in zip(chunks, packed(at - SWEEPS, case, comp)):
                    step = inv_ref[at, chunk] * force * (1.0 / theta)
                    field.append(step)
                    if 1 <= at < nodes - 1:
                        step_ref[comp, at, chunk] = step
                    if SWEEPS <= at <= SWEEPS + layers:
                        sol_ref[comp, at - SWEEPS, chunk] = step
                store_modes(at, comp, field)

        factor = 1.0 / sigma
        for sweep in range(1, SWEEPS + 1):
            factor_next = 1.0 / (2.0 * sigma - factor)
            keep, take = factor_next * factor, 2.0 * factor_next / delta
            first, end = sweep - 1, nodes - sweep
            if sweep > 1:
                for node in range(first, end + 1):
                    for comp in range(3):
                        store_modes(node, comp, [step_ref[comp, node, chunk] for chunk in chunks])
            def column(at, carry, first=first, end=end):
                chunk = pl.ds(pl.multiple_of(at * 8, 8), 8)
                low = load_modes(first, chunk)
                up = None
                for element in range(first, end):
                    high = load_modes(element + 1, chunk)
                    stiff = [stiff_ref[kind, element, chunk] for kind in range(4)]
                    f = mode_forces(modes_z(low, high), *stiff)
                    ups = []
                    for comp in range(3):
                        for i, pq in enumerate(PLANE):
                            diff = f[comp][pq + "d"]
                            where = comp * 4 + i
                            if pq == "ss":
                                ups.append(diff)
                                if up:
                                    node_ref[element, where, chunk] = up[where] - diff
                            else:
                                both = f[comp][pq + "s"]
                                ups.append(both + diff)
                                if up:
                                    node_ref[element, where, chunk] = up[where] + (both - diff)
                    low, up = high, ups
                return carry

            lax.fori_loop(0, len(chunks), column, 0)
            for node in range(first + 1, end):
                for comp in range(3):
                    g = [[node_ref[node, comp * 4 + i, chunk] for chunk in chunks] for i in range(4)]
                    if sweep == 1:
                        before = packed(node - SWEEPS, case, comp)
                    else:
                        before = [res_ref[comp, node, chunk] for chunk in chunks]
                    for chunk, res in zip(chunks, sub(before, from_modes_xy(*g))):
                        step = keep * step_ref[comp, node, chunk] + take * (inv_ref[node, chunk] * res)
                        if sweep < SWEEPS:
                            res_ref[comp, node, chunk] = res
                            step_ref[comp, node, chunk] = step
                        if SWEEPS <= node <= SWEEPS + layers:
                            sol = sol_ref[comp, node - SWEEPS, chunk] + step
                            sol_ref[comp, node - SWEEPS, chunk] = sol
                            if sweep == SWEEPS and node < SWEEPS + layers:
                                disp_ref[case, comp, node - SWEEPS, chunk] = sol
            factor = factor_next
        pltpu.make_async_copy(disp_ref.at[case], disp_hbm.at[case], disp_sem.at[case]).start()

        weight = weights_ref[load * cases + case].astype(jnp.float32)
        for node in range(layers + 1):
            for comp in range(3):
                store_modes(node, comp, [sol_ref[comp, node, chunk] for chunk in chunks])
        for chunk in chunks:
            low = load_modes(0, chunk)
            for layer in range(layers):
                high = load_modes(layer + 1, chunk)
                energy = weight * mode_energy(modes_z(low, high))
                before = jnp.where(case == 0, 0.0, energy_ref[layer, chunk])
                energy_ref[layer, chunk] = before + energy
                low = high
        return carry

    lax.fori_loop(0, cases, one_case, 0)
    weight_sum = weights_ref[0]
    for at in range(1, weights_ref.shape[0]):
        weight_sum = weight_sum + weights_ref[at]
    weight_sum = jnp.full((8, columns), weight_sum.astype(jnp.float32))
    scale = (SHEAR / 48) / weight_sum

    spans = filter_layers(
        [[jnp.where(inside(at), a, 0.0) for a in packed(at, None, 0)] for at in range(-2, layers + 2)]
    )
    recs = [
        [jnp.where(inside(layer), 1.0 / jnp.where(inside(layer), a, 1.0), 0.0) for a in span]
        for layer, span in zip(range(-1, layers + 1), spans)
    ]
    shares = filter_layers(recs)
    total = jnp.zeros((8, columns), jnp.float32)
    own_rows = own_ref.shape[2]
    own = pl.ds(pl.multiple_of(load * own_rows, own_rows), own_rows)
    for layer in range(layers):
        for kind in range(2):
            own_ref[1 + kind, layer] = pack_refs[0][pack_plane(cases, layers, cases, kind, layer), own]
        for at, chunk in enumerate(chunks):
            inner = pl.ds(8 + 8 * at, 8)
            sens = weight_ref[layer, inner] * (energy_ref[layer, chunk] * scale)
            weight_ref[layer, inner] = sens
            total = total + sens * shares[layer][at]
            energy_ref[layer, chunk] = recs[layer + 1][at]
        own_ref[0, layer] = energy_ref[layer, own]
        weight_ref[layer, :8] = jnp.zeros((8, columns), jnp.float32)
        weight_ref[layer, 8 + rows :] = jnp.zeros((8, columns), jnp.float32)
    share = jnp.sum(total, axis=0, keepdims=True)
    wide = own_rows + 2
    for step, slot_ref in enumerate(slot_refs):
        start = pl.multiple_of(partner(load, step) * own_rows, own_rows)
        for layer in range(layers):
            window = weight_ref[layer, pl.ds(start, own_rows + 16)]
            slot_ref[layer * wide : (layer + 1) * wide] = window[7 : 7 + wide]
        slot_ref[layers * wide : layers * wide + 1] = share
    for case in range(cases):
        pltpu.make_async_copy(disp_ref.at[case], disp_hbm.at[case], disp_sem.at[case]).wait()


def pack_plane(cases, layers, group, kind, layer):
    return (group * 3 + kind) * layers + layer


def stage_kernel(labels_ref, forces_ref, pack_ref):
    cases, _, layers, _, _ = forces_ref.shape
    for case in range(cases):
        for comp in range(3):
            for layer in range(layers):
                pack_ref[pack_plane(cases, layers, case, comp, layer)] = forces_ref[case, comp, layer]
    for layer in range(layers):
        marks = labels_ref[layer].astype(jnp.float32)
        pack_ref[pack_plane(cases, layers, cases, 1, layer)] = marks


def design_kernel(cases, steps, *refs):
    density_refs = refs[1 : 1 + len(steps)]
    pack_ref, design_ref = refs[-2:]
    layers, own_rows, _ = density_refs[0].shape
    load = lax.axis_index("load")
    for step, density_ref in zip(steps, density_refs):
        start = pl.multiple_of(partner(load, step) * own_rows, own_rows)
        for layer in range(layers):
            plane = pack_plane(cases, layers, cases, 0, layer)
            pack_ref[plane, pl.ds(start, own_rows)] = density_ref[layer]
    design_ref[...] = pack_ref[cases * 3 * layers :]


def sum_kernel(*refs):
    total = refs[0][...]
    for ref in refs[1:-1]:
        total = total + ref[...]
    refs[-1][...] = total


def forward_kernel(layers, wide, sum_ref, beside_ref, out_ref):
    even = lax.axis_index("gz") % 2 == 0
    end = layers * wide
    out_ref[:wide] = jnp.where(even, beside_ref[end - wide : end], beside_ref[:wide])
    out_ref[wide : wide + 1] = sum_ref[end : end + 1] + beside_ref[end : end + 1]


def share_kernel(wide, mine_ref, *refs):
    out_ref = refs[-1]
    out_ref[...] = mine_ref[...]
    out_ref[wide : wide + 1] = share_sum(wide, mine_ref, *refs[:-1])


def share_sum(wide, *refs):
    total = refs[0][wide : wide + 1]
    for ref in refs[1:]:
        total = total + ref[wide : wide + 1]
    return total


def chip_rounds(count_gz):
    edges = []
    while 2 ** (len(edges) + 1) < count_gz:
        edges.append(2 ** (len(edges) + 1) - 1)
    pairs = [edges[at : at + 2] for at in range(0, len(edges), 2)]
    return [[pair[0], pair[0] ^ pair[1], pair[1]] if len(pair) == 2 else pair for pair in pairs]


def update_kernel(cells, rounds, *refs):
    sum_ref, beside_ref, mine_ref = refs[:3]
    other_refs = refs[3:-2]
    own_ref, new_ref = refs[-2:]
    _, layers, own_rows, columns = own_ref.shape
    wide = own_rows + 2
    gz = lax.axis_index("gz")
    even, chip = gz % 2 == 0, gz // 2
    beside = jnp.where(even, beside_ref[:wide], beside_ref[(layers - 1) * wide : layers * wide])
    across = jnp.zeros((wide, columns), jnp.float32)
    for mask, other_ref in zip(sum(rounds, []), other_refs):
        borders = (chip ^ mask) == jnp.where(even, chip - 1, chip + 1)
        across = jnp.where(borders, other_ref[:wide], across)
    numers = [jnp.where(even, across, beside)]
    numers += [sum_ref[layer * wide : (layer + 1) * wide] for layer in range(layers)]
    numers += [jnp.where(even, beside, across)]
    near, far = [], []
    for numer in numers:
        back, mid, front = (numer[at : at + own_rows] for at in range(3))
        sides = back + front
        cross = sides + (last_x(mid) + next_x(mid))
        near.append(1.5 * mid + 0.5 * cross + EDGE * (last_x(sides) + next_x(sides)))
        far.append(0.5 * mid + EDGE * cross)
    total = share_sum(wide, mine_ref, *other_refs[-len(rounds[-1]) :])
    mean = jnp.sum(total, keepdims=True) * (1.0 / cells)
    mean = jnp.broadcast_to(mean, (own_rows, columns))
    for layer in range(layers):
        numer = near[layer + 1] + (far[layer] + far[layer + 2])
        filtered = numer * own_ref[0, layer]
        density = own_ref[1, layer]
        candidate = density * jnp.sqrt(filtered / mean)
        lower = jnp.maximum(density - MOVE_LIMIT, FLOOR_DENSITY)
        upper = jnp.minimum(density + MOVE_LIMIT, 1.0)
        updated = jnp.minimum(jnp.maximum(candidate, lower), upper)
        new_ref[layer] = jnp.where(own_ref[2, layer] == 2.0, 1.0, updated)


def met(block, axis, step):
    count = lax.axis_size(axis)
    return lax.ppermute(block, axis, [(partner(i, step), i) for i in range(count)])


def far_pairs(far, count, across):
    pairs = [(i - far if (i % 2 == 0) == across else i + far, i) for i in range(count)]
    pairs = [(source, i) for source, i in pairs if 0 <= source < count]
    free = [i for i in range(count) if i not in dict(pairs)]
    empty = [i for i in range(count) if i not in dict(pairs).values()]
    return pairs + list(zip(free, empty))


def on_device(density, labels, forces, case_weights):
    count_gz, count_load = lax.axis_size("gz"), lax.axis_size("load")
    cases, _, layers, rows, columns = forces.shape
    own_rows = density.shape[1]
    nodes = layers + 2 * SWEEPS + 1
    hops = -(-(SWEEPS + 1) // layers)
    wide = own_rows + 2
    f32 = jnp.float32
    plane = (rows, columns)
    plane_bytes = rows * columns * 4
    vmem = pl.BlockSpec(memory_space=pltpu.VMEM)
    smem = pl.BlockSpec(memory_space=pltpu.SMEM)

    def shape(*dims):
        return jax.ShapeDtypeStruct(dims, f32)

    def call(kernel, out, args, planes, flops, in_specs=None, scratch=(), **more):
        limit = planes * plane_bytes + (2 << 20)
        return pl.pallas_call(
            kernel,
            out_shape=out,
            in_specs=in_specs or [vmem] * len(args),
            out_specs=more.pop("out_specs", vmem),
            scratch_shapes=scratch,
            compiler_params=pltpu.CompilerParams(vmem_limit_bytes=limit),
            cost_estimate=pl.CostEstimate(flops=flops, bytes_accessed=flops // 10, transcendentals=0),
            **more,
        )(*args)

    planes = (cases * 3 + 2) * layers
    far_forces = [
        lax.ppermute(forces, "gz", far_pairs(far, count_gz, True)) for far in range(1, hops + 1)
    ]
    pack = call(stage_kernel, shape(planes, rows, columns), (labels, forces), 2 * planes, 1_000_000)
    steps = [0] + list(range(2, count_load)) + [1]
    densities = [density] + [met(density, "load", step) for step in steps[1:]]
    pack, design = call(
        functools.partial(design_kernel, cases, steps),
        (shape(planes, rows, columns), shape(2 * layers, rows, columns)),
        (pack, *densities, *far_forces),
        2 * planes + 6 * layers,
        100_000,
        in_specs=[vmem] * (1 + count_load) + [pl.BlockSpec(memory_space=pl.ANY)] * hops,
        out_specs=(vmem, vmem),
        input_output_aliases={0: 0},
    )
    packs = [pack, met(pack, "gz", 1)]
    for far, forces_far in enumerate(far_forces, 1):
        if far > 1:
            packs.append(lax.ppermute(design, "gz", far_pairs(far, count_gz, False)))
            packs.append(met(far_forces[far - 2], "gz", 1))
        packs += [lax.ppermute(design, "gz", far_pairs(far, count_gz, True)), forces_far]

    slot_rows = -(-(layers * wide + 1) // 8) * 8
    scratch = [
        pltpu.VMEM((4, nodes - 1) + plane, f32),
        pltpu.VMEM((nodes,) + plane, f32),
        pltpu.VMEM((3, nodes) + plane, f32),
        pltpu.VMEM((3, nodes) + plane, f32),
        pltpu.VMEM((3, layers + 1) + plane, f32),
        pltpu.VMEM((nodes, 12) + plane, f32),
        pltpu.VMEM((nodes, 12) + plane, f32),
        pltpu.VMEM(forces.shape, f32),
        pltpu.VMEM((layers, rows + 16, columns), f32),
        pltpu.VMEM((layers,) + plane, f32),
        pltpu.SemaphoreType.DMA((cases,)),
    ]
    smooth_planes = nodes * 35 + 3 * (layers + 1) + 4 * layers
    smooth_planes += (1 + 2 * hops) * planes + cases * 3 * layers + 8 * layers
    displacement, own, *slots = call(
        functools.partial(smooth_kernel, hops, count_gz),
        (shape(*forces.shape), shape(3, layers, own_rows, columns))
        + (shape(slot_rows, columns),) * count_load,
        (case_weights, *packs),
        smooth_planes,
        60_000_000,
        in_specs=[smem] + [vmem] * len(packs),
        out_specs=(pl.BlockSpec(memory_space=pltpu.HBM),) + (vmem,) * (1 + count_load),
        scratch=scratch,
    )

    received = [met(slots[step], "load", step) for step in range(count_load - 1, 0, -1)]
    whole = call(sum_kernel, shape(slot_rows, columns), (slots[0], *received), 2 * count_load, 100_000)
    beside = met(whole, "gz", 1)
    forward_rows = -(-(wide + 1) // 8) * 8
    mine = call(
        functools.partial(forward_kernel, layers, wide),
        shape(forward_rows, columns),
        (whole, beside),
        4 * layers,
        10_000,
    )
    others = []
    rounds = chip_rounds(count_gz)
    for at, masks in enumerate(rounds):
        if at > 0:
            mine = call(
                functools.partial(share_kernel, wide),
                shape(forward_rows, columns),
                (mine, *others[-len(rounds[at - 1]) :]),
                8,
                10_000,
            )
        others += [met(mine, "gz", 2 * mask) for mask in masks]
    new_density = call(
        functools.partial(update_kernel, float(count_gz * layers * rows * columns), rounds),
        shape(*density.shape),
        (whole, beside, mine, *others, own),
        8 * layers,
        100_000,
    )
    return (new_density, displacement)


def solution(mesh):
    return jax.shard_map(
        on_device,
        mesh=mesh,
        in_specs=(
            P("gz", "load", None),
            P("gz", None, None),
            P("load", None, "gz", None, None),
            P(),
        ),
        out_specs=(P("gz", "load", None), P("load", None, "gz", None, None)),
        check_vma=False,
    )
```

```python
import functools

import jax
import jax.numpy as jnp
from jax import lax
from jax.experimental import pallas as pl
from jax.experimental.pallas import tpu as pltpu
from jax.sharding import PartitionSpec as P

SWEEPS = 3
EMIN = 0.001
LOWER_EIG = 0.1
UPPER_EIG = 2.5
MOVE_LIMIT = 0.2
FLOOR_DENSITY = 0.001
POISSON = 0.3
LAME = POISSON / ((1 + POISSON) * (1 - 2 * POISSON))
SHEAR = 1.0 / (2 * (1 + POISSON))
KE_DIAG = (LAME + 4 * SHEAR) / 9
EDGE = 1.5 - 2.0**0.5
PLANE = ("ss", "sd", "ds", "dd")


def chunks_of(rows):
    return [pl.ds(at, 8) for at in range(0, rows, 8)]


def next_x(a):
    lanes = a.shape[1]
    lane = lax.broadcasted_iota(jnp.int32, a.shape, 1)
    return jnp.where(lane == lanes - 1, 0.0, pltpu.roll(a, lanes - 1, 1))


def last_x(a):
    lane = lax.broadcasted_iota(jnp.int32, a.shape, 1)
    return jnp.where(lane == 0, 0.0, pltpu.roll(a, 1, 1))


def next_y(plane):
    row = lax.broadcasted_iota(jnp.int32, plane[0].shape, 0)
    rolled = [pltpu.roll(a, 7, 0) for a in plane] + [jnp.zeros_like(plane[0])]
    return [jnp.where(row == 7, rolled[at + 1], rolled[at]) for at in range(len(plane))]


def last_y(plane):
    row = lax.broadcasted_iota(jnp.int32, plane[0].shape, 0)
    rolled = [jnp.zeros_like(plane[0])] + [pltpu.roll(a, 1, 0) for a in plane]
    return [jnp.where(row == 0, rolled[at], rolled[at + 1]) for at in range(len(plane))]


def add(*planes):
    return [sum(chunks[1:], chunks[0]) for chunks in zip(*planes)]


def sub(one, other):
    return [a - b for a, b in zip(one, other)]


def to_modes_xy(u):
    ux = [next_x(a) for a in u]
    s, d = add(ux, u), sub(ux, u)
    sy, dy = next_y(s), next_y(d)
    return add(sy, s), sub(sy, s), add(dy, d), sub(dy, d)


def from_modes_xy(ss, sd, ds, dd):
    s = add(sub(ss, sd), last_y(add(ss, sd)))
    d = add(sub(ds, dd), last_y(add(ds, dd)))
    return add(sub(s, d), [last_x(a) for a in add(s, d)])


def modes_z(low, high):
    modes = []
    for comp in range(3):
        one = {}
        for pq in PLANE:
            if pq != "ss":
                one[pq + "s"] = high[comp][pq] + low[comp][pq]
            one[pq + "d"] = high[comp][pq] - low[comp][pq]
        modes.append(one)
    return modes


NORMAL = ((0, "dss"), (1, "sds"), (2, "ssd"))
BENDS = (((1, "dds"), (2, "dsd")), ((0, "dds"), (2, "sdd")), ((0, "dsd"), (1, "sdd")))
SHEARS = (((0, "sds"), (1, "dss")), ((0, "ssd"), (2, "dss")), ((1, "ssd"), (2, "sds")))
STIFF = (SHEAR / 16, SHEAR / 48, (LAME + 4 * SHEAR) / 144, SHEAR / 8)
TWIST = ((0, "sdd"), (1, "dsd"), (2, "dds"))


def mode_forces(modes, e1, e2, e3, e4):
    m = lambda key: modes[key[0]][key[1]]
    out = [{}, {}, {}]

    def put(key, value):
        out[key[0]][key[1]] = value

    trace = (LAME / (2 * SHEAR)) * (m(NORMAL[0]) + m(NORMAL[1]) + m(NORMAL[2]))
    for key in NORMAL:
        put(key, e4 * (trace + m(key)))
    for a, b in BENDS:
        t = (LAME / (3 * SHEAR)) * (m(a) + m(b))
        put(a, e1 * (t + m(a)))
        put(b, e1 * (t + m(b)))
    for a, b in SHEARS:
        f = e1 * (m(a) + m(b))
        put(a, f)
        put(b, f)
    t = m(TWIST[0]) + m(TWIST[1]) + m(TWIST[2])
    for key in TWIST:
        put(key, e2 * (t + m(key)))
    for comp in range(3):
        put((comp, "ddd"), e3 * modes[comp]["ddd"])
    return out


def mode_energy(modes):
    m = lambda key: modes[key[0]][key[1]]
    sq = lambda v: v * v
    n = [m(key) for key in NORMAL]
    total = (3 * LAME / SHEAR) * sq(n[0] + n[1] + n[2]) + 6.0 * (sq(n[0]) + sq(n[1]) + sq(n[2]))
    shear = None
    for a, b in SHEARS:
        t = sq(m(a) + m(b))
        shear = t if shear is None else shear + t
    total = total + 3.0 * shear
    sums, own = None, None
    for a, b in BENDS:
        t = sq(m(a) + m(b))
        o = sq(m(a)) + sq(m(b))
        sums = t if sums is None else sums + t
        own = o if own is None else own + o
    total = total + (LAME / SHEAR) * sums + 3.0 * own
    a, b, c = (m(key) for key in TWIST)
    total = total + (sq(a + b) + sq(a + c) + sq(b + c))
    bulk = sq(modes[0]["ddd"]) + sq(modes[1]["ddd"]) + sq(modes[2]["ddd"])
    return total + ((LAME + 4 * SHEAR) / (3 * SHEAR)) * bulk


def filter_planes(plane):
    x = [last_x(a) + next_x(a) for a in plane]
    cross = add(x, add(last_y(plane), next_y(plane)))
    diagonal = add(last_y(x), next_y(x))
    near = [1.5 * a + 0.5 * c + EDGE * d for a, c, d in zip(plane, cross, diagonal)]
    return near, [0.5 * a + EDGE * c for a, c in zip(plane, cross)]


def filter_layers(layers):
    pairs = [filter_planes(plane) for plane in layers]
    return [
        add(pairs[at][0], add(pairs[at - 1][1], pairs[at + 1][1])) for at in range(1, len(layers) - 1)
    ]


def partner(index, step):
    return index ^ step


def smooth_kernel(hops, count_gz, *refs):
    blocks = 4 * hops - 1
    weights_ref = refs[0]
    pack_refs = refs[1 : 1 + blocks]
    disp_hbm, own_ref = refs[1 + blocks : 3 + blocks]
    slot_refs = refs[3 + blocks : -11]
    stiff_ref, inv_ref, res_ref, step_ref, sol_ref, mode_ref, node_ref = refs[-11:-4]
    disp_ref, weight_ref, energy_ref, disp_sem = refs[-4:]

    cases, _, layers, rows, columns = disp_ref.shape
    nodes = layers + 2 * SWEEPS + 1
    chunks = chunks_of(rows)
    gz = lax.axis_index("gz")
    load = lax.axis_index("load")
    even = gz % 2 == 0

    def packed(layer, group, kind):
        hop = layer // layers
        inner = layer - hop * layers
        plane = pack_plane(cases, layers, cases if group is None else group, kind, inner)
        if hop == 0:
            return [pack_refs[0][plane, chunk] for chunk in chunks]

        def pick(design_ref, force_ref):
            if group is None:
                return [design_ref[kind * layers + inner, chunk] for chunk in chunks]
            return [force_ref[group, kind, inner, chunk] for chunk in chunks]

        at = 4 * abs(hop) - 2
        if abs(hop) == hops:
            across = [pack_refs[at][plane, chunk] for chunk in chunks]
        else:
            across = pick(*pack_refs[at : at + 2])
        if abs(hop) == 1:
            beside = [pack_refs[1][plane, chunk] for chunk in chunks]
        else:
            beside = pick(*pack_refs[at - 2 : at])
        by_sibling = even == (hop > 0)
        return [jnp.where(by_sibling, one, other) for one, other in zip(beside, across)]

    def inside(layer):
        owner = gz + layer // layers
        return jnp.logical_and(owner >= 0, owner < count_gz)

    below = None
    for at in range(nodes + 1):
        layer = at - SWEEPS - 1
        live = jnp.where(inside(layer), 1.0, 0.0)
        marks = packed(layer, None, 1)
        moduli = []
        for chunk_at, (dense, mark) in enumerate(zip(packed(layer, None, 0), marks)):
            solid = jnp.where(mark == 2.0, 1.0, dense)
            modulus = (EMIN + (1.0 - EMIN) * solid * solid * solid) * live
            moduli.append(modulus)
            if 0 <= layer < layers:
                weight = (3.0 * (1.0 - EMIN)) * solid * solid * dense
                weight_ref[layer, pl.ds(8 + 8 * chunk_at, 8)] = weight
            if 1 <= at < nodes:
                for kind, factor in enumerate(STIFF):
                    stiff_ref[kind, at - 1, chunks[chunk_at]] = modulus * factor
        spread = add(moduli, [last_x(a) for a in moduli])
        spread = add(spread, last_y(spread))
        if at > 0:
            for chunk, mark, low, high in zip(chunks, marks, below, spread):
                free = jnp.logical_and(mark != 1.0, inside(layer))
                diag = jnp.where(free, KE_DIAG * (low + high), 1.0)
                inv_ref[at - 1, chunk] = jnp.where(free, 1.0 / diag, 0.0)
        below = spread

    theta = 0.5 * (UPPER_EIG + LOWER_EIG)
    delta = 0.5 * (UPPER_EIG - LOWER_EIG)
    sigma = theta / delta

    def load_modes(node, chunk):
        return [
            {pq: mode_ref[node, comp * 4 + i, chunk] for i, pq in enumerate(PLANE)}
            for comp in range(3)
        ]

    def store_modes(node, comp, field):
        for i, plane in enumerate(to_modes_xy(field)):
            for chunk, a in zip(chunks, plane):
                mode_ref[node, comp * 4 + i, chunk] = a

    def one_case(case, carry):
        for at in range(nodes):
            for comp in range(3):
                field = []
                for chunk, force in zip(chunks, packed(at - SWEEPS, case, comp)):
                    step = inv_ref[at, chunk] * force * (1.0 / theta)
                    field.append(step)
                    if 1 <= at < nodes - 1:
                        step_ref[comp, at, chunk] = step
                    if SWEEPS <= at <= SWEEPS + layers:
                        sol_ref[comp, at - SWEEPS, chunk] = step
                store_modes(at, comp, field)

        factor = 1.0 / sigma
        for sweep in range(1, SWEEPS + 1):
            factor_next = 1.0 / (2.0 * sigma - factor)
            keep, take = factor_next * factor, 2.0 * factor_next / delta
            first, end = sweep - 1, nodes - sweep
            if sweep > 1:
                for node in range(first, end + 1):
                    for comp in range(3):
                        store_modes(node, comp, [step_ref[comp, node, chunk] for chunk in chunks])
            for chunk in chunks:
                low = load_modes(first, chunk)
                up = None
                for element in range(first, end):
                    high = load_modes(element + 1, chunk)
                    stiff = [stiff_ref[kind, element, chunk] for kind in range(4)]
                    f = mode_forces(modes_z(low, high), *stiff)
                    ups = []
                    for comp in range(3):
                        for i, pq in enumerate(PLANE):
                            diff = f[comp][pq + "d"]
                            at = comp * 4 + i
                            if pq == "ss":
                                ups.append(diff)
                                if up:
                                    node_ref[element, at, chunk] = up[at] - diff
                            else:
                                both = f[comp][pq + "s"]
                                ups.append(both + diff)
                                if up:
                                    node_ref[element, at, chunk] = up[at] + (both - diff)
                    low, up = high, ups
            for node in range(first + 1, end):
                for comp in range(3):
                    g = [[node_ref[node, comp * 4 + i, chunk] for chunk in chunks] for i in range(4)]
                    if sweep == 1:
                        before = packed(node - SWEEPS, case, comp)
                    else:
                        before = [res_ref[comp, node, chunk] for chunk in chunks]
                    for chunk, res in zip(chunks, sub(before, from_modes_xy(*g))):
                        step = keep * step_ref[comp, node, chunk] + take * (inv_ref[node, chunk] * res)
                        if sweep < SWEEPS:
                            res_ref[comp, node, chunk] = res
                            step_ref[comp, node, chunk] = step
                        if SWEEPS <= node <= SWEEPS + layers:
                            sol = sol_ref[comp, node - SWEEPS, chunk] + step
                            sol_ref[comp, node - SWEEPS, chunk] = sol
                            if sweep == SWEEPS and node < SWEEPS + layers:
                                disp_ref[case, comp, node - SWEEPS, chunk] = sol
            factor = factor_next
        pltpu.make_async_copy(disp_ref.at[case], disp_hbm.at[case], disp_sem.at[case]).start()

        weight = weights_ref[load * cases + case].astype(jnp.float32)
        for node in range(layers + 1):
            for comp in range(3):
                store_modes(node, comp, [sol_ref[comp, node, chunk] for chunk in chunks])
        for chunk in chunks:
            low = load_modes(0, chunk)
            for layer in range(layers):
                high = load_modes(layer + 1, chunk)
                energy = weight * mode_energy(modes_z(low, high))
                before = jnp.where(case == 0, 0.0, energy_ref[layer, chunk])
                energy_ref[layer, chunk] = before + energy
                low = high
        return carry

    lax.fori_loop(0, cases, one_case, 0)
    weight_sum = weights_ref[0]
    for at in range(1, weights_ref.shape[0]):
        weight_sum = weight_sum + weights_ref[at]
    weight_sum = jnp.full((8, columns), weight_sum.astype(jnp.float32))
    scale = (SHEAR / 48) / weight_sum

    spans = filter_layers(
        [[jnp.where(inside(at), a, 0.0) for a in packed(at, None, 0)] for at in range(-2, layers + 2)]
    )
    recs = [
        [jnp.where(inside(layer), 1.0 / jnp.where(inside(layer), a, 1.0), 0.0) for a in span]
        for layer, span in zip(range(-1, layers + 1), spans)
    ]
    shares = filter_layers(recs)
    total = jnp.zeros((8, columns), jnp.float32)
    own_rows = own_ref.shape[2]
    own = pl.ds(pl.multiple_of(load * own_rows, own_rows), own_rows)
    for layer in range(layers):
        for kind in range(2):
            own_ref[1 + kind, layer] = pack_refs[0][pack_plane(cases, layers, cases, kind, layer), own]
        for at, chunk in enumerate(chunks):
            inner = pl.ds(8 + 8 * at, 8)
            sens = weight_ref[layer, inner] * (energy_ref[layer, chunk] * scale)
            weight_ref[layer, inner] = sens
            total = total + sens * shares[layer][at]
            energy_ref[layer, chunk] = recs[layer + 1][at]
        own_ref[0, layer] = energy_ref[layer, own]
        weight_ref[layer, :8] = jnp.zeros((8, columns), jnp.float32)
        weight_ref[layer, 8 + rows :] = jnp.zeros((8, columns), jnp.float32)
    share = jnp.sum(total, axis=0, keepdims=True)
    wide = own_rows + 2
    for step, slot_ref in enumerate(slot_refs):
        start = pl.multiple_of(partner(load, step) * own_rows, own_rows)
        for layer in range(layers):
            window = weight_ref[layer, pl.ds(start, own_rows + 16)]
            slot_ref[layer * wide : (layer + 1) * wide] = window[7 : 7 + wide]
        slot_ref[layers * wide : layers * wide + 1] = share
    for case in range(cases):
        pltpu.make_async_copy(disp_ref.at[case], disp_hbm.at[case], disp_sem.at[case]).wait()


def pack_plane(cases, layers, group, kind, layer):
    return (group * 3 + kind) * layers + layer


def stage_kernel(labels_ref, forces_ref, pack_ref):
    cases, _, layers, _, _ = forces_ref.shape
    for case in range(cases):
        for comp in range(3):
            for layer in range(layers):
                pack_ref[pack_plane(cases, layers, case, comp, layer)] = forces_ref[case, comp, layer]
    for layer in range(layers):
        marks = labels_ref[layer].astype(jnp.float32)
        pack_ref[pack_plane(cases, layers, cases, 1, layer)] = marks


def design_kernel(cases, steps, *refs):
    density_refs = refs[1 : 1 + len(steps)]
    pack_ref, design_ref = refs[-2:]
    layers, own_rows, _ = density_refs[0].shape
    load = lax.axis_index("load")
    for step, density_ref in zip(steps, density_refs):
        start = pl.multiple_of(partner(load, step) * own_rows, own_rows)
        for layer in range(layers):
            plane = pack_plane(cases, layers, cases, 0, layer)
            pack_ref[plane, pl.ds(start, own_rows)] = density_ref[layer]
    design_ref[...] = pack_ref[cases * 3 * layers :]


def sum_kernel(*refs):
    total = refs[0][...]
    for ref in refs[1:-1]:
        total = total + ref[...]
    refs[-1][...] = total


def forward_kernel(layers, wide, sum_ref, beside_ref, out_ref):
    even = lax.axis_index("gz") % 2 == 0
    end = layers * wide
    out_ref[:wide] = jnp.where(even, beside_ref[end - wide : end], beside_ref[:wide])
    out_ref[wide : wide + 1] = sum_ref[end : end + 1] + beside_ref[end : end + 1]


def share_kernel(wide, mine_ref, *refs):
    out_ref = refs[-1]
    out_ref[...] = mine_ref[...]
    out_ref[wide : wide + 1] = share_sum(wide, mine_ref, *refs[:-1])


def share_sum(wide, *refs):
    total = refs[0][wide : wide + 1]
    for ref in refs[1:]:
        total = total + ref[wide : wide + 1]
    return total


def chip_rounds(count_gz):
    edges = []
    while 2 ** (len(edges) + 1) < count_gz:
        edges.append(2 ** (len(edges) + 1) - 1)
    pairs = [edges[at : at + 2] for at in range(0, len(edges), 2)]
    return [[pair[0], pair[0] ^ pair[1], pair[1]] if len(pair) == 2 else pair for pair in pairs]


def update_kernel(cells, rounds, *refs):
    sum_ref, beside_ref, mine_ref = refs[:3]
    other_refs = refs[3:-2]
    own_ref, new_ref = refs[-2:]
    _, layers, own_rows, columns = own_ref.shape
    wide = own_rows + 2
    gz = lax.axis_index("gz")
    even, chip = gz % 2 == 0, gz // 2
    beside = jnp.where(even, beside_ref[:wide], beside_ref[(layers - 1) * wide : layers * wide])
    across = jnp.zeros((wide, columns), jnp.float32)
    for mask, other_ref in zip(sum(rounds, []), other_refs):
        borders = (chip ^ mask) == jnp.where(even, chip - 1, chip + 1)
        across = jnp.where(borders, other_ref[:wide], across)
    numers = [jnp.where(even, across, beside)]
    numers += [sum_ref[layer * wide : (layer + 1) * wide] for layer in range(layers)]
    numers += [jnp.where(even, beside, across)]
    near, far = [], []
    for numer in numers:
        back, mid, front = (numer[at : at + own_rows] for at in range(3))
        sides = back + front
        cross = sides + (last_x(mid) + next_x(mid))
        near.append(1.5 * mid + 0.5 * cross + EDGE * (last_x(sides) + next_x(sides)))
        far.append(0.5 * mid + EDGE * cross)
    total = share_sum(wide, mine_ref, *other_refs[-len(rounds[-1]) :])
    mean = jnp.sum(total, keepdims=True) * (1.0 / cells)
    mean = jnp.broadcast_to(mean, (own_rows, columns))
    for layer in range(layers):
        numer = near[layer + 1] + (far[layer] + far[layer + 2])
        filtered = numer * own_ref[0, layer]
        density = own_ref[1, layer]
        candidate = density * jnp.sqrt(filtered / mean)
        lower = jnp.maximum(density - MOVE_LIMIT, FLOOR_DENSITY)
        upper = jnp.minimum(density + MOVE_LIMIT, 1.0)
        updated = jnp.minimum(jnp.maximum(candidate, lower), upper)
        new_ref[layer] = jnp.where(own_ref[2, layer] == 2.0, 1.0, updated)


def met(block, axis, step):
    count = lax.axis_size(axis)
    return lax.ppermute(block, axis, [(partner(i, step), i) for i in range(count)])


def far_pairs(far, count, across):
    pairs = [(i - far if (i % 2 == 0) == across else i + far, i) for i in range(count)]
    pairs = [(source, i) for source, i in pairs if 0 <= source < count]
    free = [i for i in range(count) if i not in dict(pairs)]
    empty = [i for i in range(count) if i not in dict(pairs).values()]
    return pairs + list(zip(free, empty))


def on_device(density, labels, forces, case_weights):
    count_gz, count_load = lax.axis_size("gz"), lax.axis_size("load")
    cases, _, layers, rows, columns = forces.shape
    own_rows = density.shape[1]
    nodes = layers + 2 * SWEEPS + 1
    hops = -(-(SWEEPS + 1) // layers)
    wide = own_rows + 2
    f32 = jnp.float32
    plane = (rows, columns)
    plane_bytes = rows * columns * 4
    vmem = pl.BlockSpec(memory_space=pltpu.VMEM)
    smem = pl.BlockSpec(memory_space=pltpu.SMEM)

    def shape(*dims):
        return jax.ShapeDtypeStruct(dims, f32)

    def call(kernel, out, args, planes, flops, in_specs=None, scratch=(), **more):
        limit = planes * plane_bytes + (2 << 20)
        return pl.pallas_call(
            kernel,
            out_shape=out,
            in_specs=in_specs or [vmem] * len(args),
            out_specs=more.pop("out_specs", vmem),
            scratch_shapes=scratch,
            compiler_params=pltpu.CompilerParams(vmem_limit_bytes=limit),
            cost_estimate=pl.CostEstimate(flops=flops, bytes_accessed=flops // 10, transcendentals=0),
            **more,
        )(*args)

    planes = (cases * 3 + 2) * layers
    far_forces = [
        lax.ppermute(forces, "gz", far_pairs(far, count_gz, True)) for far in range(1, hops)
    ]
    pack = call(stage_kernel, shape(planes, rows, columns), (labels, forces), 2 * planes, 1_000_000)
    steps = [0] + list(range(2, count_load)) + [1]
    densities = [density] + [met(density, "load", step) for step in steps[1:]]
    pack, design = call(
        functools.partial(design_kernel, cases, steps),
        (shape(planes, rows, columns), shape(2 * layers, rows, columns)),
        (pack, *densities, *far_forces),
        2 * planes + 6 * layers,
        100_000,
        in_specs=[vmem] * (1 + count_load) + [pl.BlockSpec(memory_space=pl.ANY)] * (hops - 1),
        out_specs=(vmem, vmem),
        input_output_aliases={0: 0},
    )
    packs = [pack, met(pack, "gz", 1)]
    for far in range(1, hops + 1):
        if far > 1:
            packs.append(lax.ppermute(design, "gz", far_pairs(far, count_gz, False)))
            packs.append(met(far_forces[far - 2], "gz", 1))
        if far < hops:
            packs.append(lax.ppermute(design, "gz", far_pairs(far, count_gz, True)))
            packs.append(far_forces[far - 1])
        else:
            packs.append(lax.ppermute(pack, "gz", far_pairs(far, count_gz, True)))

    slot_rows = -(-(layers * wide + 1) // 8) * 8
    scratch = [
        pltpu.VMEM((4, nodes - 1) + plane, f32),
        pltpu.VMEM((nodes,) + plane, f32),
        pltpu.VMEM((3, nodes) + plane, f32),
        pltpu.VMEM((3, nodes) + plane, f32),
        pltpu.VMEM((3, layers + 1) + plane, f32),
        pltpu.VMEM((nodes, 12) + plane, f32),
        pltpu.VMEM((nodes, 12) + plane, f32),
        pltpu.VMEM(forces.shape, f32),
        pltpu.VMEM((layers, rows + 16, columns), f32),
        pltpu.VMEM((layers,) + plane, f32),
        pltpu.SemaphoreType.DMA((cases,)),
    ]
    smooth_planes = nodes * 35 + 3 * (layers + 1) + 4 * layers
    smooth_planes += (1 + 2 * hops) * planes + cases * 3 * layers + 8 * layers
    displacement, own, *slots = call(
        functools.partial(smooth_kernel, hops, count_gz),
        (shape(*forces.shape), shape(3, layers, own_rows, columns))
        + (shape(slot_rows, columns),) * count_load,
        (case_weights, *packs),
        smooth_planes,
        60_000_000,
        in_specs=[smem] + [vmem] * len(packs),
        out_specs=(pl.BlockSpec(memory_space=pltpu.HBM),) + (vmem,) * (1 + count_load),
        scratch=scratch,
    )

    received = [met(slots[step], "load", step) for step in range(count_load - 1, 0, -1)]
    whole = call(sum_kernel, shape(slot_rows, columns), (slots[0], *received), 2 * count_load, 100_000)
    beside = met(whole, "gz", 1)
    forward_rows = -(-(wide + 1) // 8) * 8
    mine = call(
        functools.partial(forward_kernel, layers, wide),
        shape(forward_rows, columns),
        (whole, beside),
        4 * layers,
        10_000,
    )
    others = []
    rounds = chip_rounds(count_gz)
    for at, masks in enumerate(rounds):
        if at > 0:
            mine = call(
                functools.partial(share_kernel, wide),
                shape(forward_rows, columns),
                (mine, *others[-len(rounds[at - 1]) :]),
                8,
                10_000,
            )
        others += [met(mine, "gz", 2 * mask) for mask in masks]
    new_density = call(
        functools.partial(update_kernel, float(count_gz * layers * rows * columns), rounds),
        shape(*density.shape),
        (whole, beside, mine, *others, own),
        8 * layers,
        100_000,
    )
    return (new_density, displacement)


def solution(mesh):
    return jax.shard_map(
        on_device,
        mesh=mesh,
        in_specs=(
            P("gz", "load", None),
            P("gz", None, None),
            P("load", None, "gz", None, None),
            P(),
        ),
        out_specs=(P("gz", "load", None), P("load", None, "gz", None, None)),
        check_vma=False,
    )
```

```python
import functools

import jax
import jax.numpy as jnp
from jax import lax
from jax.experimental import pallas as pl
from jax.experimental.pallas import tpu as pltpu
from jax.sharding import PartitionSpec as P

SWEEPS = 3
EMIN = 0.001
LOWER_EIG = 0.1
UPPER_EIG = 2.5
MOVE_LIMIT = 0.2
FLOOR_DENSITY = 0.001
POISSON = 0.3
LAME = POISSON / ((1 + POISSON) * (1 - 2 * POISSON))
SHEAR = 1.0 / (2 * (1 + POISSON))
KE_DIAG = (LAME + 4 * SHEAR) / 9
EDGE = 1.5 - 2.0**0.5
PLANE = ("ss", "sd", "ds", "dd")


def chunks_of(rows):
    return [pl.ds(at, 8) for at in range(0, rows, 8)]


def next_x(a):
    lanes = a.shape[1]
    lane = lax.broadcasted_iota(jnp.int32, a.shape, 1)
    return jnp.where(lane == lanes - 1, 0.0, pltpu.roll(a, lanes - 1, 1))


def last_x(a):
    lane = lax.broadcasted_iota(jnp.int32, a.shape, 1)
    return jnp.where(lane == 0, 0.0, pltpu.roll(a, 1, 1))


def next_y(plane):
    row = lax.broadcasted_iota(jnp.int32, plane[0].shape, 0)
    rolled = [pltpu.roll(a, 7, 0) for a in plane] + [jnp.zeros_like(plane[0])]
    return [jnp.where(row == 7, rolled[at + 1], rolled[at]) for at in range(len(plane))]


def last_y(plane):
    row = lax.broadcasted_iota(jnp.int32, plane[0].shape, 0)
    rolled = [jnp.zeros_like(plane[0])] + [pltpu.roll(a, 1, 0) for a in plane]
    return [jnp.where(row == 0, rolled[at], rolled[at + 1]) for at in range(len(plane))]


def add(*planes):
    return [sum(chunks[1:], chunks[0]) for chunks in zip(*planes)]


def sub(one, other):
    return [a - b for a, b in zip(one, other)]


def to_modes_xy(u):
    ux = [next_x(a) for a in u]
    s, d = add(ux, u), sub(ux, u)
    sy, dy = next_y(s), next_y(d)
    return add(sy, s), sub(sy, s), add(dy, d), sub(dy, d)


def from_modes_xy(ss, sd, ds, dd):
    s = add(sub(ss, sd), last_y(add(ss, sd)))
    d = add(sub(ds, dd), last_y(add(ds, dd)))
    return add(sub(s, d), [last_x(a) for a in add(s, d)])


def modes_z(low, high):
    modes = []
    for comp in range(3):
        one = {}
        for pq in PLANE:
            if pq != "ss":
                one[pq + "s"] = high[comp][pq] + low[comp][pq]
            one[pq + "d"] = high[comp][pq] - low[comp][pq]
        modes.append(one)
    return modes


NORMAL = ((0, "dss"), (1, "sds"), (2, "ssd"))
BENDS = (((1, "dds"), (2, "dsd")), ((0, "dds"), (2, "sdd")), ((0, "dsd"), (1, "sdd")))
SHEARS = (((0, "sds"), (1, "dss")), ((0, "ssd"), (2, "dss")), ((1, "ssd"), (2, "sds")))
STIFF = (SHEAR / 16, SHEAR / 48, (LAME + 4 * SHEAR) / 144, SHEAR / 8)
TWIST = ((0, "sdd"), (1, "dsd"), (2, "dds"))


def mode_forces(modes, e1, e2, e3, e4):
    m = lambda key: modes[key[0]][key[1]]
    out = [{}, {}, {}]

    def put(key, value):
        out[key[0]][key[1]] = value

    trace = (LAME / (2 * SHEAR)) * (m(NORMAL[0]) + m(NORMAL[1]) + m(NORMAL[2]))
    for key in NORMAL:
        put(key, e4 * (trace + m(key)))
    for a, b in BENDS:
        t = (LAME / (3 * SHEAR)) * (m(a) + m(b))
        put(a, e1 * (t + m(a)))
        put(b, e1 * (t + m(b)))
    for a, b in SHEARS:
        f = e1 * (m(a) + m(b))
        put(a, f)
        put(b, f)
    t = m(TWIST[0]) + m(TWIST[1]) + m(TWIST[2])
    for key in TWIST:
        put(key, e2 * (t + m(key)))
    for comp in range(3):
        put((comp, "ddd"), e3 * modes[comp]["ddd"])
    return out


def mode_energy(modes):
    m = lambda key: modes[key[0]][key[1]]
    sq = lambda v: v * v
    n = [m(key) for key in NORMAL]
    total = (3 * LAME / SHEAR) * sq(n[0] + n[1] + n[2]) + 6.0 * (sq(n[0]) + sq(n[1]) + sq(n[2]))
    shear = None
    for a, b in SHEARS:
        t = sq(m(a) + m(b))
        shear = t if shear is None else shear + t
    total = total + 3.0 * shear
    sums, own = None, None
    for a, b in BENDS:
        t = sq(m(a) + m(b))
        o = sq(m(a)) + sq(m(b))
        sums = t if sums is None else sums + t
        own = o if own is None else own + o
    total = total + (LAME / SHEAR) * sums + 3.0 * own
    a, b, c = (m(key) for key in TWIST)
    total = total + (sq(a + b) + sq(a + c) + sq(b + c))
    bulk = sq(modes[0]["ddd"]) + sq(modes[1]["ddd"]) + sq(modes[2]["ddd"])
    return total + ((LAME + 4 * SHEAR) / (3 * SHEAR)) * bulk


def filter_planes(plane):
    x = [last_x(a) + next_x(a) for a in plane]
    cross = add(x, add(last_y(plane), next_y(plane)))
    diagonal = add(last_y(x), next_y(x))
    near = [1.5 * a + 0.5 * c + EDGE * d for a, c, d in zip(plane, cross, diagonal)]
    return near, [0.5 * a + EDGE * c for a, c in zip(plane, cross)]


def filter_layers(layers):
    pairs = [filter_planes(plane) for plane in layers]
    return [
        add(pairs[at][0], add(pairs[at - 1][1], pairs[at + 1][1])) for at in range(1, len(layers) - 1)
    ]


def partner(index, step):
    return index ^ step


def smooth_kernel(hops, count_gz, *refs):
    blocks = 4 * hops - 1
    weights_ref = refs[0]
    pack_refs = refs[1 : 1 + blocks]
    disp_hbm, own_ref = refs[1 + blocks : 3 + blocks]
    slot_refs = refs[3 + blocks : -11]
    stiff_ref, inv_ref, res_ref, step_ref, sol_ref, mode_ref, node_ref = refs[-11:-4]
    disp_ref, weight_ref, energy_ref, disp_sem = refs[-4:]

    cases, _, layers, rows, columns = disp_ref.shape
    nodes = layers + 2 * SWEEPS + 1
    chunks = chunks_of(rows)
    gz = lax.axis_index("gz")
    load = lax.axis_index("load")
    even = gz % 2 == 0

    def packed(layer, group, kind):
        hop = layer // layers
        inner = layer - hop * layers
        plane = pack_plane(cases, layers, cases if group is None else group, kind, inner)
        if hop == 0:
            return [pack_refs[0][plane, chunk] for chunk in chunks]

        def pick(design_ref, force_ref):
            if group is None:
                return [design_ref[kind * layers + inner, chunk] for chunk in chunks]
            return [force_ref[group, kind, inner, chunk] for chunk in chunks]

        at = 4 * abs(hop) - 2
        if abs(hop) == hops:
            across = [pack_refs[at][plane, chunk] for chunk in chunks]
        else:
            across = pick(*pack_refs[at : at + 2])
        if abs(hop) == 1:
            beside = [pack_refs[1][plane, chunk] for chunk in chunks]
        else:
            beside = pick(*pack_refs[at - 2 : at])
        by_sibling = even == (hop > 0)
        return [jnp.where(by_sibling, one, other) for one, other in zip(beside, across)]

    def inside(layer):
        owner = gz + layer // layers
        return jnp.logical_and(owner >= 0, owner < count_gz)

    below = None
    for at in range(nodes + 1):
        layer = at - SWEEPS - 1
        live = jnp.where(inside(layer), 1.0, 0.0)
        marks = packed(layer, None, 1)
        moduli = []
        for chunk_at, (dense, mark) in enumerate(zip(packed(layer, None, 0), marks)):
            solid = jnp.where(mark == 2.0, 1.0, dense)
            modulus = (EMIN + (1.0 - EMIN) * solid * solid * solid) * live
            moduli.append(modulus)
            if 0 <= layer < layers:
                weight = (3.0 * (1.0 - EMIN)) * solid * solid * dense
                weight_ref[layer, pl.ds(8 + 8 * chunk_at, 8)] = weight
            if 1 <= at < nodes:
                for kind, factor in enumerate(STIFF):
                    stiff_ref[kind, at - 1, chunks[chunk_at]] = modulus * factor
        spread = add(moduli, [last_x(a) for a in moduli])
        spread = add(spread, last_y(spread))
        if at > 0:
            for chunk, mark, low, high in zip(chunks, marks, below, spread):
                free = jnp.logical_and(mark != 1.0, inside(layer))
                diag = jnp.where(free, KE_DIAG * (low + high), 1.0)
                inv_ref[at - 1, chunk] = jnp.where(free, 1.0 / diag, 0.0)
        below = spread

    theta = 0.5 * (UPPER_EIG + LOWER_EIG)
    delta = 0.5 * (UPPER_EIG - LOWER_EIG)
    sigma = theta / delta

    def load_modes(node, chunk):
        return [
            {pq: mode_ref[node, comp * 4 + i, chunk] for i, pq in enumerate(PLANE)}
            for comp in range(3)
        ]

    def store_modes(node, comp, field):
        for i, plane in enumerate(to_modes_xy(field)):
            for chunk, a in zip(chunks, plane):
                mode_ref[node, comp * 4 + i, chunk] = a

    def one_case(case, carry):
        for at in range(nodes):
            for comp in range(3):
                field = []
                for chunk, force in zip(chunks, packed(at - SWEEPS, case, comp)):
                    step = inv_ref[at, chunk] * force * (1.0 / theta)
                    field.append(step)
                    if 1 <= at < nodes - 1:
                        step_ref[comp, at, chunk] = step
                    if SWEEPS <= at <= SWEEPS + layers:
                        sol_ref[comp, at - SWEEPS, chunk] = step
                store_modes(at, comp, field)

        factor = 1.0 / sigma
        for sweep in range(1, SWEEPS + 1):
            factor_next = 1.0 / (2.0 * sigma - factor)
            keep, take = factor_next * factor, 2.0 * factor_next / delta
            first, end = sweep - 1, nodes - sweep
            if sweep > 1:
                for node in range(first, end + 1):
                    for comp in range(3):
                        store_modes(node, comp, [step_ref[comp, node, chunk] for chunk in chunks])
            for chunk in chunks:
                low = load_modes(first, chunk)
                up = None
                for element in range(first, end):
                    high = load_modes(element + 1, chunk)
                    stiff = [stiff_ref[kind, element, chunk] for kind in range(4)]
                    f = mode_forces(modes_z(low, high), *stiff)
                    ups = []
                    for comp in range(3):
                        for i, pq in enumerate(PLANE):
                            diff = f[comp][pq + "d"]
                            at = comp * 4 + i
                            if pq == "ss":
                                ups.append(diff)
                                if up:
                                    node_ref[element, at, chunk] = up[at] - diff
                            else:
                                both = f[comp][pq + "s"]
                                ups.append(both + diff)
                                if up:
                                    node_ref[element, at, chunk] = up[at] + (both - diff)
                    low, up = high, ups
            for node in range(first + 1, end):
                for comp in range(3):
                    g = [[node_ref[node, comp * 4 + i, chunk] for chunk in chunks] for i in range(4)]
                    if sweep == 1:
                        before = packed(node - SWEEPS, case, comp)
                    else:
                        before = [res_ref[comp, node, chunk] for chunk in chunks]
                    for chunk, res in zip(chunks, sub(before, from_modes_xy(*g))):
                        step = keep * step_ref[comp, node, chunk] + take * (inv_ref[node, chunk] * res)
                        if sweep < SWEEPS:
                            res_ref[comp, node, chunk] = res
                            step_ref[comp, node, chunk] = step
                        if SWEEPS <= node <= SWEEPS + layers:
                            sol = sol_ref[comp, node - SWEEPS, chunk] + step
                            sol_ref[comp, node - SWEEPS, chunk] = sol
                            if sweep == SWEEPS and node < SWEEPS + layers:
                                disp_ref[case, comp, node - SWEEPS, chunk] = sol
            factor = factor_next
        pltpu.make_async_copy(disp_ref.at[case], disp_hbm.at[case], disp_sem.at[case]).start()

        weight = weights_ref[load * cases + case].astype(jnp.float32)
        for node in range(layers + 1):
            for comp in range(3):
                store_modes(node, comp, [sol_ref[comp, node, chunk] for chunk in chunks])
        for chunk in chunks:
            low = load_modes(0, chunk)
            for layer in range(layers):
                high = load_modes(layer + 1, chunk)
                energy = weight * mode_energy(modes_z(low, high))
                before = jnp.where(case == 0, 0.0, energy_ref[layer, chunk])
                energy_ref[layer, chunk] = before + energy
                low = high
        return carry

    lax.fori_loop(0, cases, one_case, 0)
    weight_sum = weights_ref[0]
    for at in range(1, weights_ref.shape[0]):
        weight_sum = weight_sum + weights_ref[at]
    weight_sum = jnp.full((8, columns), weight_sum.astype(jnp.float32))
    scale = (SHEAR / 48) / weight_sum

    spans = filter_layers(
        [[jnp.where(inside(at), a, 0.0) for a in packed(at, None, 0)] for at in range(-2, layers + 2)]
    )
    recs = [
        [jnp.where(inside(layer), 1.0 / jnp.where(inside(layer), a, 1.0), 0.0) for a in span]
        for layer, span in zip(range(-1, layers + 1), spans)
    ]
    shares = filter_layers(recs)
    total = jnp.zeros((8, columns), jnp.float32)
    own_rows = own_ref.shape[2]
    own = pl.ds(pl.multiple_of(load * own_rows, own_rows), own_rows)
    for layer in range(layers):
        for kind in range(2):
            own_ref[1 + kind, layer] = pack_refs[0][pack_plane(cases, layers, cases, kind, layer), own]
        for at, chunk in enumerate(chunks):
            inner = pl.ds(8 + 8 * at, 8)
            sens = weight_ref[layer, inner] * (energy_ref[layer, chunk] * scale)
            weight_ref[layer, inner] = sens
            total = total + sens * shares[layer][at]
            energy_ref[layer, chunk] = recs[layer + 1][at]
        own_ref[0, layer] = energy_ref[layer, own]
        weight_ref[layer, :8] = jnp.zeros((8, columns), jnp.float32)
        weight_ref[layer, 8 + rows :] = jnp.zeros((8, columns), jnp.float32)
    share = jnp.sum(total, axis=0, keepdims=True)
    wide = own_rows + 2
    for step, slot_ref in enumerate(slot_refs):
        start = pl.multiple_of(partner(load, step) * own_rows, own_rows)
        for layer in range(layers):
            window = weight_ref[layer, pl.ds(start, own_rows + 16)]
            slot_ref[layer * wide : (layer + 1) * wide] = window[7 : 7 + wide]
        slot_ref[layers * wide : layers * wide + 1] = share
    for case in range(cases):
        pltpu.make_async_copy(disp_ref.at[case], disp_hbm.at[case], disp_sem.at[case]).wait()


def pack_plane(cases, layers, group, kind, layer):
    return (group * 3 + kind) * layers + layer


def stage_kernel(labels_ref, forces_ref, pack_ref):
    cases, _, layers, _, _ = forces_ref.shape
    for case in range(cases):
        for comp in range(3):
            for layer in range(layers):
                pack_ref[pack_plane(cases, layers, case, comp, layer)] = forces_ref[case, comp, layer]
    for layer in range(layers):
        marks = labels_ref[layer].astype(jnp.float32)
        pack_ref[pack_plane(cases, layers, cases, 1, layer)] = marks


def design_kernel(cases, steps, *refs):
    density_refs = refs[1 : 1 + len(steps)]
    pack_ref, design_ref = refs[-2:]
    layers, own_rows, _ = density_refs[0].shape
    load = lax.axis_index("load")
    for step, density_ref in zip(steps, density_refs):
        start = pl.multiple_of(partner(load, step) * own_rows, own_rows)
        for layer in range(layers):
            plane = pack_plane(cases, layers, cases, 0, layer)
            pack_ref[plane, pl.ds(start, own_rows)] = density_ref[layer]
    design_ref[...] = pack_ref[cases * 3 * layers :]


def sum_kernel(*refs):
    total = refs[0][...]
    for ref in refs[1:-1]:
        total = total + ref[...]
    refs[-1][...] = total


def forward_kernel(layers, wide, sum_ref, beside_ref, out_ref):
    even = lax.axis_index("gz") % 2 == 0
    end = layers * wide
    out_ref[:wide] = jnp.where(even, beside_ref[end - wide : end], beside_ref[:wide])
    out_ref[wide : wide + 1] = sum_ref[end : end + 1] + beside_ref[end : end + 1]


def share_kernel(wide, mine_ref, *refs):
    out_ref = refs[-1]
    out_ref[...] = mine_ref[...]
    out_ref[wide : wide + 1] = share_sum(wide, mine_ref, *refs[:-1])


def share_sum(wide, *refs):
    total = refs[0][wide : wide + 1]
    for ref in refs[1:]:
        total = total + ref[wide : wide + 1]
    return total


def chip_rounds(count_gz):
    edges = []
    while 2 ** (len(edges) + 1) < count_gz:
        edges.append(2 ** (len(edges) + 1) - 1)
    pairs = [edges[at : at + 2] for at in range(0, len(edges), 2)]
    return [[pair[0], pair[0] ^ pair[1], pair[1]] if len(pair) == 2 else pair for pair in pairs]


def update_kernel(cells, rounds, *refs):
    sum_ref, beside_ref, mine_ref = refs[:3]
    other_refs = refs[3:-2]
    own_ref, new_ref = refs[-2:]
    _, layers, own_rows, columns = own_ref.shape
    wide = own_rows + 2
    gz = lax.axis_index("gz")
    even, chip = gz % 2 == 0, gz // 2
    beside = jnp.where(even, beside_ref[:wide], beside_ref[(layers - 1) * wide : layers * wide])
    across = jnp.zeros((wide, columns), jnp.float32)
    for mask, other_ref in zip(sum(rounds, []), other_refs):
        borders = (chip ^ mask) == jnp.where(even, chip - 1, chip + 1)
        across = jnp.where(borders, other_ref[:wide], across)
    numers = [jnp.where(even, across, beside)]
    numers += [sum_ref[layer * wide : (layer + 1) * wide] for layer in range(layers)]
    numers += [jnp.where(even, beside, across)]
    near, far = [], []
    for numer in numers:
        back, mid, front = (numer[at : at + own_rows] for at in range(3))
        sides = back + front
        cross = sides + (last_x(mid) + next_x(mid))
        near.append(1.5 * mid + 0.5 * cross + EDGE * (last_x(sides) + next_x(sides)))
        far.append(0.5 * mid + EDGE * cross)
    total = share_sum(wide, mine_ref, *other_refs[-len(rounds[-1]) :])
    mean = jnp.sum(total, keepdims=True) * (1.0 / cells)
    mean = jnp.broadcast_to(mean, (own_rows, columns))
    for layer in range(layers):
        numer = near[layer + 1] + (far[layer] + far[layer + 2])
        filtered = numer * own_ref[0, layer]
        density = own_ref[1, layer]
        candidate = density * jnp.sqrt(filtered / mean)
        lower = jnp.maximum(density - MOVE_LIMIT, FLOOR_DENSITY)
        upper = jnp.minimum(density + MOVE_LIMIT, 1.0)
        updated = jnp.minimum(jnp.maximum(candidate, lower), upper)
        new_ref[layer] = jnp.where(own_ref[2, layer] == 2.0, 1.0, updated)


def met(block, axis, step):
    count = lax.axis_size(axis)
    return lax.ppermute(block, axis, [(partner(i, step), i) for i in range(count)])


def far_pairs(far, count, across):
    pairs = [(i - far if (i % 2 == 0) == across else i + far, i) for i in range(count)]
    pairs = [(source, i) for source, i in pairs if 0 <= source < count]
    free = [i for i in range(count) if i not in dict(pairs)]
    empty = [i for i in range(count) if i not in dict(pairs).values()]
    return pairs + list(zip(free, empty))


def on_device(density, labels, forces, case_weights):
    count_gz, count_load = lax.axis_size("gz"), lax.axis_size("load")
    cases, _, layers, rows, columns = forces.shape
    own_rows = density.shape[1]
    nodes = layers + 2 * SWEEPS + 1
    hops = -(-(SWEEPS + 1) // layers)
    wide = own_rows + 2
    f32 = jnp.float32
    plane = (rows, columns)
    plane_bytes = rows * columns * 4
    vmem = pl.BlockSpec(memory_space=pltpu.VMEM)
    smem = pl.BlockSpec(memory_space=pltpu.SMEM)

    def shape(*dims):
        return jax.ShapeDtypeStruct(dims, f32)

    def call(kernel, out, args, planes, flops, in_specs=None, scratch=(), **more):
        limit = planes * plane_bytes + (2 << 20)
        return pl.pallas_call(
            kernel,
            out_shape=out,
            in_specs=in_specs or [vmem] * len(args),
            out_specs=more.pop("out_specs", vmem),
            scratch_shapes=scratch,
            compiler_params=pltpu.CompilerParams(vmem_limit_bytes=limit),
            cost_estimate=pl.CostEstimate(flops=flops, bytes_accessed=flops // 10, transcendentals=0),
            **more,
        )(*args)

    planes = (cases * 3 + 2) * layers
    far_forces = [
        lax.ppermute(forces, "gz", far_pairs(far, count_gz, True)) for far in range(1, hops)
    ]
    beside_forces = [met(block, "gz", 1) for block in far_forces]
    pack = call(stage_kernel, shape(planes, rows, columns), (labels, forces), 2 * planes, 1_000_000)
    steps = [0] + list(range(2, count_load)) + [1]
    densities = [density] + [met(density, "load", step) for step in steps[1:]]
    pack, design = call(
        functools.partial(design_kernel, cases, steps),
        (shape(planes, rows, columns), shape(2 * layers, rows, columns)),
        (pack, *densities, *far_forces, *beside_forces),
        2 * planes + 6 * layers,
        100_000,
        in_specs=[vmem] * (1 + count_load) + [pl.BlockSpec(memory_space=pl.ANY)] * (2 * (hops - 1)),
        out_specs=(vmem, vmem),
        input_output_aliases={0: 0},
    )
    packs = [pack, met(pack, "gz", 1)]
    for far in range(1, hops + 1):
        if far > 1:
            packs.append(lax.ppermute(design, "gz", far_pairs(far, count_gz, False)))
            packs.append(beside_forces[far - 2])
        if far < hops:
            packs.append(lax.ppermute(design, "gz", far_pairs(far, count_gz, True)))
            packs.append(far_forces[far - 1])
        else:
            packs.append(lax.ppermute(pack, "gz", far_pairs(far, count_gz, True)))

    slot_rows = -(-(layers * wide + 1) // 8) * 8
    scratch = [
        pltpu.VMEM((4, nodes - 1) + plane, f32),
        pltpu.VMEM((nodes,) + plane, f32),
        pltpu.VMEM((3, nodes) + plane, f32),
        pltpu.VMEM((3, nodes) + plane, f32),
        pltpu.VMEM((3, layers + 1) + plane, f32),
        pltpu.VMEM((nodes, 12) + plane, f32),
        pltpu.VMEM((nodes, 12) + plane, f32),
        pltpu.VMEM(forces.shape, f32),
        pltpu.VMEM((layers, rows + 16, columns), f32),
        pltpu.VMEM((layers,) + plane, f32),
        pltpu.SemaphoreType.DMA((cases,)),
    ]
    smooth_planes = nodes * 35 + 3 * (layers + 1) + 4 * layers
    smooth_planes += (1 + 2 * hops) * planes + cases * 3 * layers + 8 * layers
    displacement, own, *slots = call(
        functools.partial(smooth_kernel, hops, count_gz),
        (shape(*forces.shape), shape(3, layers, own_rows, columns))
        + (shape(slot_rows, columns),) * count_load,
        (case_weights, *packs),
        smooth_planes,
        60_000_000,
        in_specs=[smem] + [vmem] * len(packs),
        out_specs=(pl.BlockSpec(memory_space=pltpu.HBM),) + (vmem,) * (1 + count_load),
        scratch=scratch,
    )

    received = [met(slots[step], "load", step) for step in range(count_load - 1, 0, -1)]
    whole = call(sum_kernel, shape(slot_rows, columns), (slots[0], *received), 2 * count_load, 100_000)
    beside = met(whole, "gz", 1)
    forward_rows = -(-(wide + 1) // 8) * 8
    mine = call(
        functools.partial(forward_kernel, layers, wide),
        shape(forward_rows, columns),
        (whole, beside),
        4 * layers,
        10_000,
    )
    others = []
    rounds = chip_rounds(count_gz)
    for at, masks in enumerate(rounds):
        if at > 0:
            mine = call(
                functools.partial(share_kernel, wide),
                shape(forward_rows, columns),
                (mine, *others[-len(rounds[at - 1]) :]),
                8,
                10_000,
            )
        others += [met(mine, "gz", 2 * mask) for mask in masks]
    new_density = call(
        functools.partial(update_kernel, float(count_gz * layers * rows * columns), rounds),
        shape(*density.shape),
        (whole, beside, mine, *others, own),
        8 * layers,
        100_000,
    )
    return (new_density, displacement)


def solution(mesh):
    return jax.shard_map(
        on_device,
        mesh=mesh,
        in_specs=(
            P("gz", "load", None),
            P("gz", None, None),
            P("load", None, "gz", None, None),
            P(),
        ),
        out_specs=(P("gz", "load", None), P("load", None, "gz", None, None)),
        check_vma=False,
    )
```
